32 devices in a mesh: segment: 4 (over y, x), rows: 8 (over z, core).
Axes of the slice: x: 2, y: 2, z: 4, core: 2. Of those that a mesh axis runs over, the one named last changes fastest.
Arguments:
- state: bfloat16 [4, 2, 16, 23040], P('segment', None, 'rows'), may hold values from -6 to 6
- bounds: int32 [5], replicated, may hold values from 0 to 5, as said below
- timesteps: int32 [2], replicated, may hold values from 0 to 999
- gains: float32 [4, 2, 320], P('segment'), may hold values from 0.1 to 1.9
- spatial_weight: bfloat16 [4, 2, 3, 3, 320, 320], P('segment'), may hold values from -0.109375 to 0.109375
- temporal_weight: bfloat16 [4, 2, 3, 320, 320], P('segment'), may hold values from -0.1875 to 0.1875
- time_weight: float32 [4, 2, 320, 320], P('segment'), may hold values from -0.5 to 0.5
Outputs:
- new_state: bfloat16 [4, 2, 16, 23040], P('segment', None, 'rows')
The draws below stay inside these ranges and needn't reach their ends.
Inputs may be any that keep to these rules, and one draw needn't show every extreme that they name: bounds[0] = 0, bounds[4] = 5, and every component holds 1 or 2 blocks; slot 1 of a component with one block may be computed but is not kept.
All inputs are finite; a program needn't handle non-finite values.
Results may differ from the reference program's by a relative error of at most 0.0065.
Values may be sent and summed in bfloat16 or wider, within the bound.
No kernel may reach another device: no remote copies, remote signals or barrier semaphores. Data moves between devices by JAX's collectives and lax.ppermute only.
A program may use at most 64 MiB of HBM per device.

```python
import math
import jax
import jax.numpy as jnp
from jax import lax

C = 320
TEMB = 320
W = 72
FRAMES = 2
STEPS = 2
H = 16
N_SEGMENT = 4


def draw_bounds(key, part):
    key = jax.random.fold_in(key, 7)
    extra = jax.random.randint(key, (), 0, N_SEGMENT)
    counts = 1 + (jnp.arange(N_SEGMENT) == extra).astype(jnp.int32)
    return jnp.concatenate([jnp.zeros((1,), jnp.int32), jnp.cumsum(counts).astype(jnp.int32)])


def levels(stream_key, extent, shards, least, largest):
    level, own = 1.0, jax.random.fold_in(stream_key, 6)
    for position, shards_of in shards:
        heights = jnp.exp(jax.random.uniform(jax.random.fold_in(own, position), (shards_of,), jnp.float32, least / len(shards), largest / len(shards)))
        level = level * jnp.repeat(heights, extent[position] // shards_of).reshape([-1 if axis == position else 1 for axis in range(len(extent))])
    return level


def noise(key, extent, spread, limit, split=(), kind=jnp.bfloat16):
    entries = jax.random.normal(key, extent, jnp.float32) * spread
    if len(split) > 0:
        entries = levels(key, extent, split, -0.22, 0.18) * entries
    return jnp.clip(entries, min=-limit, max=limit).astype(kind)


def setup_inputs(seed: int = 0) -> dict:
    streams_of = jax.random.split(jax.random.key(seed), 8)
    state = noise(streams_of[0], (N_SEGMENT, FRAMES, H, W * C), 1.0, 6.0, ((0, 4), (2, 8)))
    bounds = draw_bounds(jax.random.fold_in(streams_of[7], 71), 0)
    timesteps = jax.random.randint(streams_of[2], (STEPS,), 0, 1000).astype(jnp.int32)
    gains = jnp.clip(1.0 + 0.18 * jax.random.normal(streams_of[3], (N_SEGMENT, 2, C), jnp.float32), 0.1, 1.9)
    spatial_weight = noise(streams_of[4], (N_SEGMENT, 2, 3, 3, C, C), (9 * C) ** -0.5, 0.109375, ((0, 4),))
    temporal_weight = noise(streams_of[5], (N_SEGMENT, 2, 3, C, C), (3 * C) ** -0.5, 0.1875, ((0, 4),))
    time_weight = noise(streams_of[6], (N_SEGMENT, 2, TEMB, C), (TEMB // 2) ** -0.5, 0.5, ((0, 4),), jnp.float32)
    return dict(state=state, bounds=bounds, timesteps=timesteps, gains=gains, spatial_weight=spatial_weight, temporal_weight=temporal_weight, time_weight=time_weight)


def embed(step_time):
    half = TEMB // 2
    freq = jnp.exp(-math.log(10000.0) * jnp.arange(half, dtype=jnp.float32) / half)
    angle = step_time.astype(jnp.float32) * freq
    return jnp.concatenate([jnp.cos(angle), jnp.sin(angle)])

def block_rows(extended, gain, spatial, temporal, bias):
    values = extended.astype(jnp.float32)
    scale = lax.rsqrt(lax.optimization_barrier(jnp.mean(values * values, axis=-1, keepdims=True)) + 1e-06)
    normed = (values * scale * gain).astype(jnp.bfloat16)
    padded = jnp.pad(normed, ((0, 0), (0, 0), (1, 1), (0, 0)))
    frames, rows_in, width, chans = extended.shape
    rows_out = rows_in - 2
    total = jnp.zeros((frames * rows_out * width, chans), jnp.float32) + bias
    for shift_y in range(3):
        for shift_x in range(3):
            window = padded[:, shift_y:shift_y + rows_out, shift_x:shift_x + width, :].reshape(-1, chans)
            total = total + jnp.dot(window, spatial[shift_y, shift_x], preferred_element_type=jnp.float32)
    activated = jax.nn.silu(total).astype(jnp.bfloat16).reshape(frames, rows_out, width, chans)
    framed = jnp.pad(activated, ((1, 1), (0, 0), (0, 0), (0, 0)))
    mixed = jnp.zeros_like(total)
    for tap in range(3):
        mixed = mixed + jnp.dot(framed[tap:tap + frames].reshape(-1, chans), temporal[tap], preferred_element_type=jnp.float32)
    center = extended[:, 1:-1].astype(jnp.float32).reshape(-1, chans)
    return (center + total + mixed).astype(jnp.bfloat16).reshape(frames, rows_out, width, chans)

def reference(state, bounds, timesteps, gains, spatial_weight, temporal_weight, time_weight):
    fields = state.reshape(N_SEGMENT, FRAMES, H, W, C)
    for step in range(STEPS):
        emb = embed(timesteps[step])
        bias_all = jnp.einsum('t,kjtc->kjc', emb, time_weight, precision=lax.Precision.HIGHEST)
        outputs = []
        for segment in range(N_SEGMENT):
            count = bounds[segment + 1] - bounds[segment]

            def apply(slot, field):
                extended = jnp.pad(field, ((0, 0), (1, 1), (0, 0), (0, 0)))
                return block_rows(extended, gains[segment, slot], spatial_weight[segment, slot], temporal_weight[segment, slot], bias_all[segment, slot])
            field = apply(0, fields[(segment - 1) % N_SEGMENT])
            second = apply(1, field)
            field = jnp.where(count > 1, second, field)
            outputs.append(field)
        fields = jnp.stack(outputs)
    return fields.reshape(N_SEGMENT, FRAMES, H, W * C)
```

```python
import math

import jax
import jax.numpy as jnp
from jax import lax
from jax.experimental import pallas as pl
from jax.experimental.pallas import tpu as pltpu
from jax.sharding import PartitionSpec as P

C = 320
W = 72
STEPS = 2
FRAMES = 2
ROWS = 2

HB = 4
J = W // 2 // HB
PAIR = 2 * C
GROUP = ROWS * HB
FIELD = FRAMES * J * GROUP
PAD = 64
EPS = 1e-06


def embed(step_time, entries):
    half = entries // 2
    freq = jnp.exp(-math.log(10000.0) * jnp.arange(half, dtype=jnp.float32) / half)
    angle = step_time.astype(jnp.float32) * freq
    return jnp.concatenate([jnp.cos(angle), jnp.sin(angle)])


def rounded(value):
    return value.astype(jnp.bfloat16).astype(jnp.float32)


def is_even(shape):
    return lax.broadcasted_iota(jnp.int32, shape, len(shape) - 1) < C


def normalise(value, gain):
    even = is_even(value.shape)
    square = value * value
    first = jnp.sum(jnp.where(even, square, 0.0), axis=-1, keepdims=True)
    second = jnp.sum(jnp.where(even, 0.0, square), axis=-1, keepdims=True)
    scale = jnp.where(even, lax.rsqrt(first / C + EPS), lax.rsqrt(second / C + EPS))
    return rounded(value * scale * gain)


def roll_rows(value, by):
    return pltpu.roll(value, by % value.shape[-2], value.ndim - 2)


def shifted_h(value, by):
    flat = value.reshape(-1, value.shape[-1])
    moved = pltpu.roll(flat, by % flat.shape[0], 0)
    h = lax.rem(lax.broadcasted_iota(jnp.int32, flat.shape, 0), HB)
    edge = 0 if by == 1 else HB - 1
    return jnp.where(h == edge, 0.0, moved).reshape(value.shape)


def silu(value):
    return value * jax.nn.sigmoid(value)


def dot(a, b):
    return jnp.dot(a, b, preferred_element_type=jnp.float32)


def spatial(parts, weights, slot, bias):
    even = odd = None
    for dy in range(3):
        before = parts(dy, 0, slice(2 * C - 384, 2 * C))
        center = parts(dy, 1, slice(0, 2 * C))
        after = parts(dy, 2, slice(0, 384))
        e = dot(jnp.concatenate([before, center], axis=1), weights[slot, dy, 0:1024, :])
        o = dot(jnp.concatenate([center, after], axis=1), weights[slot, dy, PAD : PAD + 1024, :])
        even = e if even is None else even + e
        odd = o if odd is None else odd + o
    return even + bias, odd + bias


def temporal(u0, u1, weights, slot):
    v0 = dot(u0, weights[slot, 1]) + dot(u1, weights[slot, 2])
    v1 = dot(u0, weights[slot, 0]) + dot(u1, weights[slot, 1])
    return v0, v1


def step_kernel(
    info, own, core, far, bias, gains, spatial_hbm, temporal_hbm, out, wide, thin, kept, sw, tw, sems
):
    count = info[0]
    last = count - 1
    copies = {}
    for at in range(2):
        slot = 0 if at == 0 else last
        copies[at] = [
            pltpu.make_async_copy(
                spatial_hbm.at[slot, dy], sw.at[at, dy, pl.ds(PAD, 3 * C), :], sems.at[at, dy]
            )
            for dy in range(3)
        ]
        copies[at].append(
            pltpu.make_async_copy(temporal_hbm.at[slot], tw.at[at], sems.at[at, 3])
        )

    @pl.when(count > 1)
    def _():
        for copy in copies[0]:
            copy.start()

    for copy in copies[1]:
        copy.start()
    zeros = jnp.zeros((3, PAD, C), jnp.bfloat16)
    for at in range(2):
        sw[at, :, 0:PAD, :] = zeros
        sw[at, :, PAD + 3 * C : 2 * PAD + 3 * C, :] = zeros

    def load(ref):
        return ref[...].astype(jnp.float32).reshape(FRAMES * J, GROUP, PAIR)

    core_is_above = info[1] == 1
    mine = load(own)
    by_core = load(core)
    by_far = load(far)
    above = jnp.where(core_is_above, by_core, by_far)
    below = jnp.where(core_is_above, by_far, by_core)
    around = jnp.concatenate([above[:, HB:], mine, below[:, :HB]], axis=1)
    kept[...] = around

    @pl.when(count > 1)
    def _():
        gain = gains[0:1, :].reshape(1, 1, PAIR)
        n_above, n_mine, n_below = (normalise(v, gain) for v in (above, mine, below))
        taps = (
            jnp.concatenate([n_above, n_mine], axis=1),
            jnp.concatenate([n_above[:, HB:], n_mine, n_below[:, :HB]], axis=1),
            jnp.concatenate([n_mine, n_below], axis=1),
        )
        for dy in range(3):
            tiles = taps[dy].reshape(FRAMES, J, 2 * GROUP, PAIR)
            wide[dy, :, 1 : J + 1] = tiles.astype(jnp.bfloat16)
            for f in range(FRAMES):
                wide[dy, f, 0] = shifted_h(tiles[f, J - 1], 1).astype(jnp.bfloat16)
                wide[dy, f, J + 1] = shifted_h(tiles[f, 0], -1).astype(jnp.bfloat16)
        for copy in copies[0]:
            copy.wait()

        def parts(dy, j0, lanes):
            value = wide[dy, :, j0 : j0 + J, :, lanes]
            return value.reshape(FRAMES * J * 2 * GROUP, -1)

        even, odd = spatial(parts, sw, 0, bias[0:1, :])
        half = J * 2 * GROUP
        u_even, u_odd = silu(even).astype(jnp.bfloat16), silu(odd).astype(jnp.bfloat16)
        u0 = jnp.concatenate([u_even[:half], u_odd[:half]], axis=0)
        u1 = jnp.concatenate([u_even[half:], u_odd[half:]], axis=0)
        v0, v1 = temporal(u0, u1, tw, 0)
        v_even = jnp.concatenate([v0[:half], v1[:half]], axis=0)
        v_odd = jnp.concatenate([v0[half:], v1[half:]], axis=0)
        change = jnp.concatenate([even + v_even, odd + v_odd], axis=1)
        result = rounded(around + change.reshape(around.shape))
        row = lax.broadcasted_iota(jnp.int32, around.shape, 1) // HB
        outside = ((row == 0) & (info[2] == 1)) | ((row == 3) & (info[3] == 1))
        kept[...] = jnp.where(outside, 0.0, result)

    value = kept[...]
    normed = normalise(value, gains[pl.ds(last, 1), :].reshape(1, 1, PAIR))
    for dy in range(3):
        tiles = normed[:, HB * dy : HB * dy + GROUP].reshape(FRAMES, J, GROUP, PAIR)
        both = jnp.concatenate([tiles[0], tiles[1]], axis=1)
        thin[dy, 1 : J + 1] = both.astype(jnp.bfloat16)
        thin[dy, 0] = shifted_h(both[J - 1], 1).astype(jnp.bfloat16)
        thin[dy, J + 1] = shifted_h(both[0], -1).astype(jnp.bfloat16)
    for copy in copies[1]:
        copy.wait()

    def parts(dy, j0, lanes):
        return thin[dy, j0 : j0 + J, :, lanes].reshape(J * FRAMES * GROUP, -1)

    even, odd = spatial(parts, sw, 1, bias[pl.ds(last, 1), :])
    even = even.reshape(J, FRAMES, GROUP, C)
    odd = odd.reshape(J, FRAMES, GROUP, C)
    u0, u1 = (
        jnp.concatenate([silu(even[:, f]).reshape(-1, C), silu(odd[:, f]).reshape(-1, C)], axis=0)
        for f in range(FRAMES)
    )
    v0, v1 = temporal(u0.astype(jnp.bfloat16), u1.astype(jnp.bfloat16), tw, 1)
    half = J * GROUP
    for f, v in enumerate((v0, v1)):
        a_even, a_odd = even[:, f].reshape(half, C), odd[:, f].reshape(half, C)
        change = jnp.concatenate([a_even + v[:half], a_odd + v[half:]], axis=1)
        center = value[f * J : (f + 1) * J, HB : HB + GROUP].reshape(half, PAIR)
        out[f * half : (f + 1) * half, :] = (center + change).astype(jnp.bfloat16)


def apply_blocks(info, own, core, far, bias, gains, spatial_weight, temporal_weight):
    vmem = pl.BlockSpec(memory_space=pltpu.VMEM)
    anywhere = pl.BlockSpec(memory_space=pl.ANY)
    return pl.pallas_call(
        step_kernel,
        out_shape=jax.ShapeDtypeStruct((FIELD, PAIR), jnp.bfloat16),
        in_specs=[pl.BlockSpec(memory_space=pltpu.SMEM)] + [vmem] * 5 + [anywhere] * 2,
        out_specs=vmem,
        scratch_shapes=[
            pltpu.VMEM((3, FRAMES, J + 2, 2 * GROUP, PAIR), jnp.bfloat16),
            pltpu.VMEM((3, J + 2, FRAMES * GROUP, PAIR), jnp.bfloat16),
            pltpu.VMEM((FRAMES * J, 2 * GROUP, PAIR), jnp.float32),
            pltpu.VMEM((2, 3, 2 * PAD + 3 * C, C), jnp.bfloat16),
            pltpu.VMEM((2, 3, C, C), jnp.bfloat16),
            pltpu.SemaphoreType.DMA((2, 4)),
        ],
        compiler_params=pltpu.CompilerParams(vmem_limit_bytes=40 * 1024 * 1024),
        cost_estimate=pl.CostEstimate(
            flops=5_000_000_000, bytes_accessed=6_000_000, transcendentals=400_000
        ),
        name="residual_blocks",
    )(info, own, core, far, bias, gains, spatial_weight, temporal_weight)


def body(state, bounds, timesteps, gains, spatial_weight, temporal_weight, time_weight):
    groups = lax.axis_size("rows")
    segments = lax.axis_size("segment")
    segment_pos = lax.axis_index("segment")
    row_group = lax.axis_index("rows")
    count = bounds[segment_pos + 1] - bounds[segment_pos]
    info = jnp.stack(
        [
            count,
            lax.rem(row_group, 2),
            (row_group == 0).astype(jnp.int32),
            (row_group == groups - 1).astype(jnp.int32),
        ]
    )
    emb = jnp.stack([embed(timesteps[step], time_weight.shape[2]) for step in range(STEPS)])
    bias = jnp.einsum("st,jtc->sjc", emb, time_weight[0], precision=lax.Precision.HIGHEST)
    gain_pairs = jnp.concatenate([gains[0], gains[0]], axis=-1)
    spatial_rows = spatial_weight.reshape(2, 3, 3 * C, C)
    temporal_rows = temporal_weight.reshape(2, 3, C, C)

    ahead = [(i, (i + 1) % segments) for i in range(segments)]
    on_chip = [(i, i ^ 1) for i in range(groups)]
    off_chip = [(i, i + 1) for i in range(1, groups - 1, 2)]
    off_chip = off_chip + [(j, i) for i, j in off_chip]

    field = state.reshape(FRAMES, ROWS, HB, J, PAIR).transpose(0, 3, 1, 2, 4).reshape(FIELD, PAIR)
    for step in range(STEPS):
        own = lax.ppermute(field, "segment", ahead)
        far = lax.ppermute(own, "rows", off_chip)
        core = lax.ppermute(own, "rows", on_chip)
        field = apply_blocks(
            info, own, core, far, bias[step], gain_pairs, spatial_rows, temporal_rows
        )
    field = field.reshape(FRAMES, J, ROWS, HB, PAIR).transpose(0, 2, 3, 1, 4)
    return field.reshape(1, FRAMES, ROWS, W * C)


def solution(mesh):
    placed = (
        P("segment", None, "rows", None),
        P(),
        P(),
        P("segment", None, None),
        P("segment", None, None, None, None, None),
        P("segment", None, None, None, None),
        P("segment", None, None, None),
    )
    return jax.shard_map(
        body,
        mesh=mesh,
        in_specs=placed,
        out_specs=P("segment", None, "rows", None),
        check_vma=False,
    )
```

```python
import functools
import math

import jax
import jax.numpy as jnp
from jax import lax
from jax.experimental import pallas as pl
from jax.experimental.pallas import tpu as pltpu
from jax.sharding import PartitionSpec as P

C = 320
W = 72
STEPS = 2
FRAMES = 2
ROWS = 2

HB = 4
J = W // 2 // HB
PAIR = 2 * C
GROUP = ROWS * HB
FIELD = FRAMES * J * GROUP
PAD = 64
EPS = 1e-06


def rounded(value):
    return value.astype(jnp.bfloat16).astype(jnp.float32)


def is_even(shape):
    return lax.broadcasted_iota(jnp.int32, shape, len(shape) - 1) < C


def normalise(value, gain):
    even = is_even(value.shape)
    square = value * value
    first = jnp.sum(jnp.where(even, square, 0.0), axis=-1, keepdims=True)
    second = jnp.sum(jnp.where(even, 0.0, square), axis=-1, keepdims=True)
    scale = jnp.where(even, lax.rsqrt(first / C + EPS), lax.rsqrt(second / C + EPS))
    return rounded(value * scale * gain)


def roll_rows(value, by):
    return pltpu.roll(value, by % value.shape[-2], value.ndim - 2)


def shifted_h(value, by):
    flat = value.reshape(-1, value.shape[-1])
    moved = pltpu.roll(flat, by % flat.shape[0], 0)
    h = lax.rem(lax.broadcasted_iota(jnp.int32, flat.shape, 0), HB)
    edge = 0 if by == 1 else HB - 1
    return jnp.where(h == edge, 0.0, moved).reshape(value.shape)


def silu(value):
    return value * jax.nn.sigmoid(value)


def dot(a, b):
    return jnp.dot(a, b, preferred_element_type=jnp.float32)


def spatial(parts, weights, slot, bias):
    even = odd = None
    for dy in range(3):
        before = parts(dy, 0, slice(2 * C - 384, 2 * C))
        center = parts(dy, 1, slice(0, 2 * C))
        after = parts(dy, 2, slice(0, 384))
        e = dot(jnp.concatenate([before, center], axis=1), weights[slot, dy, 0:1024, :])
        o = dot(jnp.concatenate([center, after], axis=1), weights[slot, dy, PAD : PAD + 1024, :])
        even = e if even is None else even + e
        odd = o if odd is None else odd + o
    return even + bias, odd + bias


def temporal(u0, u1, weights, slot):
    gap = jnp.zeros((u0.shape[0], PAD), u0.dtype)
    both = jnp.concatenate([u0, gap, u1, gap], axis=1)
    v0 = dot(both, weights[slot, 1:3].reshape(-1, C))
    v1 = dot(both, weights[slot, 0:2].reshape(-1, C))
    return v0, v1


def prepare_kernel(
    bounds_hbm,
    timesteps_hbm,
    gains_hbm,
    time_hbm,
    info,
    bias,
    gain_pairs,
    bounds,
    timesteps,
    gains,
    time_weight,
    sems,
):
    copies = [
        pltpu.make_async_copy(source, target, sems.at[n])
        for n, (source, target) in enumerate(
            (
                (bounds_hbm, bounds),
                (timesteps_hbm, timesteps),
                (gains_hbm, gains),
                (time_hbm, time_weight),
            )
        )
    ]
    for copy in copies:
        copy.start()
    for copy in copies:
        copy.wait()
    segment = lax.axis_index("segment")
    info[...] = jnp.full(info.shape, bounds[segment + 1] - bounds[segment], jnp.int32)
    gain_pairs[...] = jnp.concatenate([gains[...], gains[...]], axis=1)
    entries = time_weight.shape[1]
    half = entries // 2
    at = lax.broadcasted_iota(jnp.int32, (8, entries), 1)
    step = lax.broadcasted_iota(jnp.int32, (8, entries), 0)
    place = jnp.where(at < half, at, at - half).astype(jnp.float32)
    times = jnp.zeros((8, entries), jnp.int32)
    for s in range(STEPS):
        times = jnp.where(step == s, timesteps[s], times)
    angle = times.astype(jnp.float32) * jnp.exp(-math.log(10000.0) * place / half)
    emb = jnp.where(at < half, jnp.cos(angle), jnp.sin(angle))
    for slot in range(2):
        made = jnp.dot(
            emb,
            time_weight[slot],
            precision=lax.Precision.HIGHEST,
            preferred_element_type=jnp.float32,
        )
        for s in range(STEPS):
            bias[s, slot : slot + 1, :] = made[s : s + 1]


def step_kernel(step, info, own, core, far, bias, gains, sw, tw, out, wide, thin, kept):
    count = jnp.max(info[0:1, :])
    last = count - 1
    row_group = lax.axis_index("rows")
    at_top = row_group == 0
    at_bottom = row_group == lax.axis_size("rows") - 1

    def load(ref):
        return ref[...].astype(jnp.float32).reshape(FRAMES * J, GROUP, PAIR)

    core_is_above = lax.rem(row_group, 2) == 1
    mine = load(own)
    by_core = load(core)
    by_far = jnp.where(at_top | at_bottom, 0.0, load(far))
    above = jnp.where(core_is_above, by_core, by_far)
    below = jnp.where(core_is_above, by_far, by_core)
    around = jnp.concatenate([above[:, HB:], mine, below[:, :HB]], axis=1)
    kept[...] = around

    @pl.when(count > 1)
    def _():
        gain = gains[0:1, :].reshape(1, 1, PAIR)
        n_above, n_mine, n_below = (normalise(v, gain) for v in (above, mine, below))
        taps = (
            jnp.concatenate([n_above, n_mine], axis=1),
            jnp.concatenate([n_above[:, HB:], n_mine, n_below[:, :HB]], axis=1),
            jnp.concatenate([n_mine, n_below], axis=1),
        )
        for dy in range(3):
            tiles = taps[dy].reshape(FRAMES, J, 2 * GROUP, PAIR)
            wide[dy, :, 1 : J + 1] = tiles.astype(jnp.bfloat16)
            for f in range(FRAMES):
                wide[dy, f, 0] = shifted_h(tiles[f, J - 1], 1).astype(jnp.bfloat16)
                wide[dy, f, J + 1] = shifted_h(tiles[f, 0], -1).astype(jnp.bfloat16)
        def parts(dy, j0, lanes):
            value = wide[dy, :, j0 : j0 + J, :, lanes]
            return value.reshape(FRAMES * J * 2 * GROUP, -1)

        even, odd = spatial(parts, sw, 0, bias[step, 0:1, :])
        half = J * 2 * GROUP
        u_even, u_odd = silu(even).astype(jnp.bfloat16), silu(odd).astype(jnp.bfloat16)
        u0 = jnp.concatenate([u_even[:half], u_odd[:half]], axis=0)
        u1 = jnp.concatenate([u_even[half:], u_odd[half:]], axis=0)
        v0, v1 = temporal(u0, u1, tw, 0)
        v_even = jnp.concatenate([v0[:half], v1[:half]], axis=0)
        v_odd = jnp.concatenate([v0[half:], v1[half:]], axis=0)
        change = jnp.concatenate([even + v_even, odd + v_odd], axis=1)
        result = rounded(around + change.reshape(around.shape))
        row = lax.broadcasted_iota(jnp.int32, around.shape, 1) // HB
        outside = ((row == 0) & at_top) | ((row == 3) & at_bottom)
        kept[...] = jnp.where(outside, 0.0, result)

    value = kept[...]
    normed = normalise(value, gains[pl.ds(last, 1), :].reshape(1, 1, PAIR))
    for dy in range(3):
        tiles = normed[:, HB * dy : HB * dy + GROUP].reshape(FRAMES, J, GROUP, PAIR)
        both = jnp.concatenate([tiles[0], tiles[1]], axis=1)
        thin[dy, 1 : J + 1] = both.astype(jnp.bfloat16)
        thin[dy, 0] = shifted_h(both[J - 1], 1).astype(jnp.bfloat16)
        thin[dy, J + 1] = shifted_h(both[0], -1).astype(jnp.bfloat16)

    def parts(dy, j0, lanes):
        return thin[dy, j0 : j0 + J, :, lanes].reshape(J * FRAMES * GROUP, -1)

    even, odd = spatial(parts, sw, last, bias[step, pl.ds(last, 1), :])
    even = even.reshape(J, FRAMES, GROUP, C)
    odd = odd.reshape(J, FRAMES, GROUP, C)
    u0, u1 = (
        jnp.concatenate([silu(even[:, f]).reshape(-1, C), silu(odd[:, f]).reshape(-1, C)], axis=0)
        for f in range(FRAMES)
    )
    v0, v1 = temporal(u0.astype(jnp.bfloat16), u1.astype(jnp.bfloat16), tw, last)
    half = J * GROUP
    for f, v in enumerate((v0, v1)):
        a_even, a_odd = even[:, f].reshape(half, C), odd[:, f].reshape(half, C)
        change = jnp.concatenate([a_even + v[:half], a_odd + v[half:]], axis=1)
        center = value[f * J : (f + 1) * J, HB : HB + GROUP].reshape(half, PAIR)
        out[f * half : (f + 1) * half, :] = (center + change).astype(jnp.bfloat16)


def prepare(bounds, timesteps, gains, time_weight):
    vmem = pl.BlockSpec(memory_space=pltpu.VMEM)
    hbm = pl.BlockSpec(memory_space=pltpu.HBM)
    return pl.pallas_call(
        prepare_kernel,
        out_shape=(
            jax.ShapeDtypeStruct((8, 128), jnp.int32),
            jax.ShapeDtypeStruct((STEPS, 2, C), jnp.float32),
            jax.ShapeDtypeStruct((2, PAIR), jnp.float32),
        ),
        in_specs=[hbm, hbm, hbm, hbm],
        out_specs=(vmem,) * 3,
        scratch_shapes=[
            pltpu.SMEM(bounds.shape, jnp.int32),
            pltpu.SMEM(timesteps.shape, jnp.int32),
            pltpu.VMEM(gains.shape, jnp.float32),
            pltpu.VMEM(time_weight.shape, jnp.float32),
            pltpu.SemaphoreType.DMA((4,)),
        ],
        compiler_params=pltpu.CompilerParams(vmem_limit_bytes=20 * 1024 * 1024),
        cost_estimate=pl.CostEstimate(
            flops=100_000_000, bytes_accessed=1_000_000, transcendentals=10_000
        ),
        name="prepare",
    )(bounds, timesteps, gains, time_weight)


def apply_blocks(step, info, own, core, far, bias, gains, sw, tw):
    vmem = pl.BlockSpec(memory_space=pltpu.VMEM)
    return pl.pallas_call(
        functools.partial(step_kernel, step),
        out_shape=jax.ShapeDtypeStruct((FIELD, PAIR), jnp.bfloat16),
        in_specs=[vmem] * 8,
        out_specs=vmem,
        scratch_shapes=[
            pltpu.VMEM((3, FRAMES, J + 2, 2 * GROUP, PAIR), jnp.bfloat16),
            pltpu.VMEM((3, J + 2, FRAMES * GROUP, PAIR), jnp.bfloat16),
            pltpu.VMEM((FRAMES * J, 2 * GROUP, PAIR), jnp.float32),
        ],
        compiler_params=pltpu.CompilerParams(vmem_limit_bytes=32 * 1024 * 1024),
        cost_estimate=pl.CostEstimate(
            flops=5_000_000_000, bytes_accessed=6_000_000, transcendentals=400_000
        ),
        name="residual_blocks",
    )(info, own, core, far, bias, gains, sw, tw)


def body(state, bounds, timesteps, gains, spatial_weight, temporal_weight, time_weight):
    groups = lax.axis_size("rows")
    segments = lax.axis_size("segment")
    info, bias, gain_pairs = prepare(bounds, timesteps, gains[0], time_weight[0])
    sw = jnp.pad(
        spatial_weight.reshape(2, 3, 3 * C, C), ((0, 0), (0, 0), (PAD, PAD), (0, 0))
    )
    tw = jnp.pad(temporal_weight.reshape(2, 3, C, C), ((0, 0), (0, 0), (0, PAD), (0, 0)))
    ahead = [(i, (i + 1) % segments) for i in range(segments)]
    on_chip = [(i, i ^ 1) for i in range(groups)]
    off_chip = [(i, i + 1) for i in range(1, groups - 1, 2)]
    off_chip = off_chip + [(j, i) for i, j in off_chip] + [(0, 0), (groups - 1, groups - 1)]

    field = state.reshape(FRAMES, ROWS, HB, J, PAIR).transpose(0, 3, 1, 2, 4).reshape(FIELD, PAIR)
    for step in range(STEPS):
        own = lax.ppermute(field, "segment", ahead)
        if step == 0:
            own, info, sw, tw, bias, gain_pairs = lax.optimization_barrier(
                (own, info, sw, tw, bias, gain_pairs)
            )
        far = lax.ppermute(own, "rows", off_chip)
        core = lax.ppermute(own, "rows", on_chip)
        field = apply_blocks(step, info, own, core, far, bias, gain_pairs, sw, tw)
    field = field.reshape(FRAMES, J, ROWS, HB, PAIR).transpose(0, 2, 3, 1, 4)
    return field.reshape(1, FRAMES, ROWS, W * C)


def solution(mesh):
    placed = (
        P("segment", None, "rows", None),
        P(),
        P(),
        P("segment", None, None),
        P("segment", None, None, None, None, None),
        P("segment", None, None, None, None),
        P("segment", None, None, None),
    )
    return jax.shard_map(
        body,
        mesh=mesh,
        in_specs=placed,
        out_specs=P("segment", None, "rows", None),
        check_vma=False,
    )
```

```python
import functools
import math

import jax
import jax.numpy as jnp
from jax import lax
from jax.experimental import pallas as pl
from jax.experimental.pallas import tpu as pltpu
from jax.sharding import PartitionSpec as P

C = 320
W = 72
STEPS = 2
FRAMES = 2
ROWS = 2

HB = 4
J = W // 2 // HB
PAIR = 2 * C
GROUP = ROWS * HB
FIELD = FRAMES * J * GROUP
PAD = 64
EPS = 1e-06


def rounded(value):
    return value.astype(jnp.bfloat16).astype(jnp.float32)


def is_even(shape):
    return lax.broadcasted_iota(jnp.int32, shape, len(shape) - 1) < C


def normalise(value, gain):
    even = is_even(value.shape)
    square = value * value
    first = jnp.sum(jnp.where(even, square, 0.0), axis=-1, keepdims=True)
    second = jnp.sum(jnp.where(even, 0.0, square), axis=-1, keepdims=True)
    scale = jnp.where(even, lax.rsqrt(first / C + EPS), lax.rsqrt(second / C + EPS))
    return rounded(value * scale * gain)


def roll_rows(value, by):
    return pltpu.roll(value, by % value.shape[-2], value.ndim - 2)


def shifted_h(value, by):
    flat = value.reshape(-1, value.shape[-1])
    moved = pltpu.roll(flat, by % flat.shape[0], 0)
    h = lax.rem(lax.broadcasted_iota(jnp.int32, flat.shape, 0), HB)
    edge = 0 if by == 1 else HB - 1
    return jnp.where(h == edge, 0.0, moved).reshape(value.shape)


def silu(value):
    return value * jax.nn.sigmoid(value)


def dot(a, b):
    return jnp.dot(a, b, preferred_element_type=jnp.float32)


def spatial(parts, weights, slot, bias):
    even = odd = None
    for dy in range(3):
        before = parts(dy, 0, slice(2 * C - 384, 2 * C))
        center = parts(dy, 1, slice(0, 2 * C))
        after = parts(dy, 2, slice(0, 384))
        e = dot(jnp.concatenate([before, center], axis=1), weights[slot, dy, 0:1024, :])
        o = dot(jnp.concatenate([center, after], axis=1), weights[slot, dy, PAD : PAD + 1024, :])
        even = e if even is None else even + e
        odd = o if odd is None else odd + o
    return even + bias, odd + bias


def temporal(u0, u1, weights, slot):
    gap = jnp.zeros((u0.shape[0], PAD), u0.dtype)
    both = jnp.concatenate([u0, gap, u1, gap], axis=1)
    v0 = dot(both, weights[slot, 1:3].reshape(-1, C))
    v1 = dot(both, weights[slot, 0:2].reshape(-1, C))
    return v0, v1


def prepare_kernel(
    bounds_hbm,
    timesteps_hbm,
    gains_hbm,
    time_hbm,
    info,
    bias,
    gain_pairs,
    bounds,
    timesteps,
    gains,
    time_weight,
    sems,
):
    copies = [
        pltpu.make_async_copy(source, target, sems.at[n])
        for n, (source, target) in enumerate(
            (
                (bounds_hbm, bounds),
                (timesteps_hbm, timesteps),
                (gains_hbm, gains),
                (time_hbm, time_weight),
            )
        )
    ]
    for copy in copies:
        copy.start()
    for copy in copies:
        copy.wait()
    segment = lax.axis_index("segment")
    info[...] = jnp.full(info.shape, bounds[segment + 1] - bounds[segment], jnp.int32)
    gain_pairs[...] = jnp.concatenate([gains[...], gains[...]], axis=1)
    entries = time_weight.shape[1]
    half = entries // 2
    at = lax.broadcasted_iota(jnp.int32, (8, entries), 1)
    step = lax.broadcasted_iota(jnp.int32, (8, entries), 0)
    place = jnp.where(at < half, at, at - half).astype(jnp.float32)
    times = jnp.zeros((8, entries), jnp.int32)
    for s in range(STEPS):
        times = jnp.where(step == s, timesteps[s], times)
    angle = times.astype(jnp.float32) * jnp.exp(-math.log(10000.0) * place / half)
    emb = jnp.where(at < half, jnp.cos(angle), jnp.sin(angle))
    for slot in range(2):
        made = jnp.dot(
            emb,
            time_weight[slot],
            precision=lax.Precision.HIGHEST,
            preferred_element_type=jnp.float32,
        )
        for s in range(STEPS):
            bias[s, slot : slot + 1, :] = made[s : s + 1]


def step_kernel(step, info, own, core, far, bias, gains, sw, tw, out, wide, thin, kept):
    count = jnp.max(info[0:1, :])
    last = count - 1
    row_group = lax.axis_index("rows")
    at_top = row_group == 0
    at_bottom = row_group == lax.axis_size("rows") - 1

    def load(ref):
        return ref[...].astype(jnp.float32).reshape(FRAMES * J, GROUP, PAIR)

    core_is_above = lax.rem(row_group, 2) == 1
    mine = load(own)
    by_core = load(core)
    by_far = jnp.where(at_top | at_bottom, 0.0, load(far))
    above = jnp.where(core_is_above, by_core, by_far)
    below = jnp.where(core_is_above, by_far, by_core)
    around = jnp.concatenate([above[:, HB:], mine, below[:, :HB]], axis=1)
    kept[...] = around

    @pl.when(count > 1)
    def _():
        gain = gains[0:1, :].reshape(1, 1, PAIR)
        n_above, n_mine, n_below = (normalise(v, gain) for v in (above, mine, below))
        taps = (
            jnp.concatenate([n_above, n_mine], axis=1),
            jnp.concatenate([n_above[:, HB:], n_mine, n_below[:, :HB]], axis=1),
            jnp.concatenate([n_mine, n_below], axis=1),
        )
        for dy in range(3):
            tiles = taps[dy].reshape(FRAMES, J, 2 * GROUP, PAIR)
            wide[dy, :, 1 : J + 1] = tiles.astype(jnp.bfloat16)
            for f in range(FRAMES):
                wide[dy, f, 0] = shifted_h(tiles[f, J - 1], 1).astype(jnp.bfloat16)
                wide[dy, f, J + 1] = shifted_h(tiles[f, 0], -1).astype(jnp.bfloat16)
        def parts(dy, j0, lanes):
            value = wide[dy, :, j0 : j0 + J, :, lanes]
            return value.reshape(FRAMES * J * 2 * GROUP, -1)

        even, odd = spatial(parts, sw, 0, bias[step, 0:1, :])
        half = J * 2 * GROUP
        u_even, u_odd = silu(even).astype(jnp.bfloat16), silu(odd).astype(jnp.bfloat16)
        u0 = jnp.concatenate([u_even[:half], u_odd[:half]], axis=0)
        u1 = jnp.concatenate([u_even[half:], u_odd[half:]], axis=0)
        v0, v1 = temporal(u0, u1, tw, 0)
        v_even = jnp.concatenate([v0[:half], v1[:half]], axis=0)
        v_odd = jnp.concatenate([v0[half:], v1[half:]], axis=0)
        change = jnp.concatenate([even + v_even, odd + v_odd], axis=1)
        result = rounded(around + change.reshape(around.shape))
        row = lax.broadcasted_iota(jnp.int32, around.shape, 1) // HB
        outside = ((row == 0) & at_top) | ((row == 3) & at_bottom)
        kept[...] = jnp.where(outside, 0.0, result)

    value = kept[...]
    normed = normalise(value, gains[pl.ds(last, 1), :].reshape(1, 1, PAIR))
    for dy in range(3):
        tiles = normed[:, HB * dy : HB * dy + GROUP].reshape(FRAMES, J, GROUP, PAIR)
        both = jnp.concatenate([tiles[0], tiles[1]], axis=1)
        thin[dy, 1 : J + 1] = both.astype(jnp.bfloat16)
        thin[dy, 0] = shifted_h(both[J - 1], 1).astype(jnp.bfloat16)
        thin[dy, J + 1] = shifted_h(both[0], -1).astype(jnp.bfloat16)

    def parts(dy, j0, lanes):
        return thin[dy, j0 : j0 + J, :, lanes].reshape(J * FRAMES * GROUP, -1)

    even, odd = spatial(parts, sw, last, bias[step, pl.ds(last, 1), :])
    even = even.reshape(J, FRAMES, GROUP, C)
    odd = odd.reshape(J, FRAMES, GROUP, C)
    u0, u1 = (
        jnp.concatenate([silu(even[:, f]).reshape(-1, C), silu(odd[:, f]).reshape(-1, C)], axis=0)
        for f in range(FRAMES)
    )
    v0, v1 = temporal(u0.astype(jnp.bfloat16), u1.astype(jnp.bfloat16), tw, last)
    half = J * GROUP
    for f, v in enumerate((v0, v1)):
        a_even, a_odd = even[:, f].reshape(half, C), odd[:, f].reshape(half, C)
        change = jnp.concatenate([a_even + v[:half], a_odd + v[half:]], axis=1)
        center = value[f * J : (f + 1) * J, HB : HB + GROUP].reshape(half, PAIR)
        out[f * half : (f + 1) * half, :] = (center + change).astype(jnp.bfloat16)


def prepare(bounds, timesteps, gains, time_weight):
    vmem = pl.BlockSpec(memory_space=pltpu.VMEM)
    hbm = pl.BlockSpec(memory_space=pltpu.HBM)
    return pl.pallas_call(
        prepare_kernel,
        out_shape=(
            jax.ShapeDtypeStruct((8, 128), jnp.int32),
            jax.ShapeDtypeStruct((STEPS, 2, C), jnp.float32),
            jax.ShapeDtypeStruct((2, PAIR), jnp.float32),
        ),
        in_specs=[hbm, hbm, hbm, hbm],
        out_specs=(vmem,) * 3,
        scratch_shapes=[
            pltpu.SMEM(bounds.shape, jnp.int32),
            pltpu.SMEM(timesteps.shape, jnp.int32),
            pltpu.VMEM(gains.shape, jnp.float32),
            pltpu.VMEM(time_weight.shape, jnp.float32),
            pltpu.SemaphoreType.DMA((4,)),
        ],
        compiler_params=pltpu.CompilerParams(vmem_limit_bytes=20 * 1024 * 1024),
        cost_estimate=pl.CostEstimate(
            flops=100_000_000, bytes_accessed=1_000_000, transcendentals=10_000
        ),
        name="prepare",
    )(bounds, timesteps, gains, time_weight)


def apply_blocks(step, info, own, core, far, bias, gains, sw, tw):
    vmem = pl.BlockSpec(memory_space=pltpu.VMEM)
    return pl.pallas_call(
        functools.partial(step_kernel, step),
        out_shape=jax.ShapeDtypeStruct((FIELD, PAIR), jnp.bfloat16),
        in_specs=[vmem] * 8,
        out_specs=vmem,
        scratch_shapes=[
            pltpu.VMEM((3, FRAMES, J + 2, 2 * GROUP, PAIR), jnp.bfloat16),
            pltpu.VMEM((3, J + 2, FRAMES * GROUP, PAIR), jnp.bfloat16),
            pltpu.VMEM((FRAMES * J, 2 * GROUP, PAIR), jnp.float32),
        ],
        compiler_params=pltpu.CompilerParams(vmem_limit_bytes=32 * 1024 * 1024),
        cost_estimate=pl.CostEstimate(
            flops=5_000_000_000, bytes_accessed=6_000_000, transcendentals=400_000
        ),
        name="residual_blocks",
    )(info, own, core, far, bias, gains, sw, tw)


def body(state, bounds, timesteps, gains, spatial_weight, temporal_weight, time_weight):
    groups = lax.axis_size("rows")
    segments = lax.axis_size("segment")
    info, bias, gain_pairs = prepare(bounds, timesteps, gains[0], time_weight[0])
    sw = jnp.pad(
        spatial_weight.reshape(2, 3, 3 * C, C), ((0, 0), (0, 0), (PAD, PAD), (0, 0))
    )
    tw = jnp.pad(temporal_weight.reshape(2, 3, C, C), ((0, 0), (0, 0), (0, PAD), (0, 0)))
    ahead = [(i, (i + 1) % segments) for i in range(segments)]
    on_chip = [(i, i ^ 1) for i in range(groups)]
    off_chip = [(i, i + 1) for i in range(1, groups - 1, 2)]
    off_chip = off_chip + [(j, i) for i, j in off_chip] + [(0, 0), (groups - 1, groups - 1)]

    off_chip_ahead = [
        (a * groups + i, b * groups + j) for a, b in ahead for i, j in off_chip
    ]

    field = state.reshape(FRAMES, ROWS, HB, J, PAIR).transpose(0, 3, 1, 2, 4).reshape(FIELD, PAIR)
    for step in range(STEPS):
        own = lax.ppermute(field, "segment", ahead)
        far = lax.ppermute(field, ("segment", "rows"), off_chip_ahead)
        if step == 0:
            own, info, sw, tw, bias, gain_pairs = lax.optimization_barrier(
                (own, info, sw, tw, bias, gain_pairs)
            )
        core = lax.ppermute(own, "rows", on_chip)
        field = apply_blocks(step, info, own, core, far, bias, gain_pairs, sw, tw)
    field = field.reshape(FRAMES, J, ROWS, HB, PAIR).transpose(0, 2, 3, 1, 4)
    return field.reshape(1, FRAMES, ROWS, W * C)


def solution(mesh):
    placed = (
        P("segment", None, "rows", None),
        P(),
        P(),
        P("segment", None, None),
        P("segment", None, None, None, None, None),
        P("segment", None, None, None, None),
        P("segment", None, None, None),
    )
    return jax.shard_map(
        body,
        mesh=mesh,
        in_specs=placed,
        out_specs=P("segment", None, "rows", None),
        check_vma=False,
    )
```

```python
import functools
import math

import jax
import jax.numpy as jnp
from jax import lax
from jax.experimental import pallas as pl
from jax.experimental.pallas import tpu as pltpu
from jax.sharding import PartitionSpec as P

C = 320
W = 72
STEPS = 2
FRAMES = 2
ROWS = 2

HB = 4
J = W // 2 // HB
PAIR = 2 * C
GROUP = ROWS * HB
FIELD = FRAMES * J * GROUP
PAD = 64
LANES = PAIR + 256
EPS = 1e-06


def low_lanes(shape):
    return lax.broadcasted_iota(jnp.int32, shape, len(shape) - 1) < PAD


def normalise(value, gain):
    low = low_lanes(value[..., 256:384].shape)
    square = value * value
    middle = square[..., 256:384]
    first = square[..., 0:128] + square[..., 128:256] + jnp.where(low, middle, 0.0)
    second = square[..., 384:512] + square[..., 512:640] + jnp.where(low, 0.0, middle)
    scale = lax.rsqrt(jnp.sum(first, axis=-1, keepdims=True) / C + EPS)
    other = lax.rsqrt(jnp.sum(second, axis=-1, keepdims=True) / C + EPS)
    scaled = jnp.concatenate(
        [
            value[..., 0:256] * scale,
            value[..., 256:384] * jnp.where(low, scale, other),
            value[..., 384:640] * other,
        ],
        axis=-1,
    )
    return scaled * gain


def load(ref):
    return ref[...].astype(jnp.float32).reshape(FRAMES * J, GROUP, PAIR)


def flip(value):
    return pltpu.roll(value, HB, 1)


def flip_if(odd, value):
    return pltpu.roll(value, HB * odd, 1)


def halves(first, second):
    row = lax.broadcasted_iota(jnp.int32, first.shape, 1)
    return jnp.where(row < HB, first, second)


def shifted_h(value, by):
    rows = value.shape[0]
    moved = pltpu.roll(value, by % rows, 0)
    h = lax.rem(lax.broadcasted_iota(jnp.int32, value.shape, 0), HB)
    edge = 0 if by == 1 else HB - 1
    return jnp.where(h == edge, 0.0, moved)


def put(ref, at, value):
    middle = value[..., 256:384]
    low = low_lanes(middle.shape)
    ref[at + (slice(None), slice(0, PAIR))] = value.astype(jnp.bfloat16)
    ref[at + (slice(None), slice(PAIR, PAIR + 128))] = jnp.where(low, 0.0, middle).astype(
        jnp.bfloat16
    )
    ref[at + (slice(None), slice(PAIR + 128, LANES))] = jnp.where(low, middle, 0.0).astype(
        jnp.bfloat16
    )


def put_wide(ref, dy, first, second):
    tiles = jnp.concatenate([first, second], axis=1).reshape(FRAMES, J, 2 * GROUP, PAIR)
    put(ref, (dy, slice(None), slice(1, J + 1)), tiles)
    for f in range(FRAMES):
        put(ref, (dy, f, 0), shifted_h(tiles[f, J - 1], 1))
        put(ref, (dy, f, J + 1), shifted_h(tiles[f, 0], -1))


def put_thin(ref, dy, value):
    tiles = value.reshape(FRAMES, J, GROUP, PAIR)
    tiles = jnp.concatenate([tiles[0], tiles[1]], axis=1)
    put(ref, (dy, slice(1, J + 1)), tiles)
    put(ref, (dy, 0), shifted_h(tiles[J - 1], 1))
    put(ref, (dy, J + 1), shifted_h(tiles[0], -1))


def rows_of(ref, dy, j0, wide, start, stop):
    if wide:
        return ref[dy, :, j0 : j0 + J, :, start:stop].reshape(-1, stop - start)
    return ref[dy, j0 : j0 + J, :, start:stop].reshape(-1, stop - start)


def silu(value):
    return value * jax.nn.sigmoid(value)


def dot(a, b):
    return jnp.dot(a, b, preferred_element_type=jnp.float32)


def spatial(ref, wide, taps, weights, slot, odd):
    even_sum = odd_sum = None
    for dy in taps:
        at = dy + odd * (2 - 2 * dy)
        rows = functools.partial(rows_of, ref, dy, wide=wide)
        center = rows(1, start=0, stop=PAIR)
        before = [rows(0, start=PAIR, stop=PAIR + 128), rows(0, start=384, stop=PAIR)]
        after = [rows(2, start=0, stop=256), rows(2, start=PAIR + 128, stop=LANES)]
        filler = weights[slot, at, 0:PAD, :]
        kernel = weights[slot, at]
        turned = jnp.concatenate([kernel[C:], filler, kernel[:C]], axis=0)
        straight = jnp.concatenate([kernel, filler], axis=0)
        e = dot(jnp.concatenate([center] + before, axis=1), turned)
        o = dot(jnp.concatenate([center] + after, axis=1), straight)
        even_sum = e if even_sum is None else even_sum + e
        odd_sum = o if odd_sum is None else odd_sum + o
    return even_sum, odd_sum


def temporal(u0, u1, weights, slot):
    gap = jnp.zeros((u0.shape[0], PAD), u0.dtype)
    both = jnp.concatenate([u0, gap, u1, gap], axis=1)
    t0, t1, t2 = (weights[slot, tap] for tap in range(3))
    v0 = dot(both, jnp.concatenate([t1, t1[:PAD], t2, t2[:PAD]], axis=0))
    v1 = dot(both, jnp.concatenate([t0, t0[:PAD], t1, t1[:PAD]], axis=0))
    return v0, v1


def prepare_kernel(
    bounds_hbm,
    timesteps_hbm,
    gains_hbm,
    time_hbm,
    info,
    bias,
    gain_pairs,
    bounds,
    timesteps,
    gains,
    time_weight,
    sems,
):
    copies = [
        pltpu.make_async_copy(source, target, sems.at[n])
        for n, (source, target) in enumerate(
            (
                (bounds_hbm, bounds),
                (timesteps_hbm, timesteps),
                (gains_hbm, gains),
                (time_hbm, time_weight),
            )
        )
    ]
    for copy in copies:
        copy.start()
    for copy in copies:
        copy.wait()
    segment = lax.axis_index("segment")
    info[...] = jnp.full(info.shape, bounds[segment + 1] - bounds[segment], jnp.int32)
    gain_pairs[...] = jnp.concatenate([gains[...], gains[...]], axis=1)
    entries = time_weight.shape[1]
    half = entries // 2
    at = lax.broadcasted_iota(jnp.int32, (8, entries), 1)
    step = lax.broadcasted_iota(jnp.int32, (8, entries), 0)
    place = jnp.where(at < half, at, at - half).astype(jnp.float32)
    times = jnp.zeros((8, entries), jnp.int32)
    for s in range(STEPS):
        times = jnp.where(step == s, timesteps[s], times)
    angle = times.astype(jnp.float32) * jnp.exp(-math.log(10000.0) * place / half)
    emb = jnp.where(at < half, jnp.cos(angle), jnp.sin(angle))
    for slot in range(2):
        made = jnp.dot(
            emb,
            time_weight[slot],
            precision=lax.Precision.HIGHEST,
            preferred_element_type=jnp.float32,
        )
        for s in range(STEPS):
            bias[s, slot : slot + 1, :] = made[s : s + 1]


def place():
    row_group = lax.axis_index("rows")
    at_end = (row_group == 0) | (row_group == lax.axis_size("rows") - 1)
    return lax.rem(row_group, 2), at_end


def first_kernel(step, info, own, far, gains, sw, part, n_own, n_far, wide, thin):
    count = jnp.max(info[0:1, :])
    odd, at_end = place()
    mine, by_far = load(own), load(far)
    if step == 0:
        mine, by_far = flip_if(odd, mine), flip_if(1 - odd, by_far)
    by_far = jnp.where(at_end, 0.0, by_far)
    gain = gains[0:1, :].reshape(1, 1, PAIR)
    normed, far_normed = normalise(mine, gain), normalise(by_far, gain)
    n_own[...] = normed
    n_far[...] = far_normed

    @pl.when(count > 1)
    def _():
        put_wide(wide, 0, flip(far_normed), normed)
        even, odd_sum = spatial(wide, True, (0,), sw, 0, odd)
        part[0], part[1] = even, odd_sum

    @pl.when(count == 1)
    def _():
        put_thin(thin, 0, halves(far_normed, flip(normed)))
        put_thin(thin, 1, normed)
        even, odd_sum = spatial(thin, False, (0, 1), sw, 0, odd)
        part[0, : FIELD], part[1, : FIELD] = even, odd_sum


def second_kernel(
    step, info, own, far, core, part, n_own, n_far, bias, gains, sw, tw, out, wide, thin, acc, center
):
    count = jnp.max(info[0:1, :])
    odd, at_end = place()
    mine, by_core = load(own), load(core)
    if step == 0:
        mine, by_core = flip_if(odd, mine), flip_if(1 - odd, by_core)
    core_normed = normalise(by_core, gains[0:1, :].reshape(1, 1, PAIR))

    @pl.when(count == 1)
    def _():
        put_thin(thin, 2, halves(flip(n_own[...]), core_normed))
        even, odd_sum = spatial(thin, False, (2,), sw, 0, odd)
        acc[0], acc[1] = part[0, :FIELD] + even, part[1, :FIELD] + odd_sum
        center[...] = mine

    @pl.when(count > 1)
    def _():
        normed = n_own[...]
        turned = flip(normed)
        put_wide(wide, 1, halves(n_far[...], turned), halves(turned, core_normed))
        put_wide(wide, 2, normed, flip(core_normed))
        even, odd_sum = spatial(wide, True, (1, 2), sw, 0, odd)
        even = part[0] + even + bias[step, 0:1, :]
        odd_sum = part[1] + odd_sum + bias[step, 0:1, :]
        half = FIELD
        u_even, u_odd = silu(even).astype(jnp.bfloat16), silu(odd_sum).astype(jnp.bfloat16)
        u0 = jnp.concatenate([u_even[:half], u_odd[:half]], axis=0)
        u1 = jnp.concatenate([u_even[half:], u_odd[half:]], axis=0)
        v0, v1 = temporal(u0, u1, tw, 0)
        v_even = jnp.concatenate([v0[:half], v1[:half]], axis=0)
        v_odd = jnp.concatenate([v0[half:], v1[half:]], axis=0)
        change = jnp.concatenate([even + v_even, odd_sum + v_odd], axis=1)
        change = change.reshape(FRAMES * J, 2 * GROUP, PAIR)
        by_far = load(far)
        if step == 0:
            by_far = flip_if(1 - odd, by_far)
        back = flip(mine)
        first = halves(by_far, back) + change[:, :GROUP]
        second = halves(back, by_core) + change[:, GROUP:]
        first = first.astype(jnp.bfloat16).astype(jnp.float32)
        second = second.astype(jnp.bfloat16).astype(jnp.float32)
        row = lax.broadcasted_iota(jnp.int32, first.shape, 1)
        first = jnp.where((row < HB) & at_end, 0.0, first)
        center[...] = halves(flip(first), flip(second))
        gain = gains[1:2, :].reshape(1, 1, PAIR)
        n_first, n_second = normalise(first, gain), normalise(second, gain)
        put_thin(thin, 0, n_first)
        put_thin(thin, 1, halves(flip(n_first), flip(n_second)))
        put_thin(thin, 2, n_second)
        even, odd_sum = spatial(thin, False, (0, 1, 2), sw, 1, odd)
        acc[0], acc[1] = even, odd_sum

    last = count - 1
    shift = bias[step, pl.ds(last, 1), :]
    even = (acc[0] + shift).reshape(J, FRAMES, GROUP, C)
    odd_sum = (acc[1] + shift).reshape(J, FRAMES, GROUP, C)
    u0, u1 = (
        jnp.concatenate(
            [silu(even[:, f]).reshape(-1, C), silu(odd_sum[:, f]).reshape(-1, C)], axis=0
        )
        for f in range(FRAMES)
    )
    v0, v1 = temporal(u0.astype(jnp.bfloat16), u1.astype(jnp.bfloat16), tw, last)
    half = J * GROUP
    for f, v in enumerate((v0, v1)):
        a_even, a_odd = even[:, f].reshape(half, C), odd_sum[:, f].reshape(half, C)
        change = jnp.concatenate([a_even + v[:half], a_odd + v[half:]], axis=1)
        result = center[f * J : (f + 1) * J] + change.reshape(J, GROUP, PAIR)
        if step == STEPS - 1:
            result = flip_if(odd, result)
        out[f * half : (f + 1) * half, :] = result.reshape(half, PAIR).astype(jnp.bfloat16)


VMEM = pl.BlockSpec(memory_space=pltpu.VMEM)


def call(kernel, name, outs, scratch, flops):
    return pl.pallas_call(
        kernel,
        out_shape=tuple(jax.ShapeDtypeStruct(shape, dtype) for shape, dtype in outs),
        out_specs=(VMEM,) * len(outs),
        scratch_shapes=[pltpu.VMEM(shape, dtype) for shape, dtype in scratch],
        compiler_params=pltpu.CompilerParams(vmem_limit_bytes=24 * 1024 * 1024),
        cost_estimate=pl.CostEstimate(
            flops=flops, bytes_accessed=1_000_000, transcendentals=400_000
        ),
        name=name,
    )


def prepare(bounds, timesteps, gains, time_weight):
    hbm = pl.BlockSpec(memory_space=pltpu.HBM)
    return pl.pallas_call(
        prepare_kernel,
        out_shape=(
            jax.ShapeDtypeStruct((8, 128), jnp.int32),
            jax.ShapeDtypeStruct((STEPS, 2, C), jnp.float32),
            jax.ShapeDtypeStruct((2, PAIR), jnp.float32),
        ),
        in_specs=[hbm, hbm, hbm, hbm],
        out_specs=(VMEM,) * 3,
        scratch_shapes=[
            pltpu.SMEM(bounds.shape, jnp.int32),
            pltpu.SMEM(timesteps.shape, jnp.int32),
            pltpu.VMEM(gains.shape, jnp.float32),
            pltpu.VMEM(time_weight.shape, jnp.float32),
            pltpu.SemaphoreType.DMA((4,)),
        ],
        compiler_params=pltpu.CompilerParams(vmem_limit_bytes=20 * 1024 * 1024),
        cost_estimate=pl.CostEstimate(
            flops=8_000_000_000, bytes_accessed=1_000_000, transcendentals=10_000
        ),
        name="prepare",
    )(bounds, timesteps, gains, time_weight)


WIDE = ((3, FRAMES, J + 2, 2 * GROUP, LANES), jnp.bfloat16)
THIN = ((3, J + 2, FRAMES * GROUP, LANES), jnp.bfloat16)
ROWS_F32 = ((FRAMES * J, GROUP, PAIR), jnp.float32)


def apply_blocks(step, info, own, far, core, bias, gains, sw, tw):
    part, n_own, n_far = call(
        functools.partial(first_kernel, step),
        "own_and_far_rows",
        [((2, 2 * FIELD, C), jnp.float32), ROWS_F32, ROWS_F32],
        [WIDE, THIN],
        2_000_000_000,
    )(info, own, far, gains, sw)
    (field,) = call(
        functools.partial(second_kernel, step),
        "residual_blocks",
        [((FIELD, PAIR), jnp.bfloat16)],
        [WIDE, THIN, ((2, FIELD, C), jnp.float32), ROWS_F32],
        4_000_000_000,
    )(info, own, far, core, part, n_own, n_far, bias, gains, sw, tw)
    return field


def body(state, bounds, timesteps, gains, spatial_weight, temporal_weight, time_weight):
    groups = lax.axis_size("rows")
    segments = lax.axis_size("segment")
    info, bias, gain_pairs = prepare(bounds, timesteps, gains[0], time_weight[0])
    sw = spatial_weight.reshape(2, 3, 3 * C, C)
    tw = temporal_weight.reshape(2, 3, C, C)
    ahead = [(i, (i + 1) % segments) for i in range(segments)]
    on_chip = [(i, i ^ 1) for i in range(groups)]
    off_chip = [(i, i + 1) for i in range(1, groups - 1, 2)]
    off_chip = off_chip + [(j, i) for i, j in off_chip] + [(0, 0), (groups - 1, groups - 1)]
    off_chip_ahead = [
        (a * groups + i, b * groups + j) for a, b in ahead for i, j in off_chip
    ]

    field = state.reshape(FRAMES, ROWS, HB, J, PAIR).transpose(0, 3, 1, 2, 4).reshape(FIELD, PAIR)
    for step in range(STEPS):
        own = lax.ppermute(field, "segment", ahead)
        far = lax.ppermute(field, ("segment", "rows"), off_chip_ahead)
        if step == 0:
            own, info, bias, gain_pairs = lax.optimization_barrier((own, info, bias, gain_pairs))
        core = lax.ppermute(own, "rows", on_chip)
        field = apply_blocks(step, info, own, far, core, bias, gain_pairs, sw, tw)
    field = field.reshape(FRAMES, J, ROWS, HB, PAIR).transpose(0, 2, 3, 1, 4)
    return field.reshape(1, FRAMES, ROWS, W * C)


def solution(mesh):
    placed = (
        P("segment", None, "rows", None),
        P(),
        P(),
        P("segment", None, None),
        P("segment", None, None, None, None, None),
        P("segment", None, None, None, None),
        P("segment", None, None, None),
    )
    return jax.shard_map(
        body,
        mesh=mesh,
        in_specs=placed,
        out_specs=P("segment", None, "rows", None),
        check_vma=False,
    )
```

```python
import functools
import math

import jax
import jax.numpy as jnp
from jax import lax
from jax.experimental import pallas as pl
from jax.experimental.pallas import tpu as pltpu
from jax.sharding import PartitionSpec as P

C = 320
W = 72
STEPS = 2
FRAMES = 2
ROWS = 2

HB = 4
J = W // 2 // HB
PAIR = 2 * C
GROUP = ROWS * HB
FIELD = FRAMES * J * GROUP
PAD = 64
LANES = PAIR + 256
EPS = 1e-06


def low_lanes(shape):
    return lax.broadcasted_iota(jnp.int32, shape, len(shape) - 1) < PAD


def normalise(value, gain):
    low = low_lanes(value[..., 256:384].shape)
    square = value * value
    middle = square[..., 256:384]
    first = square[..., 0:128] + square[..., 128:256] + jnp.where(low, middle, 0.0)
    second = square[..., 384:512] + square[..., 512:640] + jnp.where(low, 0.0, middle)
    scale = lax.rsqrt(jnp.sum(first, axis=-1, keepdims=True) / C + EPS)
    other = lax.rsqrt(jnp.sum(second, axis=-1, keepdims=True) / C + EPS)
    scaled = jnp.concatenate(
        [
            value[..., 0:256] * scale,
            value[..., 256:384] * jnp.where(low, scale, other),
            value[..., 384:640] * other,
        ],
        axis=-1,
    )
    return scaled * gain


def load(*refs):
    value = jnp.concatenate([ref[...].astype(jnp.float32) for ref in refs], axis=0)
    return value.reshape(FRAMES * J, GROUP, PAIR)


def flip(value):
    return pltpu.roll(value, HB, 1)


def flip_if(odd, value):
    return pltpu.roll(value, HB * odd, 1)


def halves(first, second):
    row = lax.broadcasted_iota(jnp.int32, first.shape, 1)
    return jnp.where(row < HB, first, second)


def shifted_h(value, by):
    rows = value.shape[0]
    moved = pltpu.roll(value, by % rows, 0)
    h = lax.rem(lax.broadcasted_iota(jnp.int32, value.shape, 0), HB)
    edge = 0 if by == 1 else HB - 1
    return jnp.where(h == edge, 0.0, moved)


def put(ref, at, value):
    middle = value[..., 256:384]
    low = low_lanes(middle.shape)
    ref[at + (slice(None), slice(0, PAIR))] = value.astype(jnp.bfloat16)
    ref[at + (slice(None), slice(PAIR, PAIR + 128))] = jnp.where(low, 0.0, middle).astype(
        jnp.bfloat16
    )
    ref[at + (slice(None), slice(PAIR + 128, LANES))] = jnp.where(low, middle, 0.0).astype(
        jnp.bfloat16
    )


def put_wide(ref, dy, first, second):
    tiles = jnp.concatenate([first, second], axis=1).reshape(FRAMES, J, 2 * GROUP, PAIR)
    put(ref, (dy, slice(None), slice(1, J + 1)), tiles)
    for f in range(FRAMES):
        put(ref, (dy, f, 0), shifted_h(tiles[f, J - 1], 1))
        put(ref, (dy, f, J + 1), shifted_h(tiles[f, 0], -1))


def put_thin(ref, dy, value):
    tiles = value.reshape(FRAMES, J, GROUP, PAIR)
    tiles = jnp.concatenate([tiles[0], tiles[1]], axis=1)
    put(ref, (dy, slice(1, J + 1)), tiles)
    put(ref, (dy, 0), shifted_h(tiles[J - 1], 1))
    put(ref, (dy, J + 1), shifted_h(tiles[0], -1))


def rows_of(ref, dy, j0, wide, start, stop):
    if wide:
        return ref[dy, :, j0 : j0 + J, :, start:stop].reshape(-1, stop - start)
    return ref[dy, j0 : j0 + J, :, start:stop].reshape(-1, stop - start)


def silu(value):
    return value * jax.nn.sigmoid(value)


def dot(a, b):
    return jnp.dot(a, b, preferred_element_type=jnp.float32)


def spatial(ref, wide, taps, weights, slot, odd):
    even_sum = odd_sum = None
    for dy in taps:
        at = dy + odd * (2 - 2 * dy)
        rows = functools.partial(rows_of, ref, dy, wide=wide)
        center = rows(1, start=0, stop=PAIR)
        before = [rows(0, start=PAIR, stop=PAIR + 128), rows(0, start=384, stop=PAIR)]
        after = [rows(2, start=0, stop=256), rows(2, start=PAIR + 128, stop=LANES)]
        filler = weights[slot, at, 0:PAD, :]
        kernel = weights[slot, at]
        turned = jnp.concatenate([kernel[C:], filler, kernel[:C]], axis=0)
        straight = jnp.concatenate([kernel, filler], axis=0)
        e = dot(jnp.concatenate([center] + before, axis=1), turned)
        o = dot(jnp.concatenate([center] + after, axis=1), straight)
        even_sum = e if even_sum is None else even_sum + e
        odd_sum = o if odd_sum is None else odd_sum + o
    return even_sum, odd_sum


def temporal(u0, u1, weights, slot):
    gap = jnp.zeros((u0.shape[0], PAD), u0.dtype)
    both = jnp.concatenate([u0, gap, u1, gap], axis=1)
    t0, t1, t2 = (weights[slot, tap] for tap in range(3))
    v0 = dot(both, jnp.concatenate([t1, t1[:PAD], t2, t2[:PAD]], axis=0))
    v1 = dot(both, jnp.concatenate([t0, t0[:PAD], t1, t1[:PAD]], axis=0))
    return v0, v1


def frequency_kernel(out):
    half = out.shape[1] // 2
    at = lax.broadcasted_iota(jnp.int32, out.shape, 1)
    index = jnp.where(at < half, at, at - half).astype(jnp.float32)
    out[...] = jnp.exp(-math.log(10000.0) * index / half)


def prepare_kernel(
    bounds_hbm,
    timesteps_hbm,
    gains_hbm,
    time_hbm,
    frequency,
    info,
    bias,
    gain_pairs,
    bounds,
    timesteps,
    gains,
    time_weight,
    sems,
):
    copies = [
        pltpu.make_async_copy(source, target, sems.at[n])
        for n, (source, target) in enumerate(
            (
                (bounds_hbm, bounds),
                (timesteps_hbm, timesteps),
                (gains_hbm, gains),
                (time_hbm, time_weight),
            )
        )
    ]
    for copy in copies:
        copy.start()
    for copy in copies:
        copy.wait()
    segment = lax.axis_index("segment")
    info[...] = jnp.full(info.shape, bounds[segment + 1] - bounds[segment], jnp.int32)
    gain_pairs[...] = jnp.concatenate([gains[...], gains[...]], axis=1)
    entries = time_weight.shape[1]
    half = entries // 2
    at = lax.broadcasted_iota(jnp.int32, (8, entries), 1)
    step = lax.broadcasted_iota(jnp.int32, (8, entries), 0)
    times = jnp.zeros((8, entries), jnp.int32)
    for s in range(STEPS):
        times = jnp.where(step == s, timesteps[s], times)
    angle = times.astype(jnp.float32) * frequency[...]
    emb = jnp.where(at < half, jnp.cos(angle), jnp.sin(angle))
    for slot in range(2):
        made = jnp.dot(
            emb,
            time_weight[slot],
            precision=lax.Precision.HIGHEST,
            preferred_element_type=jnp.float32,
        )
        for s in range(STEPS):
            bias[s, slot : slot + 1, :] = made[s : s + 1]


def place():
    row_group = lax.axis_index("rows")
    at_end = (row_group == 0) | (row_group == lax.axis_size("rows") - 1)
    return lax.rem(row_group, 2), at_end


def first_kernel(
    step, info, own0, own1, core0, core1, gains, sw, part, n_own, n_core, wide, thin
):
    count = jnp.max(info[0:1, :])
    odd, _ = place()
    mine, by_core = load(own0, own1), load(core0, core1)
    if step == 0:
        mine, by_core = flip_if(odd, mine), flip_if(1 - odd, by_core)
    gain = gains[0:1, :].reshape(1, 1, PAIR)
    normed, core_normed = normalise(mine, gain), normalise(by_core, gain)
    n_own[...] = normed
    n_core[...] = core_normed

    @pl.when(count > 1)
    def _():
        put_wide(wide, 2, normed, flip(core_normed))
        even, odd_sum = spatial(wide, True, (2,), sw, 0, odd)
        part[0], part[1] = even, odd_sum

    @pl.when(count == 1)
    def _():
        put_thin(thin, 1, normed)
        put_thin(thin, 2, halves(flip(normed), core_normed))
        even, odd_sum = spatial(thin, False, (1, 2), sw, 0, odd)
        part[0, :FIELD], part[1, :FIELD] = even, odd_sum


def second_kernel(
    step,
    info,
    own0,
    own1,
    core0,
    core1,
    far,
    part,
    n_own,
    n_core,
    bias,
    gains,
    sw,
    tw,
    *outs_and_scratch,
):
    outs, (wide, thin, acc, center) = outs_and_scratch[:-4], outs_and_scratch[-4:]
    count = jnp.max(info[0:1, :])
    odd, at_end = place()
    mine, by_far = load(own0, own1), load(far)
    if step == 0:
        mine, by_far = flip_if(odd, mine), flip_if(1 - odd, by_far)
    by_far = jnp.where(at_end, 0.0, by_far)
    far_normed = normalise(by_far, gains[0:1, :].reshape(1, 1, PAIR))

    @pl.when(count == 1)
    def _():
        put_thin(thin, 0, halves(far_normed, flip(n_own[...])))
        even, odd_sum = spatial(thin, False, (0,), sw, 0, odd)
        acc[0], acc[1] = part[0, :FIELD] + even, part[1, :FIELD] + odd_sum
        center[...] = mine

    @pl.when(count > 1)
    def _():
        normed = n_own[...]
        turned = flip(normed)
        put_wide(wide, 0, flip(far_normed), normed)
        put_wide(wide, 1, halves(far_normed, turned), halves(turned, n_core[...]))
        even, odd_sum = spatial(wide, True, (0, 1), sw, 0, odd)
        even = part[0] + even + bias[step, 0:1, :]
        odd_sum = part[1] + odd_sum + bias[step, 0:1, :]
        half = FIELD
        u_even, u_odd = silu(even).astype(jnp.bfloat16), silu(odd_sum).astype(jnp.bfloat16)
        u0 = jnp.concatenate([u_even[:half], u_odd[:half]], axis=0)
        u1 = jnp.concatenate([u_even[half:], u_odd[half:]], axis=0)
        v0, v1 = temporal(u0, u1, tw, 0)
        v_even = jnp.concatenate([v0[:half], v1[:half]], axis=0)
        v_odd = jnp.concatenate([v0[half:], v1[half:]], axis=0)
        change = jnp.concatenate([even + v_even, odd_sum + v_odd], axis=1)
        change = change.reshape(FRAMES * J, 2 * GROUP, PAIR)
        by_core = load(core0, core1)
        if step == 0:
            by_core = flip_if(1 - odd, by_core)
        back = flip(mine)
        first = halves(by_far, back) + change[:, :GROUP]
        second = halves(back, by_core) + change[:, GROUP:]
        first = first.astype(jnp.bfloat16).astype(jnp.float32)
        second = second.astype(jnp.bfloat16).astype(jnp.float32)
        row = lax.broadcasted_iota(jnp.int32, first.shape, 1)
        first = jnp.where((row < HB) & at_end, 0.0, first)
        center[...] = halves(flip(first), flip(second))
        gain = gains[1:2, :].reshape(1, 1, PAIR)
        n_first, n_second = normalise(first, gain), normalise(second, gain)
        put_thin(thin, 0, n_first)
        put_thin(thin, 1, halves(flip(n_first), flip(n_second)))
        put_thin(thin, 2, n_second)
        even, odd_sum = spatial(thin, False, (0, 1, 2), sw, 1, odd)
        acc[0], acc[1] = even, odd_sum

    last = count - 1
    shift = bias[step, pl.ds(last, 1), :]
    even = (acc[0] + shift).reshape(J, FRAMES, GROUP, C)
    odd_sum = (acc[1] + shift).reshape(J, FRAMES, GROUP, C)
    u0, u1 = (
        jnp.concatenate(
            [silu(even[:, f]).reshape(-1, C), silu(odd_sum[:, f]).reshape(-1, C)], axis=0
        )
        for f in range(FRAMES)
    )
    v0, v1 = temporal(u0.astype(jnp.bfloat16), u1.astype(jnp.bfloat16), tw, last)
    half = J * GROUP
    for f, v in enumerate((v0, v1)):
        a_even, a_odd = even[:, f].reshape(half, C), odd_sum[:, f].reshape(half, C)
        change = jnp.concatenate([a_even + v[:half], a_odd + v[half:]], axis=1)
        result = center[f * J : (f + 1) * J] + change.reshape(J, GROUP, PAIR)
        if step == STEPS - 1:
            result = flip_if(odd, result)
        result = result.reshape(half, PAIR).astype(jnp.bfloat16)
        outs[0][f * half : (f + 1) * half, :] = result
        if step < STEPS - 1:
            outs[1 + f][...] = result


VMEM = pl.BlockSpec(memory_space=pltpu.VMEM)


def call(kernel, name, outs, scratch, flops):
    return pl.pallas_call(
        kernel,
        out_shape=tuple(jax.ShapeDtypeStruct(shape, dtype) for shape, dtype in outs),
        out_specs=(VMEM,) * len(outs),
        scratch_shapes=[pltpu.VMEM(shape, dtype) for shape, dtype in scratch],
        compiler_params=pltpu.CompilerParams(vmem_limit_bytes=24 * 1024 * 1024),
        cost_estimate=pl.CostEstimate(
            flops=flops, bytes_accessed=flops // 4_000, transcendentals=0
        ),
        name=name,
    )


def prepare(bounds, timesteps, gains, time_weight):
    hbm = pl.BlockSpec(memory_space=pltpu.HBM)
    (frequency,) = call(
        frequency_kernel, "frequency", [((8, time_weight.shape[1]), jnp.float32)], [], 4_000_000_000
    )()
    return pl.pallas_call(
        prepare_kernel,
        out_shape=(
            jax.ShapeDtypeStruct((8, 128), jnp.int32),
            jax.ShapeDtypeStruct((STEPS, 2, C), jnp.float32),
            jax.ShapeDtypeStruct((2, PAIR), jnp.float32),
        ),
        in_specs=[hbm, hbm, hbm, hbm, VMEM],
        out_specs=(VMEM,) * 3,
        scratch_shapes=[
            pltpu.SMEM(bounds.shape, jnp.int32),
            pltpu.SMEM(timesteps.shape, jnp.int32),
            pltpu.VMEM(gains.shape, jnp.float32),
            pltpu.VMEM(time_weight.shape, jnp.float32),
            pltpu.SemaphoreType.DMA((4,)),
        ],
        compiler_params=pltpu.CompilerParams(vmem_limit_bytes=20 * 1024 * 1024),
        cost_estimate=pl.CostEstimate(
            flops=8_000_000_000, bytes_accessed=1_000_000, transcendentals=10_000
        ),
        name="prepare",
    )(bounds, timesteps, gains, time_weight, frequency)


WIDE = ((3, FRAMES, J + 2, 2 * GROUP, LANES), jnp.bfloat16)
THIN = ((3, J + 2, FRAMES * GROUP, LANES), jnp.bfloat16)
ROWS_F32 = ((FRAMES * J, GROUP, PAIR), jnp.float32)


def apply_blocks(step, info, own, core, far, bias, gains, sw, tw):
    part, n_own, n_core = call(
        functools.partial(first_kernel, step),
        "own_and_core_rows",
        [((2, 2 * FIELD, C), jnp.float32), ROWS_F32, ROWS_F32],
        [WIDE, THIN],
        1_000_000,
    )(info, *own, *core, gains, sw)
    outs = [((FIELD, PAIR), jnp.bfloat16)]
    if step < STEPS - 1:
        outs += [((FIELD // FRAMES, PAIR), jnp.bfloat16)] * FRAMES
    return call(
        functools.partial(second_kernel, step),
        "residual_blocks",
        outs,
        [WIDE, THIN, ((2, FIELD, C), jnp.float32), ROWS_F32],
        4_000_000_000,
    )(info, *own, *core, far, part, n_own, n_core, bias, gains, sw, tw)


def body(state, bounds, timesteps, gains, spatial_weight, temporal_weight, time_weight):
    groups = lax.axis_size("rows")
    segments = lax.axis_size("segment")
    info, bias, gain_pairs = prepare(bounds, timesteps, gains[0], time_weight[0])
    sw = spatial_weight.reshape(2, 3, 3 * C, C)
    tw = temporal_weight.reshape(2, 3, C, C)
    ahead = [(i, (i + 1) % segments) for i in range(segments)]
    on_chip = [(i, i ^ 1) for i in range(groups)]
    off_chip = [(i, i + 1) for i in range(1, groups - 1, 2)]
    off_chip = off_chip + [(j, i) for i, j in off_chip] + [(0, 0), (groups - 1, groups - 1)]
    off_chip_ahead = [
        (a * groups + i, b * groups + j) for a, b in ahead for i, j in off_chip
    ]

    field = state.reshape(FRAMES, ROWS, HB, J, PAIR).transpose(0, 3, 1, 2, 4).reshape(FIELD, PAIR)
    frames = (field[: FIELD // FRAMES], field[FIELD // FRAMES :])
    for step in range(STEPS):
        own = [lax.ppermute(frame, "segment", ahead) for frame in frames]
        far = lax.ppermute(field, ("segment", "rows"), off_chip_ahead)
        if step == 0:
            own, info, bias, gain_pairs = lax.optimization_barrier((own, info, bias, gain_pairs))
        core = [lax.ppermute(frame, "rows", on_chip) for frame in own]
        field, *frames = apply_blocks(step, info, own, core, far, bias, gain_pairs, sw, tw)
    field = field.reshape(FRAMES, J, ROWS, HB, PAIR).transpose(0, 2, 3, 1, 4)
    return field.reshape(1, FRAMES, ROWS, W * C)


def solution(mesh):
    placed = (
        P("segment", None, "rows", None),
        P(),
        P(),
        P("segment", None, None),
        P("segment", None, None, None, None, None),
        P("segment", None, None, None, None),
        P("segment", None, None, None),
    )
    return jax.shard_map(
        body,
        mesh=mesh,
        in_specs=placed,
        out_specs=P("segment", None, "rows", None),
        check_vma=False,
    )
```

```python
import functools
import math

import jax
import jax.numpy as jnp
from jax import lax
from jax.experimental import pallas as pl
from jax.experimental.pallas import tpu as pltpu
from jax.sharding import PartitionSpec as P

C = 320
W = 72
STEPS = 2
FRAMES = 2
ROWS = 2

HB = 4
J = W // 2 // HB
PAIR = 2 * C
GROUP = ROWS * HB
FIELD = FRAMES * J * GROUP
PAD = 64
LANES = PAIR + 256
EPS = 1e-06


def low_lanes(shape):
    return lax.broadcasted_iota(jnp.int32, shape, len(shape) - 1) < PAD


def normalise(value, gain):
    low = low_lanes(value[..., 256:384].shape)
    square = value * value
    middle = square[..., 256:384]
    first = square[..., 0:128] + square[..., 128:256] + jnp.where(low, middle, 0.0)
    second = square[..., 384:512] + square[..., 512:640] + jnp.where(low, 0.0, middle)
    scale = lax.rsqrt(jnp.sum(first, axis=-1, keepdims=True) / C + EPS)
    other = lax.rsqrt(jnp.sum(second, axis=-1, keepdims=True) / C + EPS)
    scaled = jnp.concatenate(
        [
            value[..., 0:256] * scale,
            value[..., 256:384] * jnp.where(low, scale, other),
            value[..., 384:640] * other,
        ],
        axis=-1,
    )
    return scaled * gain


def load(ref):
    return ref[...].astype(jnp.float32).reshape(FRAMES * J, GROUP, PAIR)


def flip(value):
    return pltpu.roll(value, HB, 1)


def flip_if(odd, value):
    return pltpu.roll(value, HB * odd, 1)


def halves(first, second):
    row = lax.broadcasted_iota(jnp.int32, first.shape, 1)
    return jnp.where(row < HB, first, second)


def shifted_h(value, by):
    rows = value.shape[0]
    moved = pltpu.roll(value, by % rows, 0)
    h = lax.rem(lax.broadcasted_iota(jnp.int32, value.shape, 0), HB)
    edge = 0 if by == 1 else HB - 1
    return jnp.where(h == edge, 0.0, moved)


def put(ref, at, value):
    middle = value[..., 256:384]
    low = low_lanes(middle.shape)
    ref[at + (slice(None), slice(0, PAIR))] = value.astype(jnp.bfloat16)
    ref[at + (slice(None), slice(PAIR, PAIR + 128))] = jnp.where(low, 0.0, middle).astype(
        jnp.bfloat16
    )
    ref[at + (slice(None), slice(PAIR + 128, LANES))] = jnp.where(low, middle, 0.0).astype(
        jnp.bfloat16
    )


def put_wide(ref, dy, first, second):
    tiles = jnp.concatenate([first, second], axis=1).reshape(FRAMES, J, 2 * GROUP, PAIR)
    put(ref, (dy, slice(None), slice(1, J + 1)), tiles)
    for f in range(FRAMES):
        put(ref, (dy, f, 0), shifted_h(tiles[f, J - 1], 1))
        put(ref, (dy, f, J + 1), shifted_h(tiles[f, 0], -1))


def put_thin(ref, dy, value):
    tiles = value.reshape(FRAMES, J, GROUP, PAIR)
    tiles = jnp.concatenate([tiles[0], tiles[1]], axis=1)
    put(ref, (dy, slice(1, J + 1)), tiles)
    put(ref, (dy, 0), shifted_h(tiles[J - 1], 1))
    put(ref, (dy, J + 1), shifted_h(tiles[0], -1))


def rows_of(ref, dy, j0, wide, start, stop):
    if wide:
        return ref[dy, :, j0 : j0 + J, :, start:stop].reshape(-1, stop - start)
    return ref[dy, j0 : j0 + J, :, start:stop].reshape(-1, stop - start)


def silu(value):
    return value * jax.nn.sigmoid(value)


def dot(a, b):
    return jnp.dot(a, b, preferred_element_type=jnp.float32)


def spatial(ref, wide, taps, weights, slot, odd):
    even_sum = odd_sum = None
    for dy in taps:
        at = dy + odd * (2 - 2 * dy)
        rows = functools.partial(rows_of, ref, dy, wide=wide)
        center = rows(1, start=0, stop=PAIR)
        before = [rows(0, start=PAIR, stop=PAIR + 128), rows(0, start=384, stop=PAIR)]
        after = [rows(2, start=0, stop=256), rows(2, start=PAIR + 128, stop=LANES)]
        filler = weights[slot, at, 0:PAD, :]
        kernel = weights[slot, at]
        turned = jnp.concatenate([kernel[C:], filler, kernel[:C]], axis=0)
        straight = jnp.concatenate([kernel, filler], axis=0)
        e = dot(jnp.concatenate([center] + before, axis=1), turned)
        o = dot(jnp.concatenate([center] + after, axis=1), straight)
        even_sum = e if even_sum is None else even_sum + e
        odd_sum = o if odd_sum is None else odd_sum + o
    return even_sum, odd_sum


def temporal(u0, u1, weights, slot):
    gap = jnp.zeros((u0.shape[0], PAD), u0.dtype)
    both = jnp.concatenate([u0, gap, u1, gap], axis=1)
    t0, t1, t2 = (weights[slot, tap] for tap in range(3))
    v0 = dot(both, jnp.concatenate([t1, t1[:PAD], t2, t2[:PAD]], axis=0))
    v1 = dot(both, jnp.concatenate([t0, t0[:PAD], t1, t1[:PAD]], axis=0))
    return v0, v1


def frequency_kernel(out):
    half = out.shape[1] // 2
    at = lax.broadcasted_iota(jnp.int32, out.shape, 1)
    index = jnp.where(at < half, at, at - half).astype(jnp.float32)
    out[...] = jnp.exp(-math.log(10000.0) * index / half)


def prepare_kernel(
    timesteps_hbm, gains_hbm, time_hbm, frequency, bias, gain_pairs, timesteps, gains, time_weight, sems
):
    copies = [
        pltpu.make_async_copy(source, target, sems.at[n])
        for n, (source, target) in enumerate(
            (
                (timesteps_hbm, timesteps),
                (gains_hbm, gains),
                (time_hbm, time_weight),
            )
        )
    ]
    for copy in copies:
        copy.start()
    for copy in copies:
        copy.wait()
    gain_pairs[...] = jnp.concatenate([gains[...], gains[...]], axis=1)
    entries = time_weight.shape[1]
    half = entries // 2
    at = lax.broadcasted_iota(jnp.int32, (8, entries), 1)
    step = lax.broadcasted_iota(jnp.int32, (8, entries), 0)
    times = jnp.zeros((8, entries), jnp.int32)
    for s in range(STEPS):
        times = jnp.where(step == s, timesteps[s], times)
    angle = times.astype(jnp.float32) * frequency[...]
    emb = jnp.where(at < half, jnp.cos(angle), jnp.sin(angle))
    for slot in range(2):
        made = jnp.dot(
            emb,
            time_weight[slot],
            precision=lax.Precision.HIGHEST,
            preferred_element_type=jnp.float32,
        )
        for s in range(STEPS):
            bias[s, slot : slot + 1, :] = made[s : s + 1]


def place(e):
    row_group = lax.axis_index("rows")
    at_end = (row_group == 0) | (row_group == lax.axis_size("rows") - 1)
    return lax.rem(row_group, 2), at_end, lax.axis_index("segment") == e


def follows(e):
    return lax.axis_index("segment") == (e + 1) % lax.axis_size("segment")


def first_kernel(step, e, *refs):
    inputs, refs = refs[: 2 + 2 * step], refs[2 + 2 * step :]
    gains, sw, part, n_own, n_far, raw_own, raw_far, wide, thin = refs
    odd, at_end, two = place(e)
    mine, by_far = load(inputs[0]), load(inputs[1])
    if step == 0:
        mine, by_far = flip_if(odd, mine), flip_if(1 - odd, by_far)
    else:
        late = follows(e)
        near = inputs[3][...].astype(jnp.float32).reshape(FRAMES * J, HB, PAIR)
        mine = jnp.where(late, load(inputs[2]), mine)
        by_far = jnp.where(late, jnp.concatenate([near, near], axis=1), by_far)
    by_far = jnp.where(at_end, 0.0, by_far)
    raw_own[...] = mine
    raw_far[...] = by_far
    gain = gains[0:1, :].reshape(1, 1, PAIR)
    normed, far_normed = normalise(mine, gain), normalise(by_far, gain)
    n_own[...] = normed
    n_far[...] = far_normed

    @pl.when(two)
    def _():
        put_wide(wide, 0, flip(far_normed), normed)
        even, odd_sum = spatial(wide, True, (0,), sw, 0, odd)
        part[0], part[1] = even, odd_sum

    @pl.when(jnp.logical_not(two))
    def _():
        put_thin(thin, 0, halves(far_normed, flip(normed)))
        put_thin(thin, 1, normed)
        even, odd_sum = spatial(thin, False, (0, 1), sw, 0, odd)
        part[0, :FIELD], part[1, :FIELD] = even, odd_sum


def second_kernel(step, e, counts, *refs):
    cores, refs = refs[: 1 + step], refs[1 + step :]
    part, n_own, n_far, raw_own, raw_far, bias, gains, sw, tw = refs[:9]
    outs, (wide, thin, acc, center) = refs[9:-4], refs[-4:]
    odd, at_end, two = place(e)

    def from_core():
        by_core = load(cores[0])
        if step == 0:
            return flip_if(1 - odd, by_core)
        return jnp.where(follows(e), load(cores[1]), by_core)

    gain = gains[0:1, :].reshape(1, 1, PAIR)

    def one_block():
        core_normed = normalise(from_core(), gain)
        put_thin(thin, 2, halves(flip(n_own[...]), core_normed))
        even, odd_sum = spatial(thin, False, (2,), sw, 0, odd)
        acc[0], acc[1] = part[0, :FIELD] + even, part[1, :FIELD] + odd_sum
        center[...] = raw_own[...]

    def two_blocks():
        by_core = from_core()
        core_normed = normalise(by_core, gain)
        normed = n_own[...]
        turned = flip(normed)
        put_wide(wide, 1, halves(n_far[...], turned), halves(turned, core_normed))
        put_wide(wide, 2, normed, flip(core_normed))
        even, odd_sum = spatial(wide, True, (1, 2), sw, 0, odd)
        even = part[0] + even + bias[step, 0:1, :]
        odd_sum = part[1] + odd_sum + bias[step, 0:1, :]
        half = FIELD
        u_even, u_odd = silu(even).astype(jnp.bfloat16), silu(odd_sum).astype(jnp.bfloat16)
        u0 = jnp.concatenate([u_even[:half], u_odd[:half]], axis=0)
        u1 = jnp.concatenate([u_even[half:], u_odd[half:]], axis=0)
        v0, v1 = temporal(u0, u1, tw, 0)
        v_even = jnp.concatenate([v0[:half], v1[:half]], axis=0)
        v_odd = jnp.concatenate([v0[half:], v1[half:]], axis=0)
        change = jnp.concatenate([even + v_even, odd_sum + v_odd], axis=1)
        change = change.reshape(FRAMES * J, 2 * GROUP, PAIR)
        back = flip(raw_own[...])
        first = halves(raw_far[...], back) + change[:, :GROUP]
        second = halves(back, by_core) + change[:, GROUP:]
        first = first.astype(jnp.bfloat16).astype(jnp.float32)
        second = second.astype(jnp.bfloat16).astype(jnp.float32)
        row = lax.broadcasted_iota(jnp.int32, first.shape, 1)
        first = jnp.where((row < HB) & at_end, 0.0, first)
        center[...] = halves(flip(first), flip(second))
        next_gain = gains[1:2, :].reshape(1, 1, PAIR)
        n_first, n_second = normalise(first, next_gain), normalise(second, next_gain)
        put_thin(thin, 0, n_first)
        put_thin(thin, 1, halves(flip(n_first), flip(n_second)))
        put_thin(thin, 2, n_second)
        acc[0], acc[1] = spatial(thin, False, (0, 1, 2), sw, 1, odd)

    def finish(last):
        shift = bias[step, pl.ds(last, 1), :]
        even = (acc[0] + shift).reshape(J, FRAMES, GROUP, C)
        odd_sum = (acc[1] + shift).reshape(J, FRAMES, GROUP, C)
        u0, u1 = (
            jnp.concatenate(
                [silu(even[:, f]).reshape(-1, C), silu(odd_sum[:, f]).reshape(-1, C)], axis=0
            )
            for f in range(FRAMES)
        )
        v0, v1 = temporal(u0.astype(jnp.bfloat16), u1.astype(jnp.bfloat16), tw, last)
        half = J * GROUP
        for f, v in enumerate((v0, v1)):
            a_even, a_odd = even[:, f].reshape(half, C), odd_sum[:, f].reshape(half, C)
            change = jnp.concatenate([a_even + v[:half], a_odd + v[half:]], axis=1)
            result = center[f * J : (f + 1) * J] + change.reshape(J, GROUP, PAIR)
            if step == STEPS - 1:
                result = flip_if(odd, result)
            if len(outs) > 1:
                near = result[:, :HB].reshape(half // ROWS, PAIR)
                outs[1][f * half // ROWS : (f + 1) * half // ROWS, :] = near.astype(jnp.bfloat16)
            outs[0][f * half : (f + 1) * half, :] = result.reshape(half, PAIR).astype(jnp.bfloat16)

    if counts == (1,):

        @pl.when(jnp.logical_not(two))
        def _():
            one_block()
            finish(0)

    elif counts == (2,):

        @pl.when(two)
        def _():
            two_blocks()
            finish(1)

    else:
        pl.when(two)(two_blocks)
        pl.when(jnp.logical_not(two))(one_block)
        finish(two.astype(jnp.int32))


VMEM = pl.BlockSpec(memory_space=pltpu.VMEM)


def call(kernel, name, outs, scratch, flops):
    return pl.pallas_call(
        kernel,
        out_shape=tuple(jax.ShapeDtypeStruct(shape, dtype) for shape, dtype in outs),
        out_specs=(VMEM,) * len(outs),
        scratch_shapes=[pltpu.VMEM(shape, dtype) for shape, dtype in scratch],
        compiler_params=pltpu.CompilerParams(vmem_limit_bytes=24 * 1024 * 1024),
        cost_estimate=pl.CostEstimate(
            flops=flops, bytes_accessed=1_000_000, transcendentals=400_000
        ),
        name=name,
    )


def prepare(timesteps, gains, time_weight):
    hbm = pl.BlockSpec(memory_space=pltpu.HBM)
    (frequency,) = call(
        frequency_kernel, "frequency", [((8, time_weight.shape[1]), jnp.float32)], [], 4_000_000_000
    )()
    return pl.pallas_call(
        prepare_kernel,
        out_shape=(
            jax.ShapeDtypeStruct((STEPS, 2, C), jnp.float32),
            jax.ShapeDtypeStruct((2, PAIR), jnp.float32),
        ),
        in_specs=[hbm, hbm, hbm, VMEM],
        out_specs=(VMEM,) * 2,
        scratch_shapes=[
            pltpu.SMEM(timesteps.shape, jnp.int32),
            pltpu.VMEM(gains.shape, jnp.float32),
            pltpu.VMEM(time_weight.shape, jnp.float32),
            pltpu.SemaphoreType.DMA((3,)),
        ],
        compiler_params=pltpu.CompilerParams(vmem_limit_bytes=20 * 1024 * 1024),
        cost_estimate=pl.CostEstimate(
            flops=8_000_000_000, bytes_accessed=1_000_000, transcendentals=10_000
        ),
        name="prepare",
    )(timesteps, gains, time_weight, frequency)


WIDE = ((3, FRAMES, J + 2, 2 * GROUP, LANES), jnp.bfloat16)
THIN = ((3, J + 2, FRAMES * GROUP, LANES), jnp.bfloat16)
ROWS_F32 = ((FRAMES * J, GROUP, PAIR), jnp.float32)


def own_and_far(step, e, inputs, gains, sw):
    return call(
        functools.partial(first_kernel, step, e),
        "own_and_far_rows",
        [((2, 2 * FIELD, C), jnp.float32)] + [ROWS_F32] * 4,
        [WIDE, THIN],
        2_000_000_000,
    )(*inputs, gains, sw)


def remaining(step, e, counts, cores, parts, bias, gains, sw, tw):
    outs = [((FIELD, PAIR), jnp.bfloat16)]
    if counts == (2,):
        outs.append(((FIELD // ROWS, PAIR), jnp.bfloat16))
    return call(
        functools.partial(second_kernel, step, e, counts),
        "residual_blocks_" + "_or_".join(map(str, counts)),
        outs,
        [WIDE, THIN, ((2, FIELD, C), jnp.float32), ROWS_F32],
        4_000_000_000,
    )(*cores, *parts, bias, gains, sw, tw)


def program(e, state, timesteps, gains, spatial_weight, temporal_weight, time_weight):
    groups = lax.axis_size("rows")
    segments = lax.axis_size("segment")
    follower = (e + 1) % segments
    bias, gain_pairs = prepare(timesteps, gains[0], time_weight[0])
    sw = spatial_weight.reshape(2, 3, 3 * C, C)
    tw = temporal_weight.reshape(2, 3, C, C)
    on_chip = [(i, i ^ 1) for i in range(groups)]
    off_chip = [(i, i + 1) for i in range(1, groups - 1, 2)]
    off_chip = off_chip + [(j, i) for i, j in off_chip]
    same = [(i, i) for i in range(groups)]
    ahead = [(k, (k + 1) % segments) for k in range(segments)]
    early = [(k, n) for k, n in ahead if k != e]
    rest = [(k, k) for k in range(segments) if k != follower]

    def send(value, along, rows):
        pairs = [(a * groups + i, b * groups + j) for a, b in along for i, j in rows]
        return lax.ppermute(value, ("segment", "rows"), pairs)

    field = state.reshape(FRAMES, ROWS, HB, J, PAIR).transpose(0, 3, 1, 2, 4).reshape(FIELD, PAIR)
    own = send(field, ahead, same)
    far = send(field, ahead, off_chip)
    own, bias, gain_pairs = lax.optimization_barrier((own, bias, gain_pairs))
    core = send(own, [(k, k) for k in range(segments)], on_chip)
    parts = own_and_far(0, e, (own, far), gain_pairs, sw)
    (field,) = remaining(0, e, (1,), (core,), parts, bias, gain_pairs, sw, tw)
    own = send(field, early, same)
    far = send(field, early, off_chip)
    parts, _ = lax.optimization_barrier((parts, field))
    late_field, late_near = remaining(0, e, (2,), (core,), parts, bias, gain_pairs, sw, tw)
    late_own = send(late_field, [(e, follower)], same)
    late_far = send(late_near, [(e, follower)], off_chip)
    own, far, late_far = lax.optimization_barrier((own, far, late_far))
    core = send(own, rest, on_chip)
    late_own, core = lax.optimization_barrier((late_own, core))
    late_core = send(late_own, [(follower, follower)], on_chip)
    parts = own_and_far(1, e, (own, far, late_own, late_far), gain_pairs, sw)
    (field,) = remaining(1, e, (1, 2), (core, late_core), parts, bias, gain_pairs, sw, tw)
    field = field.reshape(FRAMES, J, ROWS, HB, PAIR).transpose(0, 2, 3, 1, 4)
    return field.reshape(1, FRAMES, ROWS, W * C)


def body(state, bounds, timesteps, gains, spatial_weight, temporal_weight, time_weight):
    counts = bounds[1:] - bounds[:-1]
    segments = lax.axis_size("segment")
    return lax.switch(
        jnp.argmax(counts).astype(jnp.int32),
        [functools.partial(program, e) for e in range(segments)],
        state,
        timesteps,
        gains,
        spatial_weight,
        temporal_weight,
        time_weight,
    )


def solution(mesh):
    placed = (
        P("segment", None, "rows", None),
        P(),
        P(),
        P("segment", None, None),
        P("segment", None, None, None, None, None),
        P("segment", None, None, None, None),
        P("segment", None, None, None),
    )
    return jax.shard_map(
        body,
        mesh=mesh,
        in_specs=placed,
        out_specs=P("segment", None, "rows", None),
        check_vma=False,
    )
```

```python
import functools
import math

import jax
import jax.numpy as jnp
from jax import lax
from jax.experimental import pallas as pl
from jax.experimental.pallas import tpu as pltpu
from jax.sharding import PartitionSpec as P

C = 320
W = 72
STEPS = 2
FRAMES = 2
ROWS = 2

HB = 4
J = W // 2 // HB
PAIR = 2 * C
GROUP = ROWS * HB
FIELD = FRAMES * J * GROUP
PAD = 64
LANES = PAIR + 256
EPS = 1e-06


def low_lanes(shape):
    return lax.broadcasted_iota(jnp.int32, shape, len(shape) - 1) < PAD


def normalise(value, gain):
    low = low_lanes(value[..., 256:384].shape)
    square = value * value
    middle = square[..., 256:384]
    first = square[..., 0:128] + square[..., 128:256] + jnp.where(low, middle, 0.0)
    second = square[..., 384:512] + square[..., 512:640] + jnp.where(low, 0.0, middle)
    scale = lax.rsqrt(jnp.sum(first, axis=-1, keepdims=True) / C + EPS)
    other = lax.rsqrt(jnp.sum(second, axis=-1, keepdims=True) / C + EPS)
    scaled = jnp.concatenate(
        [
            value[..., 0:256] * scale,
            value[..., 256:384] * jnp.where(low, scale, other),
            value[..., 384:640] * other,
        ],
        axis=-1,
    )
    return scaled * gain


def load(ref):
    return ref[...].astype(jnp.float32).reshape(FRAMES * J, GROUP, PAIR)


def flip(value):
    return pltpu.roll(value, HB, 1)


def flip_if(odd, value):
    return pltpu.roll(value, HB * odd, 1)


def halves(first, second):
    row = lax.broadcasted_iota(jnp.int32, first.shape, 1)
    return jnp.where(row < HB, first, second)


def shifted_h(value, by):
    rows = value.shape[0]
    moved = pltpu.roll(value, by % rows, 0)
    h = lax.rem(lax.broadcasted_iota(jnp.int32, value.shape, 0), HB)
    edge = 0 if by == 1 else HB - 1
    return jnp.where(h == edge, 0.0, moved)


def put(ref, at, value):
    middle = value[..., 256:384]
    low = low_lanes(middle.shape)
    ref[at + (slice(None), slice(0, PAIR))] = value.astype(jnp.bfloat16)
    ref[at + (slice(None), slice(PAIR, PAIR + 128))] = jnp.where(low, 0.0, middle).astype(
        jnp.bfloat16
    )
    ref[at + (slice(None), slice(PAIR + 128, LANES))] = jnp.where(low, middle, 0.0).astype(
        jnp.bfloat16
    )


def put_wide(ref, dy, first, second):
    tiles = jnp.concatenate([first, second], axis=1).reshape(FRAMES, J, 2 * GROUP, PAIR)
    put(ref, (dy, slice(None), slice(1, J + 1)), tiles)
    for f in range(FRAMES):
        put(ref, (dy, f, 0), shifted_h(tiles[f, J - 1], 1))
        put(ref, (dy, f, J + 1), shifted_h(tiles[f, 0], -1))


def put_thin(ref, dy, value):
    tiles = value.reshape(FRAMES, J, GROUP, PAIR)
    tiles = jnp.concatenate([tiles[0], tiles[1]], axis=1)
    put(ref, (dy, slice(1, J + 1)), tiles)
    put(ref, (dy, 0), shifted_h(tiles[J - 1], 1))
    put(ref, (dy, J + 1), shifted_h(tiles[0], -1))


def rows_of(ref, dy, j0, wide, start, stop):
    if wide:
        return ref[dy, :, j0 : j0 + J, :, start:stop].reshape(-1, stop - start)
    return ref[dy, j0 : j0 + J, :, start:stop].reshape(-1, stop - start)


def silu(value):
    half = 0.5 * value
    return half + half * jnp.tanh(half)


def dot(a, b):
    return jnp.dot(a, b, preferred_element_type=jnp.float32)


def spatial(ref, wide, taps, weights, slot, odd):
    left_even, left_odd, turned, straight = [], [], [], []
    for dy in taps:
        at = dy + odd * (2 - 2 * dy)
        rows = functools.partial(rows_of, ref, dy, wide=wide)
        center = rows(1, start=0, stop=PAIR)
        left_even += [center, rows(0, start=PAIR, stop=PAIR + 128), rows(0, start=384, stop=PAIR)]
        left_odd += [center, rows(2, start=0, stop=256), rows(2, start=PAIR + 128, stop=LANES)]
        filler = weights[slot, at, 0:PAD, :]
        kernel = weights[slot, at]
        turned += [kernel[C:], filler, kernel[:C]]
        straight += [kernel, filler]
    even_sum = dot(jnp.concatenate(left_even, axis=1), jnp.concatenate(turned, axis=0))
    odd_sum = dot(jnp.concatenate(left_odd, axis=1), jnp.concatenate(straight, axis=0))
    return even_sum, odd_sum


def temporal(u0, u1, weights, slot):
    gap = jnp.zeros((u0.shape[0], PAD), u0.dtype)
    both = jnp.concatenate([u0, gap, u1, gap], axis=1)
    t0, t1, t2 = (weights[slot, tap] for tap in range(3))
    v0 = dot(both, jnp.concatenate([t1, t1[:PAD], t2, t2[:PAD]], axis=0))
    v1 = dot(both, jnp.concatenate([t0, t0[:PAD], t1, t1[:PAD]], axis=0))
    return v0, v1


def prepare_kernel(
    bounds_hbm,
    timesteps_hbm,
    gains_hbm,
    time_hbm,
    info,
    bias,
    gain_pairs,
    bounds,
    timesteps,
    gains,
    time_weight,
    sems,
):
    copies = [
        pltpu.make_async_copy(source, target, sems.at[n])
        for n, (source, target) in enumerate(
            (
                (bounds_hbm, bounds),
                (timesteps_hbm, timesteps),
                (gains_hbm, gains),
                (time_hbm, time_weight),
            )
        )
    ]
    for copy in copies:
        copy.start()
    for copy in copies:
        copy.wait()
    segment = lax.axis_index("segment")
    info[...] = jnp.full(info.shape, bounds[segment + 1] - bounds[segment], jnp.int32)
    gain_pairs[...] = jnp.concatenate([gains[...], gains[...]], axis=1)
    entries = time_weight.shape[1]
    half = entries // 2
    at = lax.broadcasted_iota(jnp.int32, (8, entries), 1)
    step = lax.broadcasted_iota(jnp.int32, (8, entries), 0)
    place = jnp.where(at < half, at, at - half).astype(jnp.float32)
    times = jnp.zeros((8, entries), jnp.int32)
    for s in range(STEPS):
        times = jnp.where(step == s, timesteps[s], times)
    angle = times.astype(jnp.float32) * jnp.exp(-math.log(10000.0) * place / half)
    emb = jnp.where(at < half, jnp.cos(angle), jnp.sin(angle))
    for slot in range(2):
        made = jnp.dot(
            emb,
            time_weight[slot],
            precision=lax.Precision.HIGHEST,
            preferred_element_type=jnp.float32,
        )
        for s in range(STEPS):
            bias[s, slot : slot + 1, :] = made[s : s + 1]


def place():
    row_group = lax.axis_index("rows")
    at_end = (row_group == 0) | (row_group == lax.axis_size("rows") - 1)
    return lax.rem(row_group, 2), at_end


def first_kernel(step, info, own, far, gains, sw, part, n_own, n_far, wide, thin):
    count = jnp.max(info[0:1, :])
    odd, at_end = place()
    mine, by_far = load(own), load(far)
    if step == 0:
        mine, by_far = flip_if(odd, mine), flip_if(1 - odd, by_far)
    by_far = jnp.where(at_end, 0.0, by_far)
    gain = gains[0:1, :].reshape(1, 1, PAIR)
    normed, far_normed = normalise(mine, gain), normalise(by_far, gain)
    n_own[...] = normed
    n_far[...] = far_normed

    @pl.when(count > 1)
    def _():
        put_wide(wide, 0, flip(far_normed), normed)
        even, odd_sum = spatial(wide, True, (0,), sw, 0, odd)
        part[0], part[1] = even, odd_sum

    @pl.when(count == 1)
    def _():
        put_thin(thin, 0, halves(far_normed, flip(normed)))
        put_thin(thin, 1, normed)
        even, odd_sum = spatial(thin, False, (0, 1), sw, 0, odd)
        part[0, : FIELD], part[1, : FIELD] = even, odd_sum


def second_kernel(
    step, info, own, far, core, part, n_own, n_far, bias, gains, sw, tw, out, wide, thin, acc, center
):
    count = jnp.max(info[0:1, :])
    odd, at_end = place()
    mine, by_core = load(own), load(core)
    if step == 0:
        mine, by_core = flip_if(odd, mine), flip_if(1 - odd, by_core)
    core_normed = normalise(by_core, gains[0:1, :].reshape(1, 1, PAIR))

    @pl.when(count == 1)
    def _():
        put_thin(thin, 2, halves(flip(n_own[...]), core_normed))
        even, odd_sum = spatial(thin, False, (2,), sw, 0, odd)
        acc[0], acc[1] = part[0, :FIELD] + even, part[1, :FIELD] + odd_sum
        center[...] = mine

    @pl.when(count > 1)
    def _():
        normed = n_own[...]
        turned = flip(normed)
        put_wide(wide, 1, halves(n_far[...], turned), halves(turned, core_normed))
        put_wide(wide, 2, normed, flip(core_normed))
        even, odd_sum = spatial(wide, True, (1, 2), sw, 0, odd)
        even = part[0] + even + bias[step, 0:1, :]
        odd_sum = part[1] + odd_sum + bias[step, 0:1, :]
        half = FIELD
        u_even, u_odd = silu(even).astype(jnp.bfloat16), silu(odd_sum).astype(jnp.bfloat16)
        u0 = jnp.concatenate([u_even[:half], u_odd[:half]], axis=0)
        u1 = jnp.concatenate([u_even[half:], u_odd[half:]], axis=0)
        v0, v1 = temporal(u0, u1, tw, 0)
        v_even = jnp.concatenate([v0[:half], v1[:half]], axis=0)
        v_odd = jnp.concatenate([v0[half:], v1[half:]], axis=0)
        change = jnp.concatenate([even + v_even, odd_sum + v_odd], axis=1)
        change = change.reshape(FRAMES * J, 2 * GROUP, PAIR)
        by_far = load(far)
        if step == 0:
            by_far = flip_if(1 - odd, by_far)
        back = flip(mine)
        first = halves(by_far, back) + change[:, :GROUP]
        second = halves(back, by_core) + change[:, GROUP:]
        first = first.astype(jnp.bfloat16).astype(jnp.float32)
        second = second.astype(jnp.bfloat16).astype(jnp.float32)
        row = lax.broadcasted_iota(jnp.int32, first.shape, 1)
        first = jnp.where((row < HB) & at_end, 0.0, first)
        center[...] = halves(flip(first), flip(second))
        gain = gains[1:2, :].reshape(1, 1, PAIR)
        n_first, n_second = normalise(first, gain), normalise(second, gain)
        put_thin(thin, 0, n_first)
        put_thin(thin, 1, halves(flip(n_first), flip(n_second)))
        put_thin(thin, 2, n_second)
        even, odd_sum = spatial(thin, False, (0, 1, 2), sw, 1, odd)
        acc[0], acc[1] = even, odd_sum

    last = count - 1
    shift = bias[step, pl.ds(last, 1), :]
    even = (acc[0] + shift).reshape(J, FRAMES, GROUP, C)
    odd_sum = (acc[1] + shift).reshape(J, FRAMES, GROUP, C)
    u0, u1 = (
        jnp.concatenate(
            [silu(even[:, f]).reshape(-1, C), silu(odd_sum[:, f]).reshape(-1, C)], axis=0
        )
        for f in range(FRAMES)
    )
    v0, v1 = temporal(u0.astype(jnp.bfloat16), u1.astype(jnp.bfloat16), tw, last)
    half = J * GROUP
    for f, v in enumerate((v0, v1)):
        a_even, a_odd = even[:, f].reshape(half, C), odd_sum[:, f].reshape(half, C)
        change = jnp.concatenate([a_even + v[:half], a_odd + v[half:]], axis=1)
        result = center[f * J : (f + 1) * J] + change.reshape(J, GROUP, PAIR)
        if step == STEPS - 1:
            result = flip_if(odd, result)
        out[f * half : (f + 1) * half, :] = result.reshape(half, PAIR).astype(jnp.bfloat16)


VMEM = pl.BlockSpec(memory_space=pltpu.VMEM)


def call(kernel, name, outs, scratch, flops):
    return pl.pallas_call(
        kernel,
        out_shape=tuple(jax.ShapeDtypeStruct(shape, dtype) for shape, dtype in outs),
        out_specs=(VMEM,) * len(outs),
        scratch_shapes=[pltpu.VMEM(shape, dtype) for shape, dtype in scratch],
        compiler_params=pltpu.CompilerParams(vmem_limit_bytes=24 * 1024 * 1024),
        cost_estimate=pl.CostEstimate(
            flops=flops, bytes_accessed=1_000_000, transcendentals=400_000
        ),
        name=name,
    )


def prepare(bounds, timesteps, gains, time_weight):
    hbm = pl.BlockSpec(memory_space=pltpu.HBM)
    return pl.pallas_call(
        prepare_kernel,
        out_shape=(
            jax.ShapeDtypeStruct((8, 128), jnp.int32),
            jax.ShapeDtypeStruct((STEPS, 2, C), jnp.float32),
            jax.ShapeDtypeStruct((2, PAIR), jnp.float32),
        ),
        in_specs=[hbm, hbm, hbm, hbm],
        out_specs=(VMEM,) * 3,
        scratch_shapes=[
            pltpu.SMEM(bounds.shape, jnp.int32),
            pltpu.SMEM(timesteps.shape, jnp.int32),
            pltpu.VMEM(gains.shape, jnp.float32),
            pltpu.VMEM(time_weight.shape, jnp.float32),
            pltpu.SemaphoreType.DMA((4,)),
        ],
        compiler_params=pltpu.CompilerParams(vmem_limit_bytes=20 * 1024 * 1024),
        cost_estimate=pl.CostEstimate(
            flops=8_000_000_000, bytes_accessed=1_000_000, transcendentals=10_000
        ),
        name="prepare",
    )(bounds, timesteps, gains, time_weight)


WIDE = ((3, FRAMES, J + 2, 2 * GROUP, LANES), jnp.bfloat16)
THIN = ((3, J + 2, FRAMES * GROUP, LANES), jnp.bfloat16)
ROWS_F32 = ((FRAMES * J, GROUP, PAIR), jnp.float32)


def apply_blocks(step, info, own, far, core, bias, gains, sw, tw):
    part, n_own, n_far = call(
        functools.partial(first_kernel, step),
        "own_and_far_rows",
        [((2, 2 * FIELD, C), jnp.float32), ROWS_F32, ROWS_F32],
        [WIDE, THIN],
        2_000_000_000,
    )(info, own, far, gains, sw)
    (field,) = call(
        functools.partial(second_kernel, step),
        "residual_blocks",
        [((FIELD, PAIR), jnp.bfloat16)],
        [WIDE, THIN, ((2, FIELD, C), jnp.float32), ROWS_F32],
        4_000_000_000,
    )(info, own, far, core, part, n_own, n_far, bias, gains, sw, tw)
    return field


def body(state, bounds, timesteps, gains, spatial_weight, temporal_weight, time_weight):
    groups = lax.axis_size("rows")
    segments = lax.axis_size("segment")
    info, bias, gain_pairs = prepare(bounds, timesteps, gains[0], time_weight[0])
    sw = spatial_weight.reshape(2, 3, 3 * C, C)
    tw = temporal_weight.reshape(2, 3, C, C)
    ahead = [(i, (i + 1) % segments) for i in range(segments)]
    on_chip = [(i, i ^ 1) for i in range(groups)]
    off_chip = [(i, i + 1) for i in range(1, groups - 1, 2)]
    off_chip = off_chip + [(j, i) for i, j in off_chip]
    off_chip_ahead = [
        (a * groups + i, b * groups + j) for a, b in ahead for i, j in off_chip
    ]

    field = state.reshape(FRAMES, ROWS, HB, J, PAIR).transpose(0, 3, 1, 2, 4).reshape(FIELD, PAIR)
    for step in range(STEPS):
        own = lax.ppermute(field, "segment", ahead)
        far = lax.ppermute(field, ("segment", "rows"), off_chip_ahead)
        if step == 0:
            own, info, bias, gain_pairs = lax.optimization_barrier((own, info, bias, gain_pairs))
        core = lax.ppermute(own, "rows", on_chip)
        field = apply_blocks(step, info, own, far, core, bias, gain_pairs, sw, tw)
    field = field.reshape(FRAMES, J, ROWS, HB, PAIR).transpose(0, 2, 3, 1, 4)
    return field.reshape(1, FRAMES, ROWS, W * C)


def solution(mesh):
    placed = (
        P("segment", None, "rows", None),
        P(),
        P(),
        P("segment", None, None),
        P("segment", None, None, None, None, None),
        P("segment", None, None, None, None),
        P("segment", None, None, None),
    )
    return jax.shard_map(
        body,
        mesh=mesh,
        in_specs=placed,
        out_specs=P("segment", None, "rows", None),
        check_vma=False,
    )
```

```python
import functools
import math

import jax
import jax.numpy as jnp
from jax import lax
from jax.experimental import pallas as pl
from jax.experimental.pallas import tpu as pltpu
from jax.sharding import PartitionSpec as P

C = 320
W = 72
STEPS = 2
FRAMES = 2
ROWS = 2

HB = 4
J = W // 2 // HB
PAIR = 2 * C
GROUP = ROWS * HB
FIELD = FRAMES * J * GROUP
PAD = 64
LANES = PAIR + 256
EPS = 1e-06


def low_lanes(shape):
    return lax.broadcasted_iota(jnp.int32, shape, len(shape) - 1) < PAD


def normalise(value, gain):
    low = low_lanes(value[..., 256:384].shape)
    square = value * value
    middle = square[..., 256:384]
    first = square[..., 0:128] + square[..., 128:256] + jnp.where(low, middle, 0.0)
    second = square[..., 384:512] + square[..., 512:640] + jnp.where(low, 0.0, middle)
    scale = lax.rsqrt(jnp.sum(first, axis=-1, keepdims=True) / C + EPS)
    other = lax.rsqrt(jnp.sum(second, axis=-1, keepdims=True) / C + EPS)
    scaled = jnp.concatenate(
        [
            value[..., 0:256] * scale,
            value[..., 256:384] * jnp.where(low, scale, other),
            value[..., 384:640] * other,
        ],
        axis=-1,
    )
    return scaled * gain


def load(ref):
    return ref[...].astype(jnp.float32).reshape(FRAMES * J, GROUP, PAIR)


def flip(value):
    return pltpu.roll(value, HB, 1)


def flip_if(odd, value):
    return pltpu.roll(value, HB * odd, 1)


def halves(first, second):
    row = lax.broadcasted_iota(jnp.int32, first.shape, 1)
    return jnp.where(row < HB, first, second)


def shifted_h(value, by):
    rows = value.shape[0]
    moved = pltpu.roll(value, by % rows, 0)
    h = lax.rem(lax.broadcasted_iota(jnp.int32, value.shape, 0), HB)
    edge = 0 if by == 1 else HB - 1
    return jnp.where(h == edge, 0.0, moved)


def put(ref, at, value):
    middle = value[..., 256:384]
    low = low_lanes(middle.shape)
    ref[at + (slice(None), slice(0, PAIR))] = value.astype(jnp.bfloat16)
    ref[at + (slice(None), slice(PAIR, PAIR + 128))] = jnp.where(low, 0.0, middle).astype(
        jnp.bfloat16
    )
    ref[at + (slice(None), slice(PAIR + 128, LANES))] = jnp.where(low, middle, 0.0).astype(
        jnp.bfloat16
    )


def put_wide(ref, dy, first, second):
    tiles = jnp.concatenate([first, second], axis=1).reshape(FRAMES, J, 2 * GROUP, PAIR)
    put(ref, (dy, slice(None), slice(1, J + 1)), tiles)
    for f in range(FRAMES):
        put(ref, (dy, f, 0), shifted_h(tiles[f, J - 1], 1))
        put(ref, (dy, f, J + 1), shifted_h(tiles[f, 0], -1))


def put_thin(ref, dy, value):
    tiles = value.reshape(FRAMES, J, GROUP, PAIR)
    tiles = jnp.concatenate([tiles[0], tiles[1]], axis=1)
    put(ref, (dy, slice(1, J + 1)), tiles)
    put(ref, (dy, 0), shifted_h(tiles[J - 1], 1))
    put(ref, (dy, J + 1), shifted_h(tiles[0], -1))


def rows_of(ref, dy, j0, wide, start, stop):
    if wide:
        return ref[dy, :, j0 : j0 + J, :, start:stop].reshape(-1, stop - start)
    return ref[dy, j0 : j0 + J, :, start:stop].reshape(-1, stop - start)


def silu(value):
    half = 0.5 * value
    return half + half * jnp.tanh(half)


def dot(a, b):
    return jnp.dot(a, b, preferred_element_type=jnp.float32)


def spatial(ref, wide, taps, weights, slot, odd):
    left_even, left_odd, turned, straight = [], [], [], []
    for dy in taps:
        at = dy + odd * (2 - 2 * dy)
        rows = functools.partial(rows_of, ref, dy, wide=wide)
        center = rows(1, start=0, stop=PAIR)
        left_even += [center, rows(0, start=PAIR, stop=PAIR + 128), rows(0, start=384, stop=PAIR)]
        left_odd += [center, rows(2, start=0, stop=256), rows(2, start=PAIR + 128, stop=LANES)]
        filler = weights[slot, at, 0:PAD, :]
        kernel = weights[slot, at]
        turned += [kernel[C:], filler, kernel[:C]]
        straight += [kernel, filler]
    even_sum = dot(jnp.concatenate(left_even, axis=1), jnp.concatenate(turned, axis=0))
    odd_sum = dot(jnp.concatenate(left_odd, axis=1), jnp.concatenate(straight, axis=0))
    return even_sum, odd_sum


def temporal(u0, u1, weights, slot):
    gap = jnp.zeros((u0.shape[0], PAD), u0.dtype)
    both = jnp.concatenate([u0, gap, u1, gap], axis=1)
    t0, t1, t2 = (weights[slot, tap] for tap in range(3))
    v0 = dot(both, jnp.concatenate([t1, t1[:PAD], t2, t2[:PAD]], axis=0))
    v1 = dot(both, jnp.concatenate([t0, t0[:PAD], t1, t1[:PAD]], axis=0))
    return v0, v1


def prepare_kernel(
    bounds_hbm,
    timesteps_hbm,
    gains_hbm,
    time_hbm,
    info,
    bias,
    gain_pairs,
    bounds,
    timesteps,
    gains,
    time_weight,
    sems,
):
    copies = [
        pltpu.make_async_copy(source, target, sems.at[n])
        for n, (source, target) in enumerate(
            (
                (bounds_hbm, bounds),
                (timesteps_hbm, timesteps),
                (gains_hbm, gains),
                (time_hbm, time_weight),
            )
        )
    ]
    for copy in copies:
        copy.start()
    for copy in copies:
        copy.wait()
    segment = lax.axis_index("segment")
    info[...] = jnp.full(info.shape, bounds[segment + 1] - bounds[segment], jnp.int32)
    gain_pairs[...] = jnp.concatenate([gains[...], gains[...]], axis=1)
    entries = time_weight.shape[1]
    half = entries // 2
    at = lax.broadcasted_iota(jnp.int32, (8, entries), 1)
    step = lax.broadcasted_iota(jnp.int32, (8, entries), 0)
    place = jnp.where(at < half, at, at - half).astype(jnp.float32)
    times = jnp.zeros((8, entries), jnp.int32)
    for s in range(STEPS):
        times = jnp.where(step == s, timesteps[s], times)
    angle = times.astype(jnp.float32) * jnp.exp(-math.log(10000.0) * place / half)
    emb = jnp.where(at < half, jnp.cos(angle), jnp.sin(angle))
    for slot in range(2):
        made = jnp.dot(
            emb,
            time_weight[slot],
            precision=lax.Precision.HIGHEST,
            preferred_element_type=jnp.float32,
        )
        for s in range(STEPS):
            bias[s, slot : slot + 1, :] = made[s : s + 1]


def place():
    row_group = lax.axis_index("rows")
    at_end = (row_group == 0) | (row_group == lax.axis_size("rows") - 1)
    return lax.rem(row_group, 2), at_end


def first_kernel(step, info, own, far, gains, sw, part, n_own, n_far, wide, thin):
    count = jnp.max(info[0:1, :])
    odd, at_end = place()
    mine, by_far = load(own), load(far)
    if step == 0:
        mine, by_far = flip_if(odd, mine), flip_if(1 - odd, by_far)
    by_far = jnp.where(at_end, 0.0, by_far)
    gain = gains[0:1, :].reshape(1, 1, PAIR)
    normed, far_normed = normalise(mine, gain), normalise(by_far, gain)
    n_own[...] = normed
    n_far[...] = far_normed

    @pl.when(count > 1)
    def _():
        put_wide(wide, 0, flip(far_normed), normed)
        even, odd_sum = spatial(wide, True, (0,), sw, 0, odd)
        part[0], part[1] = even, odd_sum

    @pl.when(count == 1)
    def _():
        put_thin(thin, 0, halves(far_normed, flip(normed)))
        put_thin(thin, 1, normed)
        even, odd_sum = spatial(thin, False, (0, 1), sw, 0, odd)
        part[0, : FIELD], part[1, : FIELD] = even, odd_sum


def second_kernel(
    step, info, own, far, core, part, n_own, n_far, bias, gains, sw, tw, out, wide, thin, acc, center
):
    count = jnp.max(info[0:1, :])
    odd, at_end = place()
    mine, by_core = load(own), load(core)
    if step == 0:
        mine, by_core = flip_if(odd, mine), flip_if(1 - odd, by_core)
    core_normed = normalise(by_core, gains[0:1, :].reshape(1, 1, PAIR))

    @pl.when(count == 1)
    def _():
        put_thin(thin, 2, halves(flip(n_own[...]), core_normed))
        even, odd_sum = spatial(thin, False, (2,), sw, 0, odd)
        acc[0], acc[1] = part[0, :FIELD] + even, part[1, :FIELD] + odd_sum
        center[...] = mine

    @pl.when(count > 1)
    def _():
        normed = n_own[...]
        turned = flip(normed)
        put_wide(wide, 1, halves(n_far[...], turned), halves(turned, core_normed))
        put_wide(wide, 2, normed, flip(core_normed))
        even, odd_sum = spatial(wide, True, (1, 2), sw, 0, odd)
        even = part[0] + even + bias[step, 0:1, :]
        odd_sum = part[1] + odd_sum + bias[step, 0:1, :]
        half = FIELD
        u_even, u_odd = silu(even).astype(jnp.bfloat16), silu(odd_sum).astype(jnp.bfloat16)
        u0 = jnp.concatenate([u_even[:half], u_odd[:half]], axis=0)
        u1 = jnp.concatenate([u_even[half:], u_odd[half:]], axis=0)
        v0, v1 = temporal(u0, u1, tw, 0)
        v_even = jnp.concatenate([v0[:half], v1[:half]], axis=0)
        v_odd = jnp.concatenate([v0[half:], v1[half:]], axis=0)
        change = jnp.concatenate([even + v_even, odd_sum + v_odd], axis=1)
        change = change.reshape(FRAMES * J, 2 * GROUP, PAIR)
        by_far = load(far)
        if step == 0:
            by_far = flip_if(1 - odd, by_far)
        back = flip(mine)
        first = halves(by_far, back) + change[:, :GROUP]
        second = halves(back, by_core) + change[:, GROUP:]
        first = first.astype(jnp.bfloat16).astype(jnp.float32)
        second = second.astype(jnp.bfloat16).astype(jnp.float32)
        row = lax.broadcasted_iota(jnp.int32, first.shape, 1)
        first = jnp.where((row < HB) & at_end, 0.0, first)
        center[...] = halves(flip(first), flip(second))
        gain = gains[1:2, :].reshape(1, 1, PAIR)
        n_first, n_second = normalise(first, gain), normalise(second, gain)
        put_thin(thin, 0, n_first)
        put_thin(thin, 1, halves(flip(n_first), flip(n_second)))
        put_thin(thin, 2, n_second)
        even, odd_sum = spatial(thin, False, (0, 1, 2), sw, 1, odd)
        acc[0], acc[1] = even, odd_sum

    last = count - 1
    shift = bias[step, pl.ds(last, 1), :]
    even = (acc[0] + shift).reshape(J, FRAMES, GROUP, C)
    odd_sum = (acc[1] + shift).reshape(J, FRAMES, GROUP, C)
    u0, u1 = (
        jnp.concatenate(
            [silu(even[:, f]).reshape(-1, C), silu(odd_sum[:, f]).reshape(-1, C)], axis=0
        )
        for f in range(FRAMES)
    )
    v0, v1 = temporal(u0.astype(jnp.bfloat16), u1.astype(jnp.bfloat16), tw, last)
    half = J * GROUP
    for f, v in enumerate((v0, v1)):
        a_even, a_odd = even[:, f].reshape(half, C), odd_sum[:, f].reshape(half, C)
        change = jnp.concatenate([a_even + v[:half], a_odd + v[half:]], axis=1)
        result = center[f * J : (f + 1) * J] + change.reshape(J, GROUP, PAIR)
        if step == STEPS - 1:
            result = flip_if(odd, result)
        out[f * half : (f + 1) * half, :] = result.reshape(half, PAIR).astype(jnp.bfloat16)


VMEM = pl.BlockSpec(memory_space=pltpu.VMEM)


def call(kernel, name, outs, scratch, flops):
    return pl.pallas_call(
        kernel,
        out_shape=tuple(jax.ShapeDtypeStruct(shape, dtype) for shape, dtype in outs),
        out_specs=(VMEM,) * len(outs),
        scratch_shapes=[pltpu.VMEM(shape, dtype) for shape, dtype in scratch],
        compiler_params=pltpu.CompilerParams(vmem_limit_bytes=24 * 1024 * 1024),
        cost_estimate=pl.CostEstimate(
            flops=flops, bytes_accessed=flops // 4_000, transcendentals=0
        ),
        name=name,
    )


def prepare(bounds, timesteps, gains, time_weight):
    hbm = pl.BlockSpec(memory_space=pltpu.HBM)
    return pl.pallas_call(
        prepare_kernel,
        out_shape=(
            jax.ShapeDtypeStruct((8, 128), jnp.int32),
            jax.ShapeDtypeStruct((STEPS, 2, C), jnp.float32),
            jax.ShapeDtypeStruct((2, PAIR), jnp.float32),
        ),
        in_specs=[hbm, hbm, hbm, hbm],
        out_specs=(VMEM,) * 3,
        scratch_shapes=[
            pltpu.SMEM(bounds.shape, jnp.int32),
            pltpu.SMEM(timesteps.shape, jnp.int32),
            pltpu.VMEM(gains.shape, jnp.float32),
            pltpu.VMEM(time_weight.shape, jnp.float32),
            pltpu.SemaphoreType.DMA((4,)),
        ],
        compiler_params=pltpu.CompilerParams(vmem_limit_bytes=20 * 1024 * 1024),
        cost_estimate=pl.CostEstimate(
            flops=8_000_000_000, bytes_accessed=1_000_000, transcendentals=10_000
        ),
        name="prepare",
    )(bounds, timesteps, gains, time_weight)


WIDE = ((3, FRAMES, J + 2, 2 * GROUP, LANES), jnp.bfloat16)
THIN = ((3, J + 2, FRAMES * GROUP, LANES), jnp.bfloat16)
ROWS_F32 = ((FRAMES * J, GROUP, PAIR), jnp.float32)


def apply_blocks(step, info, own, far, core, bias, gains, sw, tw):
    part, n_own, n_far = call(
        functools.partial(first_kernel, step),
        "own_and_far_rows",
        [((2, 2 * FIELD, C), jnp.float32), ROWS_F32, ROWS_F32],
        [WIDE, THIN],
        1_000_000,
    )(info, own, far, gains, sw)
    (field,) = call(
        functools.partial(second_kernel, step),
        "residual_blocks",
        [((FIELD, PAIR), jnp.bfloat16)],
        [WIDE, THIN, ((2, FIELD, C), jnp.float32), ROWS_F32],
        4_000_000_000,
    )(info, own, far, core, part, n_own, n_far, bias, gains, sw, tw)
    return field


def body(state, bounds, timesteps, gains, spatial_weight, temporal_weight, time_weight):
    groups = lax.axis_size("rows")
    segments = lax.axis_size("segment")
    info, bias, gain_pairs = prepare(bounds, timesteps, gains[0], time_weight[0])
    sw = spatial_weight.reshape(2, 3, 3 * C, C)
    tw = temporal_weight.reshape(2, 3, C, C)
    ahead = [(i, (i + 1) % segments) for i in range(segments)]
    on_chip = [(i, i ^ 1) for i in range(groups)]
    off_chip = [(i, i + 1) for i in range(1, groups - 1, 2)]
    off_chip = off_chip + [(j, i) for i, j in off_chip] + [(0, 0), (groups - 1, groups - 1)]
    off_chip_ahead = [
        (a * groups + i, b * groups + j) for a, b in ahead for i, j in off_chip
    ]

    field = state.reshape(FRAMES, ROWS, HB, J, PAIR).transpose(0, 3, 1, 2, 4).reshape(FIELD, PAIR)
    for step in range(STEPS):
        far = lax.ppermute(field, ("segment", "rows"), off_chip_ahead)
        own = lax.ppermute(field, "segment", ahead)
        if step == 0:
            far, own, info, bias, gain_pairs = lax.optimization_barrier(
                (far, own, info, bias, gain_pairs)
            )
        core = lax.ppermute(own, "rows", on_chip)
        field = apply_blocks(step, info, own, far, core, bias, gain_pairs, sw, tw)
    field = field.reshape(FRAMES, J, ROWS, HB, PAIR).transpose(0, 2, 3, 1, 4)
    return field.reshape(1, FRAMES, ROWS, W * C)


def solution(mesh):
    placed = (
        P("segment", None, "rows", None),
        P(),
        P(),
        P("segment", None, None),
        P("segment", None, None, None, None, None),
        P("segment", None, None, None, None),
        P("segment", None, None, None),
    )
    return jax.shard_map(
        body,
        mesh=mesh,
        in_specs=placed,
        out_specs=P("segment", None, "rows", None),
        check_vma=False,
    )
```

```python
import functools
import math

import jax
import jax.numpy as jnp
from jax import lax
from jax.experimental import pallas as pl
from jax.experimental.pallas import tpu as pltpu
from jax.sharding import PartitionSpec as P

C = 320
W = 72
STEPS = 2
FRAMES = 2
ROWS = 2

HB = 4
J = W // 2 // HB
PAIR = 2 * C
GROUP = ROWS * HB
FIELD = FRAMES * J * GROUP
PAD = 64
LANES = PAIR + 256
SECOND = C + PAD
EPS = 1e-06


def low_lanes(shape):
    return lax.broadcasted_iota(jnp.int32, shape, len(shape) - 1) < PAD


def normalise(value, gain):
    low = low_lanes(value[..., 256:384].shape)
    square = value * value
    middle = square[..., 256:384]
    first = square[..., 0:128] + square[..., 128:256] + jnp.where(low, middle, 0.0)
    second = square[..., 384:512] + square[..., 512:640] + jnp.where(low, 0.0, middle)
    scale = lax.rsqrt(jnp.sum(first, axis=-1, keepdims=True) / C + EPS)
    other = lax.rsqrt(jnp.sum(second, axis=-1, keepdims=True) / C + EPS)
    scaled = jnp.concatenate(
        [
            value[..., 0:256] * scale,
            value[..., 256:384] * jnp.where(low, scale, other),
            value[..., 384:640] * other,
        ],
        axis=-1,
    )
    return scaled * gain


def load(ref):
    return ref[...].astype(jnp.float32).reshape(FRAMES * J, GROUP, PAIR)


def flip(value):
    return pltpu.roll(value, HB, 1)


def flip_if(odd, value):
    return pltpu.roll(value, HB * odd, 1)


def halves(first, second):
    row = lax.broadcasted_iota(jnp.int32, first.shape, 1)
    return jnp.where(row < HB, first, second)


def shifted_h(value, by):
    rows = value.shape[0]
    moved = pltpu.roll(value, by % rows, 0)
    h = lax.rem(lax.broadcasted_iota(jnp.int32, value.shape, 0), HB)
    edge = 0 if by == 1 else HB - 1
    return jnp.where(h == edge, 0.0, moved)


def put(ref, at, value):
    middle = value[..., 256:384]
    low = low_lanes(middle.shape)
    ref[at + (slice(None), slice(0, PAIR))] = value.astype(jnp.bfloat16)
    ref[at + (slice(None), slice(PAIR, PAIR + 128))] = jnp.where(low, 0.0, middle).astype(
        jnp.bfloat16
    )
    ref[at + (slice(None), slice(PAIR + 128, LANES))] = jnp.where(low, middle, 0.0).astype(
        jnp.bfloat16
    )


def put_wide(ref, dy, first, second):
    tiles = jnp.concatenate([first, second], axis=1).reshape(FRAMES, J, 2 * GROUP, PAIR)
    put(ref, (dy, slice(None), slice(1, J + 1)), tiles)
    for f in range(FRAMES):
        put(ref, (dy, f, 0), shifted_h(tiles[f, J - 1], 1))
        put(ref, (dy, f, J + 1), shifted_h(tiles[f, 0], -1))


def put_thin(ref, dy, value):
    tiles = value.reshape(FRAMES, J, GROUP, PAIR)
    tiles = jnp.concatenate([tiles[0], tiles[1]], axis=1)
    put(ref, (dy, slice(1, J + 1)), tiles)
    put(ref, (dy, 0), shifted_h(tiles[J - 1], 1))
    put(ref, (dy, J + 1), shifted_h(tiles[0], -1))


def rows_of(ref, dy, j0, wide, start, stop):
    if wide:
        return ref[dy, :, j0 : j0 + J, :, start:stop].reshape(-1, stop - start)
    return ref[dy, j0 : j0 + J, :, start:stop].reshape(-1, stop - start)


def silu(value):
    half = 0.5 * value
    return half + half * jnp.tanh(half)


def dot(a, b):
    return jnp.dot(a, b, preferred_element_type=jnp.float32)


def spatial(ref, wide, taps, weights, pairs, slot, odd):
    center, before, after, joint, left, right = [], [], [], [], [], []
    for dy in taps:
        at = dy + odd * (2 - 2 * dy)
        rows = functools.partial(rows_of, ref, dy, wide=wide)
        center.append(rows(1, start=0, stop=PAIR))
        before += [rows(0, start=PAIR, stop=PAIR + 128), rows(0, start=384, stop=PAIR)]
        after += [rows(2, start=0, stop=256), rows(2, start=PAIR + 128, stop=LANES)]
        filler = weights[slot, at, 0:PAD, :]
        joint.append(pairs[slot, at])
        left += [filler, weights[slot, at, 0:C, :]]
        right += [weights[slot, at, 2 * C :, :], filler]
    both = dot(jnp.concatenate(center, axis=1), jnp.concatenate(joint, axis=0))
    even_sum = dot(jnp.concatenate(before, axis=1), jnp.concatenate(left, axis=0))
    odd_sum = dot(jnp.concatenate(after, axis=1), jnp.concatenate(right, axis=0))
    return both[:, :C] + even_sum, both[:, SECOND:] + odd_sum


def temporal(u0, u1, pairs, slot):
    gap = jnp.zeros((u0.shape[0], PAD), u0.dtype)
    both = dot(jnp.concatenate([u0, gap, u1, gap], axis=1), pairs[slot])
    return both[:, :C], both[:, SECOND:]


def frequency_kernel(out):
    half = out.shape[1] // 2
    at = lax.broadcasted_iota(jnp.int32, out.shape, 1)
    index = jnp.where(at < half, at, at - half).astype(jnp.float32)
    out[...] = jnp.exp(-math.log(10000.0) * index / half)


def prepare_kernel(
    bounds_hbm,
    timesteps_hbm,
    gains_hbm,
    time_hbm,
    frequency,
    spatial_weight,
    temporal_weight,
    info,
    bias,
    gain_pairs,
    spatial_pairs,
    temporal_pairs,
    bounds,
    timesteps,
    gains,
    time_weight,
    sems,
):
    copies = [
        pltpu.make_async_copy(source, target, sems.at[n])
        for n, (source, target) in enumerate(
            (
                (bounds_hbm, bounds),
                (timesteps_hbm, timesteps),
                (gains_hbm, gains),
                (time_hbm, time_weight),
            )
        )
    ]
    for copy in copies:
        copy.start()
    for slot in range(2):
        for dy in range(3):
            kernel = spatial_weight.at[slot, dy]
            spatial_pairs[slot, dy, :, 0:C] = kernel[C : 3 * C, :]
            spatial_pairs[slot, dy, :, SECOND : SECOND + C] = kernel[0 : 2 * C, :]
        for frame, lanes in enumerate((slice(0, C), slice(SECOND, SECOND + C))):
            for other in range(2):
                tap = temporal_weight.at[slot, 1 - frame + other]
                temporal_pairs[slot, other * SECOND : other * SECOND + C, lanes] = tap[...]
                temporal_pairs[slot, other * SECOND + C : (other + 1) * SECOND, lanes] = tap[0:PAD, :]
    for copy in copies:
        copy.wait()
    segment = lax.axis_index("segment")
    info[...] = jnp.full(info.shape, bounds[segment + 1] - bounds[segment], jnp.int32)
    gain_pairs[...] = jnp.concatenate([gains[...], gains[...]], axis=1)
    entries = time_weight.shape[1]
    half = entries // 2
    at = lax.broadcasted_iota(jnp.int32, (8, entries), 1)
    step = lax.broadcasted_iota(jnp.int32, (8, entries), 0)
    times = jnp.zeros((8, entries), jnp.int32)
    for s in range(STEPS):
        times = jnp.where(step == s, timesteps[s], times)
    angle = times.astype(jnp.float32) * frequency[...]
    emb = jnp.where(at < half, jnp.cos(angle), jnp.sin(angle))
    for slot in range(2):
        made = jnp.dot(
            emb,
            time_weight[slot],
            precision=lax.Precision.HIGHEST,
            preferred_element_type=jnp.float32,
        )
        for s in range(STEPS):
            bias[s, slot : slot + 1, :] = made[s : s + 1]


def place():
    row_group = lax.axis_index("rows")
    at_end = (row_group == 0) | (row_group == lax.axis_size("rows") - 1)
    return lax.rem(row_group, 2), at_end


def first_kernel(step, info, own, far, gains, sw, sp, part, n_own, n_far, wide, thin):
    count = jnp.max(info[0:1, :])
    odd, at_end = place()
    mine, by_far = load(own), load(far)
    if step == 0:
        mine, by_far = flip_if(odd, mine), flip_if(1 - odd, by_far)
    by_far = jnp.where(at_end, 0.0, by_far)
    gain = gains[0:1, :].reshape(1, 1, PAIR)
    normed, far_normed = normalise(mine, gain), normalise(by_far, gain)
    n_own[...] = normed
    n_far[...] = far_normed

    @pl.when(count > 1)
    def _():
        put_wide(wide, 0, flip(far_normed), normed)
        even, odd_sum = spatial(wide, True, (0,), sw, sp, 0, odd)
        part[0], part[1] = even, odd_sum

    @pl.when(count == 1)
    def _():
        put_thin(thin, 0, halves(far_normed, flip(normed)))
        put_thin(thin, 1, normed)
        even, odd_sum = spatial(thin, False, (0, 1), sw, sp, 0, odd)
        part[0, : FIELD], part[1, : FIELD] = even, odd_sum


def second_kernel(
    step, info, own, far, core, part, n_own, n_far, bias, gains, sw, sp, tp, out, wide, thin, acc, center
):
    count = jnp.max(info[0:1, :])
    odd, at_end = place()
    mine, by_core = load(own), load(core)
    if step == 0:
        mine, by_core = flip_if(odd, mine), flip_if(1 - odd, by_core)
    core_normed = normalise(by_core, gains[0:1, :].reshape(1, 1, PAIR))

    @pl.when(count == 1)
    def _():
        put_thin(thin, 2, halves(flip(n_own[...]), core_normed))
        even, odd_sum = spatial(thin, False, (2,), sw, sp, 0, odd)
        acc[0], acc[1] = part[0, :FIELD] + even, part[1, :FIELD] + odd_sum
        center[...] = mine

    @pl.when(count > 1)
    def _():
        normed = n_own[...]
        turned = flip(normed)
        put_wide(wide, 1, halves(n_far[...], turned), halves(turned, core_normed))
        put_wide(wide, 2, normed, flip(core_normed))
        even, odd_sum = spatial(wide, True, (1, 2), sw, sp, 0, odd)
        even = part[0] + even + bias[step, 0:1, :]
        odd_sum = part[1] + odd_sum + bias[step, 0:1, :]
        half = FIELD
        u_even, u_odd = silu(even).astype(jnp.bfloat16), silu(odd_sum).astype(jnp.bfloat16)
        u0 = jnp.concatenate([u_even[:half], u_odd[:half]], axis=0)
        u1 = jnp.concatenate([u_even[half:], u_odd[half:]], axis=0)
        v0, v1 = temporal(u0, u1, tp, 0)
        v_even = jnp.concatenate([v0[:half], v1[:half]], axis=0)
        v_odd = jnp.concatenate([v0[half:], v1[half:]], axis=0)
        change = jnp.concatenate([even + v_even, odd_sum + v_odd], axis=1)
        change = change.reshape(FRAMES * J, 2 * GROUP, PAIR)
        by_far = load(far)
        if step == 0:
            by_far = flip_if(1 - odd, by_far)
        back = flip(mine)
        first = halves(by_far, back) + change[:, :GROUP]
        second = halves(back, by_core) + change[:, GROUP:]
        first = first.astype(jnp.bfloat16).astype(jnp.float32)
        second = second.astype(jnp.bfloat16).astype(jnp.float32)
        row = lax.broadcasted_iota(jnp.int32, first.shape, 1)
        first = jnp.where((row < HB) & at_end, 0.0, first)
        center[...] = halves(flip(first), flip(second))
        gain = gains[1:2, :].reshape(1, 1, PAIR)
        n_first, n_second = normalise(first, gain), normalise(second, gain)
        put_thin(thin, 0, n_first)
        put_thin(thin, 1, halves(flip(n_first), flip(n_second)))
        put_thin(thin, 2, n_second)
        even, odd_sum = spatial(thin, False, (0, 1, 2), sw, sp, 1, odd)
        acc[0], acc[1] = even, odd_sum

    last = count - 1
    shift = bias[step, pl.ds(last, 1), :]
    even = (acc[0] + shift).reshape(J, FRAMES, GROUP, C)
    odd_sum = (acc[1] + shift).reshape(J, FRAMES, GROUP, C)
    u0, u1 = (
        jnp.concatenate(
            [silu(even[:, f]).reshape(-1, C), silu(odd_sum[:, f]).reshape(-1, C)], axis=0
        )
        for f in range(FRAMES)
    )
    v0, v1 = temporal(u0.astype(jnp.bfloat16), u1.astype(jnp.bfloat16), tp, last)
    half = J * GROUP
    for f, v in enumerate((v0, v1)):
        a_even, a_odd = even[:, f].reshape(half, C), odd_sum[:, f].reshape(half, C)
        change = jnp.concatenate([a_even + v[:half], a_odd + v[half:]], axis=1)
        result = center[f * J : (f + 1) * J] + change.reshape(J, GROUP, PAIR)
        if step == STEPS - 1:
            result = flip_if(odd, result)
        out[f * half : (f + 1) * half, :] = result.reshape(half, PAIR).astype(jnp.bfloat16)


VMEM = pl.BlockSpec(memory_space=pltpu.VMEM)


def call(kernel, name, outs, scratch, flops):
    return pl.pallas_call(
        kernel,
        out_shape=tuple(jax.ShapeDtypeStruct(shape, dtype) for shape, dtype in outs),
        out_specs=(VMEM,) * len(outs),
        scratch_shapes=[pltpu.VMEM(shape, dtype) for shape, dtype in scratch],
        compiler_params=pltpu.CompilerParams(vmem_limit_bytes=24 * 1024 * 1024),
        cost_estimate=pl.CostEstimate(
            flops=flops, bytes_accessed=flops // 4_000, transcendentals=0
        ),
        name=name,
    )


def prepare(bounds, timesteps, gains, time_weight, spatial_weight, temporal_weight):
    hbm = pl.BlockSpec(memory_space=pltpu.HBM)
    (frequency,) = call(
        frequency_kernel, "frequency", [((8, time_weight.shape[1]), jnp.float32)], [], 4_000_000_000
    )()
    return pl.pallas_call(
        prepare_kernel,
        out_shape=(
            jax.ShapeDtypeStruct((8, 128), jnp.int32),
            jax.ShapeDtypeStruct((STEPS, 2, C), jnp.float32),
            jax.ShapeDtypeStruct((2, PAIR), jnp.float32),
            jax.ShapeDtypeStruct((2, 3, 2 * C, SECOND + C), jnp.bfloat16),
            jax.ShapeDtypeStruct((2, 2 * SECOND, SECOND + C), jnp.bfloat16),
        ),
        in_specs=[hbm, hbm, hbm, hbm, VMEM, VMEM, VMEM],
        out_specs=(VMEM,) * 5,
        scratch_shapes=[
            pltpu.SMEM(bounds.shape, jnp.int32),
            pltpu.SMEM(timesteps.shape, jnp.int32),
            pltpu.VMEM(gains.shape, jnp.float32),
            pltpu.VMEM(time_weight.shape, jnp.float32),
            pltpu.SemaphoreType.DMA((4,)),
        ],
        compiler_params=pltpu.CompilerParams(vmem_limit_bytes=24 * 1024 * 1024),
        cost_estimate=pl.CostEstimate(
            flops=8_000_000_000, bytes_accessed=1_000_000, transcendentals=10_000
        ),
        name="prepare",
    )(bounds, timesteps, gains, time_weight, frequency, spatial_weight, temporal_weight)


WIDE = ((3, FRAMES, J + 2, 2 * GROUP, LANES), jnp.bfloat16)
THIN = ((3, J + 2, FRAMES * GROUP, LANES), jnp.bfloat16)
ROWS_F32 = ((FRAMES * J, GROUP, PAIR), jnp.float32)


def apply_blocks(step, info, own, far, core, bias, gains, sw, sp, tp):
    part, n_own, n_far = call(
        functools.partial(first_kernel, step),
        "own_and_far_rows",
        [((2, 2 * FIELD, C), jnp.float32), ROWS_F32, ROWS_F32],
        [WIDE, THIN],
        1_000_000,
    )(info, own, far, gains, sw, sp)
    (field,) = call(
        functools.partial(second_kernel, step),
        "residual_blocks",
        [((FIELD, PAIR), jnp.bfloat16)],
        [WIDE, THIN, ((2, FIELD, C), jnp.float32), ROWS_F32],
        4_000_000_000,
    )(info, own, far, core, part, n_own, n_far, bias, gains, sw, sp, tp)
    return field


def body(state, bounds, timesteps, gains, spatial_weight, temporal_weight, time_weight):
    groups = lax.axis_size("rows")
    segments = lax.axis_size("segment")
    sw = spatial_weight.reshape(2, 3, 3 * C, C)
    tw = temporal_weight.reshape(2, 3, C, C)
    made = prepare(bounds, timesteps, gains[0], time_weight[0], sw, tw)
    ahead = [(i, (i + 1) % segments) for i in range(segments)]
    on_chip = [(i, i ^ 1) for i in range(groups)]
    off_chip = [(i, i + 1) for i in range(1, groups - 1, 2)]
    off_chip = off_chip + [(j, i) for i, j in off_chip] + [(0, 0), (groups - 1, groups - 1)]
    off_chip_ahead = [
        (a * groups + i, b * groups + j) for a, b in ahead for i, j in off_chip
    ]

    field = state.reshape(FRAMES, ROWS, HB, J, PAIR).transpose(0, 3, 1, 2, 4).reshape(FIELD, PAIR)
    for step in range(STEPS):
        far = lax.ppermute(field, ("segment", "rows"), off_chip_ahead)
        own = lax.ppermute(field, "segment", ahead)
        if step == 0:
            far, own, made = lax.optimization_barrier((far, own, made))
            info, bias, gain_pairs, sp, tp = made
        core = lax.ppermute(own, "rows", on_chip)
        field = apply_blocks(step, info, own, far, core, bias, gain_pairs, sw, sp, tp)
    field = field.reshape(FRAMES, J, ROWS, HB, PAIR).transpose(0, 2, 3, 1, 4)
    return field.reshape(1, FRAMES, ROWS, W * C)


def solution(mesh):
    placed = (
        P("segment", None, "rows", None),
        P(),
        P(),
        P("segment", None, None),
        P("segment", None, None, None, None, None),
        P("segment", None, None, None, None),
        P("segment", None, None, None),
    )
    return jax.shard_map(
        body,
        mesh=mesh,
        in_specs=placed,
        out_specs=P("segment", None, "rows", None),
        check_vma=False,
    )
```

```python
import functools
import math

import jax
import jax.numpy as jnp
from jax import lax
from jax.experimental import pallas as pl
from jax.experimental.pallas import tpu as pltpu
from jax.sharding import PartitionSpec as P

C = 320
W = 72
STEPS = 2
FRAMES = 2
ROWS = 2

HB = 4
J = W // 2 // HB
PAIR = 2 * C
GROUP = ROWS * HB
FIELD = FRAMES * J * GROUP
PAD = 64
LANES = PAIR + 256
SECOND = C + PAD
EPS = 1e-06


def low_lanes(shape):
    return lax.broadcasted_iota(jnp.int32, shape, len(shape) - 1) < PAD


def normalise(value, gain):
    low = low_lanes(value[..., 256:384].shape)
    square = value * value
    middle = square[..., 256:384]
    first = square[..., 0:128] + square[..., 128:256] + jnp.where(low, middle, 0.0)
    second = square[..., 384:512] + square[..., 512:640] + jnp.where(low, 0.0, middle)
    scale = lax.rsqrt(jnp.sum(first, axis=-1, keepdims=True) / C + EPS)
    other = lax.rsqrt(jnp.sum(second, axis=-1, keepdims=True) / C + EPS)
    scaled = jnp.concatenate(
        [
            value[..., 0:256] * scale,
            value[..., 256:384] * jnp.where(low, scale, other),
            value[..., 384:640] * other,
        ],
        axis=-1,
    )
    return scaled * gain


def load(ref):
    return ref[...].astype(jnp.float32).reshape(FRAMES * J, GROUP, PAIR)


def flip(value):
    return pltpu.roll(value, HB, 1)


def flip_if(odd, value):
    return pltpu.roll(value, HB * odd, 1)


def halves(first, second):
    row = lax.broadcasted_iota(jnp.int32, first.shape, 1)
    return jnp.where(row < HB, first, second)


def shifted_h(value, by):
    rows = value.shape[0]
    moved = pltpu.roll(value, by % rows, 0)
    h = lax.rem(lax.broadcasted_iota(jnp.int32, value.shape, 0), HB)
    edge = 0 if by == 1 else HB - 1
    return jnp.where(h == edge, 0.0, moved)


def put(ref, at, value):
    middle = value[..., 256:384]
    low = low_lanes(middle.shape)
    ref[at + (slice(None), slice(0, PAIR))] = value.astype(jnp.bfloat16)
    ref[at + (slice(None), slice(PAIR, PAIR + 128))] = jnp.where(low, 0.0, middle).astype(
        jnp.bfloat16
    )
    ref[at + (slice(None), slice(PAIR + 128, LANES))] = jnp.where(low, middle, 0.0).astype(
        jnp.bfloat16
    )


def put_wide(ref, dy, first, second):
    tiles = jnp.concatenate([first, second], axis=1).reshape(FRAMES, J, 2 * GROUP, PAIR)
    put(ref, (dy, slice(None), slice(1, J + 1)), tiles)
    for f in range(FRAMES):
        put(ref, (dy, f, 0), shifted_h(tiles[f, J - 1], 1))
        put(ref, (dy, f, J + 1), shifted_h(tiles[f, 0], -1))


def put_thin(ref, dy, value):
    tiles = value.reshape(FRAMES, J, GROUP, PAIR)
    tiles = jnp.concatenate([tiles[0], tiles[1]], axis=1)
    put(ref, (dy, slice(1, J + 1)), tiles)
    put(ref, (dy, 0), shifted_h(tiles[J - 1], 1))
    put(ref, (dy, J + 1), shifted_h(tiles[0], -1))


def rows_of(ref, dy, j0, wide, start, stop):
    if wide:
        return ref[dy, :, j0 : j0 + J, :, start:stop].reshape(-1, stop - start)
    return ref[dy, j0 : j0 + J, :, start:stop].reshape(-1, stop - start)


def silu(value):
    half = 0.5 * value
    return half + half * jnp.tanh(half)


def dot(a, b):
    return jnp.dot(a, b, preferred_element_type=jnp.float32)


def spatial(ref, wide, taps, weights, pairs, slot, odd):
    center, before, after, joint, left, right = [], [], [], [], [], []
    for dy in taps:
        at = dy + odd * (2 - 2 * dy)
        rows = functools.partial(rows_of, ref, dy, wide=wide)
        center.append(rows(1, start=0, stop=PAIR))
        before += [rows(0, start=PAIR, stop=PAIR + 128), rows(0, start=384, stop=PAIR)]
        after += [rows(2, start=0, stop=256), rows(2, start=PAIR + 128, stop=LANES)]
        filler = weights[slot, at, 0:PAD, :]
        joint.append(pairs[slot, at])
        left += [filler, weights[slot, at, 0:C, :]]
        right += [weights[slot, at, 2 * C :, :], filler]
    both = dot(jnp.concatenate(center, axis=1), jnp.concatenate(joint, axis=0))
    even_sum = dot(jnp.concatenate(before, axis=1), jnp.concatenate(left, axis=0))
    odd_sum = dot(jnp.concatenate(after, axis=1), jnp.concatenate(right, axis=0))
    return both[:, :C] + even_sum, both[:, SECOND:] + odd_sum


def temporal(u0, u1, pairs, slot):
    gap = jnp.zeros((u0.shape[0], PAD), u0.dtype)
    both = dot(jnp.concatenate([u0, gap, u1, gap], axis=1), pairs[slot])
    return both[:, :C], both[:, SECOND:]


def frequency_kernel(out):
    half = out.shape[1] // 2
    at = lax.broadcasted_iota(jnp.int32, out.shape, 1)
    index = jnp.where(at < half, at, at - half).astype(jnp.float32)
    out[...] = jnp.exp(-math.log(10000.0) * index / half)


def prepare_kernel(
    bounds_hbm,
    timesteps_hbm,
    gains_hbm,
    time_hbm,
    frequency,
    spatial_weight,
    temporal_weight,
    info,
    bias,
    gain_pairs,
    spatial_pairs,
    temporal_pairs,
    bounds,
    timesteps,
    gains,
    time_weight,
    sems,
):
    copies = [
        pltpu.make_async_copy(source, target, sems.at[n])
        for n, (source, target) in enumerate(
            (
                (bounds_hbm, bounds),
                (timesteps_hbm, timesteps),
                (gains_hbm, gains),
                (time_hbm, time_weight),
            )
        )
    ]
    for copy in copies:
        copy.start()
    for slot in range(2):
        for dy in range(3):
            kernel = spatial_weight.at[slot, dy]
            spatial_pairs[slot, dy, :, 0:C] = kernel[C : 3 * C, :]
            spatial_pairs[slot, dy, :, SECOND : SECOND + C] = kernel[0 : 2 * C, :]
        for frame, lanes in enumerate((slice(0, C), slice(SECOND, SECOND + C))):
            for other in range(2):
                tap = temporal_weight.at[slot, 1 - frame + other]
                temporal_pairs[slot, other * SECOND : other * SECOND + C, lanes] = tap[...]
                temporal_pairs[slot, other * SECOND + C : (other + 1) * SECOND, lanes] = tap[0:PAD, :]
    for copy in copies:
        copy.wait()
    segment = lax.axis_index("segment")
    info[...] = jnp.full(info.shape, bounds[segment + 1] - bounds[segment], jnp.int32)
    gain_pairs[...] = jnp.concatenate([gains[...], gains[...]], axis=1)
    entries = time_weight.shape[1]
    half = entries // 2
    at = lax.broadcasted_iota(jnp.int32, (8, entries), 1)
    step = lax.broadcasted_iota(jnp.int32, (8, entries), 0)
    times = jnp.zeros((8, entries), jnp.int32)
    for s in range(STEPS):
        times = jnp.where(step == s, timesteps[s], times)
    angle = times.astype(jnp.float32) * frequency[...]
    emb = jnp.where(at < half, jnp.cos(angle), jnp.sin(angle))
    for slot in range(2):
        made = jnp.dot(
            emb,
            time_weight[slot],
            precision=lax.Precision.HIGHEST,
            preferred_element_type=jnp.float32,
        )
        for s in range(STEPS):
            bias[s, slot : slot + 1, :] = made[s : s + 1]


def place():
    row_group = lax.axis_index("rows")
    at_end = (row_group == 0) | (row_group == lax.axis_size("rows") - 1)
    return lax.rem(row_group, 2), at_end


def first_kernel(step, info, own, far, gains, sw, sp, part, n_own, n_far, wide, thin):
    count = jnp.max(info[0:1, :])
    odd, at_end = place()
    mine, by_far = load(own), load(far)
    if step == 0:
        mine, by_far = flip_if(odd, mine), flip_if(1 - odd, by_far)
    by_far = jnp.where(at_end, 0.0, by_far)
    gain = gains[0:1, :].reshape(1, 1, PAIR)
    normed, far_normed = normalise(mine, gain), normalise(by_far, gain)
    n_own[...] = normed
    n_far[...] = far_normed

    @pl.when(count > 1)
    def _():
        put_wide(wide, 0, flip(far_normed), normed)
        even, odd_sum = spatial(wide, True, (0,), sw, sp, 0, odd)
        part[0], part[1] = even, odd_sum

    @pl.when(count == 1)
    def _():
        put_thin(thin, 0, halves(far_normed, flip(normed)))
        put_thin(thin, 1, normed)
        even, odd_sum = spatial(thin, False, (0, 1), sw, sp, 0, odd)
        part[0, : FIELD], part[1, : FIELD] = even, odd_sum


def second_kernel(
    step, info, own, far, core, part, n_own, n_far, bias, gains, sw, sp, tp, out, wide, thin, acc, center
):
    count = jnp.max(info[0:1, :])
    odd, at_end = place()
    mine, by_core = load(own), load(core)
    if step == 0:
        mine, by_core = flip_if(odd, mine), flip_if(1 - odd, by_core)
    core_normed = normalise(by_core, gains[0:1, :].reshape(1, 1, PAIR))

    @pl.when(count == 1)
    def _():
        put_thin(thin, 2, halves(flip(n_own[...]), core_normed))
        even, odd_sum = spatial(thin, False, (2,), sw, sp, 0, odd)
        acc[0], acc[1] = part[0, :FIELD] + even, part[1, :FIELD] + odd_sum
        center[...] = mine

    @pl.when(count > 1)
    def _():
        normed = n_own[...]
        turned = flip(normed)
        put_wide(wide, 1, halves(n_far[...], turned), halves(turned, core_normed))
        put_wide(wide, 2, normed, flip(core_normed))
        even, odd_sum = spatial(wide, True, (1, 2), sw, sp, 0, odd)
        even = part[0] + even + bias[step, 0:1, :]
        odd_sum = part[1] + odd_sum + bias[step, 0:1, :]
        half = FIELD
        u_even, u_odd = silu(even).astype(jnp.bfloat16), silu(odd_sum).astype(jnp.bfloat16)
        u0 = jnp.concatenate([u_even[:half], u_odd[:half]], axis=0)
        u1 = jnp.concatenate([u_even[half:], u_odd[half:]], axis=0)
        v0, v1 = temporal(u0, u1, tp, 0)
        v_even = jnp.concatenate([v0[:half], v1[:half]], axis=0)
        v_odd = jnp.concatenate([v0[half:], v1[half:]], axis=0)
        change = jnp.concatenate([even + v_even, odd_sum + v_odd], axis=1)
        change = change.reshape(FRAMES * J, 2 * GROUP, PAIR)
        by_far = load(far)
        if step == 0:
            by_far = flip_if(1 - odd, by_far)
        back = flip(mine)
        first = halves(by_far, back) + change[:, :GROUP]
        second = halves(back, by_core) + change[:, GROUP:]
        first = first.astype(jnp.bfloat16).astype(jnp.float32)
        second = second.astype(jnp.bfloat16).astype(jnp.float32)
        row = lax.broadcasted_iota(jnp.int32, first.shape, 1)
        first = jnp.where((row < HB) & at_end, 0.0, first)
        center[...] = halves(flip(first), flip(second))
        gain = gains[1:2, :].reshape(1, 1, PAIR)
        n_first, n_second = normalise(first, gain), normalise(second, gain)
        put_thin(thin, 0, n_first)
        put_thin(thin, 1, halves(flip(n_first), flip(n_second)))
        put_thin(thin, 2, n_second)
        even, odd_sum = spatial(thin, False, (0, 1, 2), sw, sp, 1, odd)
        acc[0], acc[1] = even, odd_sum

    last = count - 1
    shift = bias[step, pl.ds(last, 1), :]
    even = (acc[0] + shift).reshape(J, FRAMES, GROUP, C)
    odd_sum = (acc[1] + shift).reshape(J, FRAMES, GROUP, C)
    u0, u1 = (
        jnp.concatenate(
            [silu(even[:, f]).reshape(-1, C), silu(odd_sum[:, f]).reshape(-1, C)], axis=0
        )
        for f in range(FRAMES)
    )
    v0, v1 = temporal(u0.astype(jnp.bfloat16), u1.astype(jnp.bfloat16), tp, last)
    half = J * GROUP
    for f, v in enumerate((v0, v1)):
        a_even, a_odd = even[:, f].reshape(half, C), odd_sum[:, f].reshape(half, C)
        change = jnp.concatenate([a_even + v[:half], a_odd + v[half:]], axis=1)
        result = center[f * J : (f + 1) * J] + change.reshape(J, GROUP, PAIR)
        if step == STEPS - 1:
            result = flip_if(odd, result)
        out[f * half : (f + 1) * half, :] = result.reshape(half, PAIR).astype(jnp.bfloat16)


VMEM = pl.BlockSpec(memory_space=pltpu.VMEM)


def call(kernel, name, outs, scratch, flops):
    return pl.pallas_call(
        kernel,
        out_shape=tuple(jax.ShapeDtypeStruct(shape, dtype) for shape, dtype in outs),
        out_specs=(VMEM,) * len(outs),
        scratch_shapes=[pltpu.VMEM(shape, dtype) for shape, dtype in scratch],
        compiler_params=pltpu.CompilerParams(vmem_limit_bytes=24 * 1024 * 1024),
        cost_estimate=pl.CostEstimate(
            flops=flops, bytes_accessed=flops // 4_000, transcendentals=0
        ),
        name=name,
    )


def prepare(bounds, timesteps, gains, time_weight, spatial_weight, temporal_weight):
    hbm = pl.BlockSpec(memory_space=pltpu.HBM)
    (frequency,) = call(
        frequency_kernel, "frequency", [((8, time_weight.shape[1]), jnp.float32)], [], 4_000_000_000
    )()
    return pl.pallas_call(
        prepare_kernel,
        out_shape=(
            jax.ShapeDtypeStruct((8, 128), jnp.int32),
            jax.ShapeDtypeStruct((STEPS, 2, C), jnp.float32),
            jax.ShapeDtypeStruct((2, PAIR), jnp.float32),
            jax.ShapeDtypeStruct((2, 3, 2 * C, SECOND + C), jnp.bfloat16),
            jax.ShapeDtypeStruct((2, 2 * SECOND, SECOND + C), jnp.bfloat16),
        ),
        in_specs=[hbm, hbm, hbm, hbm, VMEM, VMEM, VMEM],
        out_specs=(VMEM,) * 5,
        scratch_shapes=[
            pltpu.SMEM(bounds.shape, jnp.int32),
            pltpu.SMEM(timesteps.shape, jnp.int32),
            pltpu.VMEM(gains.shape, jnp.float32),
            pltpu.VMEM(time_weight.shape, jnp.float32),
            pltpu.SemaphoreType.DMA((4,)),
        ],
        compiler_params=pltpu.CompilerParams(vmem_limit_bytes=24 * 1024 * 1024),
        cost_estimate=pl.CostEstimate(
            flops=8_000_000_000, bytes_accessed=1_000_000, transcendentals=10_000
        ),
        name="prepare",
    )(bounds, timesteps, gains, time_weight, frequency, spatial_weight, temporal_weight)


WIDE = ((3, FRAMES, J + 2, 2 * GROUP, LANES), jnp.bfloat16)
THIN = ((3, J + 2, FRAMES * GROUP, LANES), jnp.bfloat16)
ROWS_F32 = ((FRAMES * J, GROUP, PAIR), jnp.float32)


def apply_blocks(step, info, own, far, core, bias, gains, sw, sp, tp):
    part, n_own, n_far = call(
        functools.partial(first_kernel, step),
        "own_and_far_rows",
        [((2, 2 * FIELD, C), jnp.float32), ROWS_F32, ROWS_F32],
        [WIDE, THIN],
        1_000_000,
    )(info, own, far, gains, sw, sp)
    (field,) = call(
        functools.partial(second_kernel, step),
        "residual_blocks",
        [((FIELD, PAIR), jnp.bfloat16)],
        [WIDE, THIN, ((2, FIELD, C), jnp.float32), ROWS_F32],
        4_000_000_000,
    )(info, own, far, core, part, n_own, n_far, bias, gains, sw, sp, tp)
    return field


def body(state, bounds, timesteps, gains, spatial_weight, temporal_weight, time_weight):
    groups = lax.axis_size("rows")
    segments = lax.axis_size("segment")
    sw = spatial_weight.reshape(2, 3, 3 * C, C)
    tw = temporal_weight.reshape(2, 3, C, C)
    made = prepare(bounds, timesteps, gains[0], time_weight[0], sw, tw)
    ahead = [(i, (i + 1) % segments) for i in range(segments)]
    on_chip = [(i, i ^ 1) for i in range(groups)]
    off_chip = [(i, i + 1) for i in range(1, groups - 1, 2)]
    off_chip = off_chip + [(j, i) for i, j in off_chip]
    off_chip_ahead = [
        (a * groups + i, b * groups + j) for a, b in ahead for i, j in off_chip
    ]
    ends = [k * groups + i for k in range(segments) for i in (0, groups - 1)]
    off_chip_ahead += [(i, i) for i in ends]

    field = state.reshape(FRAMES, ROWS, HB, J, PAIR).transpose(0, 3, 1, 2, 4).reshape(FIELD, PAIR)
    for step in range(STEPS):
        far = lax.ppermute(field, ("segment", "rows"), off_chip_ahead)
        own = lax.ppermute(field, "segment", ahead)
        if step == 0:
            far, own, made = lax.optimization_barrier((far, own, made))
            info, bias, gain_pairs, sp, tp = made
        core = lax.ppermute(own, "rows", on_chip)
        field = apply_blocks(step, info, own, far, core, bias, gain_pairs, sw, sp, tp)
    field = field.reshape(FRAMES, J, ROWS, HB, PAIR).transpose(0, 2, 3, 1, 4)
    return field.reshape(1, FRAMES, ROWS, W * C)


def solution(mesh):
    placed = (
        P("segment", None, "rows", None),
        P(),
        P(),
        P("segment", None, None),
        P("segment", None, None, None, None, None),
        P("segment", None, None, None, None),
        P("segment", None, None, None),
    )
    return jax.shard_map(
        body,
        mesh=mesh,
        in_specs=placed,
        out_specs=P("segment", None, "rows", None),
        check_vma=False,
    )
```

```python
import functools
import math

import jax
import jax.numpy as jnp
from jax import lax
from jax.experimental import pallas as pl
from jax.experimental.pallas import tpu as pltpu
from jax.sharding import PartitionSpec as P

C = 320
W = 72
STEPS = 2
FRAMES = 2
ROWS = 2

HB = 4
J = W // 2 // HB
PAIR = 2 * C
GROUP = ROWS * HB
FIELD = FRAMES * J * GROUP
PAD = 64
LANES = PAIR + 256
SECOND = C + PAD
EPS = 1e-06


def low_lanes(shape):
    return lax.broadcasted_iota(jnp.int32, shape, len(shape) - 1) < PAD


def normalise(value, gain):
    low = low_lanes(value[..., 256:384].shape)
    square = value * value
    middle = square[..., 256:384]
    first = square[..., 0:128] + square[..., 128:256] + jnp.where(low, middle, 0.0)
    second = square[..., 384:512] + square[..., 512:640] + jnp.where(low, 0.0, middle)
    scale = lax.rsqrt(jnp.sum(first, axis=-1, keepdims=True) / C + EPS)
    other = lax.rsqrt(jnp.sum(second, axis=-1, keepdims=True) / C + EPS)
    scaled = jnp.concatenate(
        [
            value[..., 0:256] * scale,
            value[..., 256:384] * jnp.where(low, scale, other),
            value[..., 384:640] * other,
        ],
        axis=-1,
    )
    return scaled * gain


def load(ref):
    return ref[...].astype(jnp.float32).reshape(FRAMES * J, GROUP, PAIR)


def flip(value):
    return pltpu.roll(value, HB, 1)


def flip_if(odd, value):
    return pltpu.roll(value, HB * odd, 1)


def halves(first, second):
    row = lax.broadcasted_iota(jnp.int32, first.shape, 1)
    return jnp.where(row < HB, first, second)


def shifted_h(value, by):
    rows = value.shape[0]
    moved = pltpu.roll(value, by % rows, 0)
    h = lax.rem(lax.broadcasted_iota(jnp.int32, value.shape, 0), HB)
    edge = 0 if by == 1 else HB - 1
    return jnp.where(h == edge, 0.0, moved)


def put(ref, at, value):
    middle = value[..., 256:384]
    low = low_lanes(middle.shape)
    ref[at + (slice(None), slice(0, PAIR))] = value.astype(jnp.bfloat16)
    ref[at + (slice(None), slice(PAIR, PAIR + 128))] = jnp.where(low, 0.0, middle).astype(
        jnp.bfloat16
    )
    ref[at + (slice(None), slice(PAIR + 128, LANES))] = jnp.where(low, middle, 0.0).astype(
        jnp.bfloat16
    )


def put_wide(ref, dy, first, second):
    tiles = jnp.concatenate([first, second], axis=1).reshape(FRAMES, J, 2 * GROUP, PAIR)
    put(ref, (dy, slice(None), slice(1, J + 1)), tiles)
    for f in range(FRAMES):
        put(ref, (dy, f, 0), shifted_h(tiles[f, J - 1], 1))
        put(ref, (dy, f, J + 1), shifted_h(tiles[f, 0], -1))


def put_thin(ref, dy, value):
    tiles = value.reshape(FRAMES, J, GROUP, PAIR)
    tiles = jnp.concatenate([tiles[0], tiles[1]], axis=1)
    put(ref, (dy, slice(1, J + 1)), tiles)
    put(ref, (dy, 0), shifted_h(tiles[J - 1], 1))
    put(ref, (dy, J + 1), shifted_h(tiles[0], -1))


def rows_of(ref, dy, j0, wide, start, stop):
    if wide:
        return ref[dy, :, j0 : j0 + J, :, start:stop].reshape(-1, stop - start)
    return ref[dy, j0 : j0 + J, :, start:stop].reshape(-1, stop - start)


def silu(value):
    half = 0.5 * value
    return half + half * jnp.tanh(half)


def dot(a, b):
    return jnp.dot(a, b, preferred_element_type=jnp.float32)


def spatial(ref, wide, taps, weights, pairs, slot, odd):
    center, before, after, joint, left, right = [], [], [], [], [], []
    for dy in taps:
        at = dy + odd * (2 - 2 * dy)
        rows = functools.partial(rows_of, ref, dy, wide=wide)
        center.append(rows(1, start=0, stop=PAIR))
        before += [rows(0, start=PAIR, stop=PAIR + 128), rows(0, start=384, stop=PAIR)]
        after += [rows(2, start=0, stop=256), rows(2, start=PAIR + 128, stop=LANES)]
        filler = weights[slot, at, 0:PAD, :]
        joint.append(pairs[slot, at])
        left += [filler, weights[slot, at, 0:C, :]]
        right += [weights[slot, at, 2 * C :, :], filler]
    both = dot(jnp.concatenate(center, axis=1), jnp.concatenate(joint, axis=0))
    even_sum = dot(jnp.concatenate(before, axis=1), jnp.concatenate(left, axis=0))
    odd_sum = dot(jnp.concatenate(after, axis=1), jnp.concatenate(right, axis=0))
    return both[:, :C] + even_sum, both[:, SECOND:] + odd_sum


def temporal(u0, u1, pairs, slot):
    gap = jnp.zeros((u0.shape[0], PAD), u0.dtype)
    both = dot(jnp.concatenate([u0, gap, u1, gap], axis=1), pairs[slot])
    return both[:, :C], both[:, SECOND:]


def frequency_kernel(out):
    half = out.shape[1] // 2
    at = lax.broadcasted_iota(jnp.int32, out.shape, 1)
    index = jnp.where(at < half, at, at - half).astype(jnp.float32)
    out[...] = jnp.exp(-math.log(10000.0) * index / half)


def prepare_kernel(
    bounds_hbm,
    timesteps_hbm,
    gains_hbm,
    time_hbm,
    frequency,
    spatial_weight,
    temporal_weight,
    info,
    bias,
    gain_pairs,
    spatial_pairs,
    temporal_pairs,
    bounds,
    timesteps,
    gains,
    time_weight,
    sems,
):
    copies = [
        pltpu.make_async_copy(source, target, sems.at[n])
        for n, (source, target) in enumerate(
            (
                (bounds_hbm, bounds),
                (timesteps_hbm, timesteps),
                (gains_hbm, gains),
                (time_hbm, time_weight),
            )
        )
    ]
    for copy in copies:
        copy.start()
    for slot in range(2):
        for dy in range(3):
            kernel = spatial_weight.at[slot, dy]
            spatial_pairs[slot, dy, :, 0:C] = kernel[C : 3 * C, :]
            spatial_pairs[slot, dy, :, SECOND : SECOND + C] = kernel[0 : 2 * C, :]
        for frame, lanes in enumerate((slice(0, C), slice(SECOND, SECOND + C))):
            for other in range(2):
                tap = temporal_weight.at[slot, 1 - frame + other]
                temporal_pairs[slot, other * SECOND : other * SECOND + C, lanes] = tap[...]
                temporal_pairs[slot, other * SECOND + C : (other + 1) * SECOND, lanes] = tap[0:PAD, :]
    for copy in copies:
        copy.wait()
    segment = lax.axis_index("segment")
    info[...] = jnp.full(info.shape, bounds[segment + 1] - bounds[segment], jnp.int32)
    gain_pairs[...] = jnp.concatenate([gains[...], gains[...]], axis=1)
    entries = time_weight.shape[1]
    half = entries // 2
    at = lax.broadcasted_iota(jnp.int32, (8, entries), 1)
    step = lax.broadcasted_iota(jnp.int32, (8, entries), 0)
    times = jnp.zeros((8, entries), jnp.int32)
    for s in range(STEPS):
        times = jnp.where(step == s, timesteps[s], times)
    angle = times.astype(jnp.float32) * frequency[...]
    emb = jnp.where(at < half, jnp.cos(angle), jnp.sin(angle))
    for slot in range(2):
        made = jnp.dot(
            emb,
            time_weight[slot],
            precision=lax.Precision.HIGHEST,
            preferred_element_type=jnp.float32,
        )
        for s in range(STEPS):
            bias[s, slot : slot + 1, :] = made[s : s + 1]


def place():
    row_group = lax.axis_index("rows")
    at_end = (row_group == 0) | (row_group == lax.axis_size("rows") - 1)
    return lax.rem(row_group, 2), at_end


def first_kernel(step, info, own, far, gains, sw, sp, part, n_own, n_far, wide, thin):
    count = jnp.max(info[0:1, :])
    odd, at_end = place()
    mine, by_far = load(own), load(far)
    if step == 0:
        mine, by_far = flip_if(odd, mine), flip_if(1 - odd, by_far)
    by_far = jnp.where(at_end, 0.0, by_far)
    gain = gains[0:1, :].reshape(1, 1, PAIR)
    normed, far_normed = normalise(mine, gain), normalise(by_far, gain)
    n_own[...] = normed
    n_far[...] = far_normed

    @pl.when(count > 1)
    def _():
        put_wide(wide, 0, flip(far_normed), normed)
        even, odd_sum = spatial(wide, True, (0,), sw, sp, 0, odd)
        part[0], part[1] = even, odd_sum

    @pl.when(count == 1)
    def _():
        put_thin(thin, 0, halves(far_normed, flip(normed)))
        put_thin(thin, 1, normed)
        even, odd_sum = spatial(thin, False, (0, 1), sw, sp, 0, odd)
        part[0, : FIELD], part[1, : FIELD] = even, odd_sum


def second_kernel(
    step, info, own, far, core, part, n_own, n_far, bias, gains, sw, sp, tp, out, wide, thin, acc, center
):
    count = jnp.max(info[0:1, :])
    odd, at_end = place()
    mine, by_core = load(own), load(core)
    if step == 0:
        mine, by_core = flip_if(odd, mine), flip_if(1 - odd, by_core)
    core_normed = normalise(by_core, gains[0:1, :].reshape(1, 1, PAIR))

    @pl.when(count == 1)
    def _():
        put_thin(thin, 2, halves(flip(n_own[...]), core_normed))
        even, odd_sum = spatial(thin, False, (2,), sw, sp, 0, odd)
        acc[0], acc[1] = part[0, :FIELD] + even, part[1, :FIELD] + odd_sum
        center[...] = mine

    @pl.when(count > 1)
    def _():
        normed = n_own[...]
        turned = flip(normed)
        put_wide(wide, 1, halves(n_far[...], turned), halves(turned, core_normed))
        put_wide(wide, 2, normed, flip(core_normed))
        even, odd_sum = spatial(wide, True, (1, 2), sw, sp, 0, odd)
        even = part[0] + even + bias[step, 0:1, :]
        odd_sum = part[1] + odd_sum + bias[step, 0:1, :]
        half = FIELD
        u_even, u_odd = silu(even).astype(jnp.bfloat16), silu(odd_sum).astype(jnp.bfloat16)
        u0 = jnp.concatenate([u_even[:half], u_odd[:half]], axis=0)
        u1 = jnp.concatenate([u_even[half:], u_odd[half:]], axis=0)
        v0, v1 = temporal(u0, u1, tp, 0)
        v_even = jnp.concatenate([v0[:half], v1[:half]], axis=0)
        v_odd = jnp.concatenate([v0[half:], v1[half:]], axis=0)
        change = jnp.concatenate([even + v_even, odd_sum + v_odd], axis=1)
        change = change.reshape(FRAMES * J, 2 * GROUP, PAIR)
        by_far = load(far)
        if step == 0:
            by_far = flip_if(1 - odd, by_far)
        back = flip(mine)
        first = halves(by_far, back) + change[:, :GROUP]
        second = halves(back, by_core) + change[:, GROUP:]
        first = first.astype(jnp.bfloat16).astype(jnp.float32)
        second = second.astype(jnp.bfloat16).astype(jnp.float32)
        row = lax.broadcasted_iota(jnp.int32, first.shape, 1)
        first = jnp.where((row < HB) & at_end, 0.0, first)
        center[...] = halves(flip(first), flip(second))
        gain = gains[1:2, :].reshape(1, 1, PAIR)
        n_first, n_second = normalise(first, gain), normalise(second, gain)
        put_thin(thin, 0, n_first)
        put_thin(thin, 1, halves(flip(n_first), flip(n_second)))
        put_thin(thin, 2, n_second)
        even, odd_sum = spatial(thin, False, (0, 1, 2), sw, sp, 1, odd)
        acc[0], acc[1] = even, odd_sum

    last = count - 1
    shift = bias[step, pl.ds(last, 1), :]
    even = (acc[0] + shift).reshape(J, FRAMES, GROUP, C)
    odd_sum = (acc[1] + shift).reshape(J, FRAMES, GROUP, C)
    u0, u1 = (
        jnp.concatenate(
            [silu(even[:, f]).reshape(-1, C), silu(odd_sum[:, f]).reshape(-1, C)], axis=0
        )
        for f in range(FRAMES)
    )
    v0, v1 = temporal(u0.astype(jnp.bfloat16), u1.astype(jnp.bfloat16), tp, last)
    half = J * GROUP
    for f, v in enumerate((v0, v1)):
        a_even, a_odd = even[:, f].reshape(half, C), odd_sum[:, f].reshape(half, C)
        change = jnp.concatenate([a_even + v[:half], a_odd + v[half:]], axis=1)
        result = center[f * J : (f + 1) * J] + change.reshape(J, GROUP, PAIR)
        if step == STEPS - 1:
            result = flip_if(odd, result)
        out[f * half : (f + 1) * half, :] = result.reshape(half, PAIR).astype(jnp.bfloat16)


VMEM = pl.BlockSpec(memory_space=pltpu.VMEM)


def call(kernel, name, outs, scratch, flops):
    return pl.pallas_call(
        kernel,
        out_shape=tuple(jax.ShapeDtypeStruct(shape, dtype) for shape, dtype in outs),
        out_specs=(VMEM,) * len(outs),
        scratch_shapes=[pltpu.VMEM(shape, dtype) for shape, dtype in scratch],
        compiler_params=pltpu.CompilerParams(vmem_limit_bytes=24 * 1024 * 1024),
        cost_estimate=pl.CostEstimate(
            flops=flops, bytes_accessed=flops // 4_000, transcendentals=0
        ),
        name=name,
    )


def prepare(bounds, timesteps, gains, time_weight, spatial_weight, temporal_weight):
    hbm = pl.BlockSpec(memory_space=pltpu.HBM)
    (frequency,) = call(
        frequency_kernel, "frequency", [((8, time_weight.shape[1]), jnp.float32)], [], 4_000_000_000
    )()
    return pl.pallas_call(
        prepare_kernel,
        out_shape=(
            jax.ShapeDtypeStruct((8, 128), jnp.int32),
            jax.ShapeDtypeStruct((STEPS, 2, C), jnp.float32),
            jax.ShapeDtypeStruct((2, PAIR), jnp.float32),
            jax.ShapeDtypeStruct((2, 3, 2 * C, SECOND + C), jnp.bfloat16),
            jax.ShapeDtypeStruct((2, 2 * SECOND, SECOND + C), jnp.bfloat16),
        ),
        in_specs=[hbm, hbm, hbm, hbm, VMEM, VMEM, VMEM],
        out_specs=(VMEM,) * 5,
        scratch_shapes=[
            pltpu.SMEM(bounds.shape, jnp.int32),
            pltpu.SMEM(timesteps.shape, jnp.int32),
            pltpu.VMEM(gains.shape, jnp.float32),
            pltpu.VMEM(time_weight.shape, jnp.float32),
            pltpu.SemaphoreType.DMA((4,)),
        ],
        compiler_params=pltpu.CompilerParams(vmem_limit_bytes=24 * 1024 * 1024),
        cost_estimate=pl.CostEstimate(
            flops=8_000_000_000, bytes_accessed=1_000_000, transcendentals=10_000
        ),
        name="prepare",
    )(bounds, timesteps, gains, time_weight, frequency, spatial_weight, temporal_weight)


WIDE = ((3, FRAMES, J + 2, 2 * GROUP, LANES), jnp.bfloat16)
THIN = ((3, J + 2, FRAMES * GROUP, LANES), jnp.bfloat16)
ROWS_F32 = ((FRAMES * J, GROUP, PAIR), jnp.float32)


def apply_blocks(step, info, own, far, core, bias, gains, sw, sp, tp):
    part, n_own, n_far = call(
        functools.partial(first_kernel, step),
        "own_and_far_rows",
        [((2, 2 * FIELD, C), jnp.float32), ROWS_F32, ROWS_F32],
        [WIDE, THIN],
        1_000_000,
    )(info, own, far, gains, sw, sp)
    (field,) = call(
        functools.partial(second_kernel, step),
        "residual_blocks",
        [((FIELD, PAIR), jnp.bfloat16)],
        [WIDE, THIN, ((2, FIELD, C), jnp.float32), ROWS_F32],
        4_000_000_000,
    )(info, own, far, core, part, n_own, n_far, bias, gains, sw, sp, tp)
    return field


def body(state, bounds, timesteps, gains, spatial_weight, temporal_weight, time_weight):
    groups = lax.axis_size("rows")
    segments = lax.axis_size("segment")
    sw = spatial_weight.reshape(2, 3, 3 * C, C)
    tw = temporal_weight.reshape(2, 3, C, C)
    made = prepare(bounds, timesteps, gains[0], time_weight[0], sw, tw)
    ahead = [(i, (i + 1) % segments) for i in range(segments)]
    on_chip = [(i, i ^ 1) for i in range(groups)]
    off_chip = [(i, i + 1) for i in range(1, groups - 1, 2)]
    off_chip = off_chip + [(j, i) for i, j in off_chip]
    off_chip_ahead = [
        (a * groups + i, b * groups + j) for a, b in ahead for i, j in off_chip
    ]
    across = [(k, (k + segments // 2) % segments) for k in range(segments)]
    off_chip_ahead += [
        (a * groups + i, b * groups + i) for a, b in across for i in (0, groups - 1)
    ]

    field = state.reshape(FRAMES, ROWS, HB, J, PAIR).transpose(0, 3, 1, 2, 4).reshape(FIELD, PAIR)
    for step in range(STEPS):
        far = lax.ppermute(field, ("segment", "rows"), off_chip_ahead)
        own = lax.ppermute(field, "segment", ahead)
        if step == 0:
            far, own, made = lax.optimization_barrier((far, own, made))
            info, bias, gain_pairs, sp, tp = made
        core = lax.ppermute(own, "rows", on_chip)
        field = apply_blocks(step, info, own, far, core, bias, gain_pairs, sw, sp, tp)
    field = field.reshape(FRAMES, J, ROWS, HB, PAIR).transpose(0, 2, 3, 1, 4)
    return field.reshape(1, FRAMES, ROWS, W * C)


def solution(mesh):
    placed = (
        P("segment", None, "rows", None),
        P(),
        P(),
        P("segment", None, None),
        P("segment", None, None, None, None, None),
        P("segment", None, None, None, None),
        P("segment", None, None, None),
    )
    return jax.shard_map(
        body,
        mesh=mesh,
        in_specs=placed,
        out_specs=P("segment", None, "rows", None),
        check_vma=False,
    )
```

```python
import functools
import math

import jax
import jax.numpy as jnp
from jax import lax
from jax.experimental import pallas as pl
from jax.experimental.pallas import tpu as pltpu
from jax.sharding import PartitionSpec as P

C = 320
W = 72
STEPS = 2
FRAMES = 2
ROWS = 2

HB = 4
J = W // 2 // HB
PAIR = 2 * C
GROUP = ROWS * HB
FIELD = FRAMES * J * GROUP
PAD = 64
LANES = PAIR + 256
SECOND = C + PAD
EPS = 1e-06


def low_lanes(shape):
    return lax.broadcasted_iota(jnp.int32, shape, len(shape) - 1) < PAD


def normalise(value, gain):
    low = low_lanes(value[..., 256:384].shape)
    square = value * value
    middle = square[..., 256:384]
    first = square[..., 0:128] + square[..., 128:256] + jnp.where(low, middle, 0.0)
    second = square[..., 384:512] + square[..., 512:640] + jnp.where(low, 0.0, middle)
    scale = lax.rsqrt(jnp.sum(first, axis=-1, keepdims=True) / C + EPS)
    other = lax.rsqrt(jnp.sum(second, axis=-1, keepdims=True) / C + EPS)
    scaled = jnp.concatenate(
        [
            value[..., 0:256] * scale,
            value[..., 256:384] * jnp.where(low, scale, other),
            value[..., 384:640] * other,
        ],
        axis=-1,
    )
    return scaled * gain


def load(ref):
    return ref[...].astype(jnp.float32).reshape(FRAMES * J, GROUP, PAIR)


def flip(value):
    return pltpu.roll(value, HB, 1)


def flip_if(odd, value):
    return pltpu.roll(value, HB * odd, 1)


def halves(first, second):
    row = lax.broadcasted_iota(jnp.int32, first.shape, 1)
    return jnp.where(row < HB, first, second)


def shifted_h(value, by):
    rows = value.shape[0]
    moved = pltpu.roll(value, by % rows, 0)
    h = lax.rem(lax.broadcasted_iota(jnp.int32, value.shape, 0), HB)
    edge = 0 if by == 1 else HB - 1
    return jnp.where(h == edge, 0.0, moved)


def put(ref, at, value):
    middle = value[..., 256:384]
    low = low_lanes(middle.shape)
    ref[at + (slice(None), slice(0, PAIR))] = value.astype(jnp.bfloat16)
    ref[at + (slice(None), slice(PAIR, PAIR + 128))] = jnp.where(low, 0.0, middle).astype(
        jnp.bfloat16
    )
    ref[at + (slice(None), slice(PAIR + 128, LANES))] = jnp.where(low, middle, 0.0).astype(
        jnp.bfloat16
    )


def put_wide(ref, dy, first, second):
    tiles = jnp.concatenate([first, second], axis=1).reshape(FRAMES, J, 2 * GROUP, PAIR)
    put(ref, (dy, slice(None), slice(1, J + 1)), tiles)
    for f in range(FRAMES):
        put(ref, (dy, f, 0), shifted_h(tiles[f, J - 1], 1))
        put(ref, (dy, f, J + 1), shifted_h(tiles[f, 0], -1))


def put_thin(ref, dy, value):
    tiles = value.reshape(FRAMES, J, GROUP, PAIR)
    tiles = jnp.concatenate([tiles[0], tiles[1]], axis=1)
    put(ref, (dy, slice(1, J + 1)), tiles)
    put(ref, (dy, 0), shifted_h(tiles[J - 1], 1))
    put(ref, (dy, J + 1), shifted_h(tiles[0], -1))


def rows_of(ref, dy, j0, wide, start, stop):
    if wide is not None:
        return ref[dy, wide, j0 : j0 + J, :, start:stop].reshape(-1, stop - start)
    return ref[dy, j0 : j0 + J, :, start:stop].reshape(-1, stop - start)


def silu(value):
    half = 0.5 * value
    return half + half * jnp.tanh(half)


def dot(a, b):
    return jnp.dot(a, b, preferred_element_type=jnp.float32)


def spatial(ref, wide, taps, weights, pairs, slot, odd):
    if wide is True:
        sums = [spatial(ref, f, taps, weights, pairs, slot, odd) for f in range(FRAMES)]
        return tuple(jnp.concatenate(parity, axis=0) for parity in zip(*sums))
    center, before, after, joint, left, right = [], [], [], [], [], []
    for dy in taps:
        at = dy + odd * (2 - 2 * dy)
        rows = functools.partial(rows_of, ref, dy, wide=wide)
        center.append(rows(1, start=0, stop=PAIR))
        before += [rows(0, start=PAIR, stop=PAIR + 128), rows(0, start=384, stop=PAIR)]
        after += [rows(2, start=0, stop=256), rows(2, start=PAIR + 128, stop=LANES)]
        filler = weights[slot, at, 0:PAD, :]
        joint.append(pairs[slot, at])
        left += [filler, weights[slot, at, 0:C, :]]
        right += [weights[slot, at, 2 * C :, :], filler]
    both = dot(jnp.concatenate(center, axis=1), jnp.concatenate(joint, axis=0))
    even_sum = dot(jnp.concatenate(before, axis=1), jnp.concatenate(left, axis=0))
    odd_sum = dot(jnp.concatenate(after, axis=1), jnp.concatenate(right, axis=0))
    return both[:, :C] + even_sum, both[:, SECOND:] + odd_sum


def temporal(u0, u1, pairs, slot):
    gap = jnp.zeros((u0.shape[0], PAD), u0.dtype)
    both = dot(jnp.concatenate([u0, gap, u1, gap], axis=1), pairs[slot])
    return both[:, :C], both[:, SECOND:]


def frequency_kernel(out):
    half = out.shape[1] // 2
    at = lax.broadcasted_iota(jnp.int32, out.shape, 1)
    index = jnp.where(at < half, at, at - half).astype(jnp.float32)
    out[...] = jnp.exp(-math.log(10000.0) * index / half)


def prepare_kernel(
    bounds_hbm,
    timesteps_hbm,
    gains_hbm,
    time_hbm,
    frequency,
    spatial_weight,
    temporal_weight,
    info,
    bias,
    gain_pairs,
    spatial_pairs,
    temporal_pairs,
    bounds,
    timesteps,
    gains,
    time_weight,
    sems,
):
    copies = [
        pltpu.make_async_copy(source, target, sems.at[n])
        for n, (source, target) in enumerate(
            (
                (bounds_hbm, bounds),
                (timesteps_hbm, timesteps),
                (gains_hbm, gains),
                (time_hbm, time_weight),
            )
        )
    ]
    for copy in copies:
        copy.start()
    for slot in range(2):
        for dy in range(3):
            kernel = spatial_weight.at[slot, dy]
            spatial_pairs[slot, dy, :, 0:C] = kernel[C : 3 * C, :]
            spatial_pairs[slot, dy, :, SECOND : SECOND + C] = kernel[0 : 2 * C, :]
        for frame, lanes in enumerate((slice(0, C), slice(SECOND, SECOND + C))):
            for other in range(2):
                tap = temporal_weight.at[slot, 1 - frame + other]
                temporal_pairs[slot, other * SECOND : other * SECOND + C, lanes] = tap[...]
                temporal_pairs[slot, other * SECOND + C : (other + 1) * SECOND, lanes] = tap[0:PAD, :]
    for copy in copies:
        copy.wait()
    segment = lax.axis_index("segment")
    info[...] = jnp.full(info.shape, bounds[segment + 1] - bounds[segment], jnp.int32)
    gain_pairs[...] = jnp.concatenate([gains[...], gains[...]], axis=1)
    entries = time_weight.shape[1]
    half = entries // 2
    at = lax.broadcasted_iota(jnp.int32, (8, entries), 1)
    step = lax.broadcasted_iota(jnp.int32, (8, entries), 0)
    times = jnp.zeros((8, entries), jnp.int32)
    for s in range(STEPS):
        times = jnp.where(step == s, timesteps[s], times)
    angle = times.astype(jnp.float32) * frequency[...]
    emb = jnp.where(at < half, jnp.cos(angle), jnp.sin(angle))
    for slot in range(2):
        made = jnp.dot(
            emb,
            time_weight[slot],
            precision=lax.Precision.HIGHEST,
            preferred_element_type=jnp.float32,
        )
        for s in range(STEPS):
            bias[s, slot : slot + 1, :] = made[s : s + 1]


def place():
    row_group = lax.axis_index("rows")
    at_end = (row_group == 0) | (row_group == lax.axis_size("rows") - 1)
    return lax.rem(row_group, 2), at_end


def first_kernel(step, info, own, far, gains, sw, sp, part, n_own, n_far, wide, thin):
    count = jnp.max(info[0:1, :])
    odd, at_end = place()
    mine, by_far = load(own), load(far)
    if step == 0:
        mine, by_far = flip_if(odd, mine), flip_if(1 - odd, by_far)
    by_far = jnp.where(at_end, 0.0, by_far)
    gain = gains[0:1, :].reshape(1, 1, PAIR)
    normed, far_normed = normalise(mine, gain), normalise(by_far, gain)
    n_own[...] = normed
    n_far[...] = far_normed

    @pl.when(count > 1)
    def _():
        put_wide(wide, 0, flip(far_normed), normed)
        even, odd_sum = spatial(wide, True, (0,), sw, sp, 0, odd)
        part[0], part[1] = even, odd_sum

    @pl.when(count == 1)
    def _():
        put_thin(thin, 0, halves(far_normed, flip(normed)))
        put_thin(thin, 1, normed)
        even, odd_sum = spatial(thin, None, (0, 1), sw, sp, 0, odd)
        part[0, : FIELD], part[1, : FIELD] = even, odd_sum


def second_kernel(
    step, info, own, far, core, part, n_own, n_far, bias, gains, sw, sp, tp, out, wide, thin, acc, center
):
    count = jnp.max(info[0:1, :])
    odd, at_end = place()
    mine, by_core = load(own), load(core)
    if step == 0:
        mine, by_core = flip_if(odd, mine), flip_if(1 - odd, by_core)
    core_normed = normalise(by_core, gains[0:1, :].reshape(1, 1, PAIR))

    @pl.when(count == 1)
    def _():
        put_thin(thin, 2, halves(flip(n_own[...]), core_normed))
        even, odd_sum = spatial(thin, None, (2,), sw, sp, 0, odd)
        acc[0], acc[1] = part[0, :FIELD] + even, part[1, :FIELD] + odd_sum
        center[...] = mine

    @pl.when(count > 1)
    def _():
        normed = n_own[...]
        turned = flip(normed)
        put_wide(wide, 1, halves(n_far[...], turned), halves(turned, core_normed))
        put_wide(wide, 2, normed, flip(core_normed))
        even, odd_sum = spatial(wide, True, (1, 2), sw, sp, 0, odd)
        even = part[0] + even + bias[step, 0:1, :]
        odd_sum = part[1] + odd_sum + bias[step, 0:1, :]
        half = FIELD
        u_even, u_odd = silu(even).astype(jnp.bfloat16), silu(odd_sum).astype(jnp.bfloat16)
        u0 = jnp.concatenate([u_even[:half], u_odd[:half]], axis=0)
        u1 = jnp.concatenate([u_even[half:], u_odd[half:]], axis=0)
        v0, v1 = temporal(u0, u1, tp, 0)
        v_even = jnp.concatenate([v0[:half], v1[:half]], axis=0)
        v_odd = jnp.concatenate([v0[half:], v1[half:]], axis=0)
        change = jnp.concatenate([even + v_even, odd_sum + v_odd], axis=1)
        change = change.reshape(FRAMES * J, 2 * GROUP, PAIR)
        by_far = load(far)
        if step == 0:
            by_far = flip_if(1 - odd, by_far)
        back = flip(mine)
        first = halves(by_far, back) + change[:, :GROUP]
        second = halves(back, by_core) + change[:, GROUP:]
        first = first.astype(jnp.bfloat16).astype(jnp.float32)
        second = second.astype(jnp.bfloat16).astype(jnp.float32)
        row = lax.broadcasted_iota(jnp.int32, first.shape, 1)
        first = jnp.where((row < HB) & at_end, 0.0, first)
        center[...] = halves(flip(first), flip(second))
        gain = gains[1:2, :].reshape(1, 1, PAIR)
        n_first, n_second = normalise(first, gain), normalise(second, gain)
        put_thin(thin, 0, n_first)
        put_thin(thin, 1, halves(flip(n_first), flip(n_second)))
        put_thin(thin, 2, n_second)
        even, odd_sum = spatial(thin, None, (0, 1, 2), sw, sp, 1, odd)
        acc[0], acc[1] = even, odd_sum

    last = count - 1
    shift = bias[step, pl.ds(last, 1), :]
    even = (acc[0] + shift).reshape(J, FRAMES, GROUP, C)
    odd_sum = (acc[1] + shift).reshape(J, FRAMES, GROUP, C)
    u0, u1 = (
        jnp.concatenate(
            [silu(even[:, f]).reshape(-1, C), silu(odd_sum[:, f]).reshape(-1, C)], axis=0
        )
        for f in range(FRAMES)
    )
    v0, v1 = temporal(u0.astype(jnp.bfloat16), u1.astype(jnp.bfloat16), tp, last)
    half = J * GROUP
    for f, v in enumerate((v0, v1)):
        a_even, a_odd = even[:, f].reshape(half, C), odd_sum[:, f].reshape(half, C)
        change = jnp.concatenate([a_even + v[:half], a_odd + v[half:]], axis=1)
        result = center[f * J : (f + 1) * J] + change.reshape(J, GROUP, PAIR)
        if step == STEPS - 1:
            result = flip_if(odd, result)
        out[f * half : (f + 1) * half, :] = result.reshape(half, PAIR).astype(jnp.bfloat16)


VMEM = pl.BlockSpec(memory_space=pltpu.VMEM)


def call(kernel, name, outs, scratch, flops):
    return pl.pallas_call(
        kernel,
        out_shape=tuple(jax.ShapeDtypeStruct(shape, dtype) for shape, dtype in outs),
        out_specs=(VMEM,) * len(outs),
        scratch_shapes=[pltpu.VMEM(shape, dtype) for shape, dtype in scratch],
        compiler_params=pltpu.CompilerParams(vmem_limit_bytes=24 * 1024 * 1024),
        cost_estimate=pl.CostEstimate(
            flops=flops, bytes_accessed=flops // 4_000, transcendentals=0
        ),
        name=name,
    )


def prepare(bounds, timesteps, gains, time_weight, spatial_weight, temporal_weight):
    hbm = pl.BlockSpec(memory_space=pltpu.HBM)
    (frequency,) = call(
        frequency_kernel, "frequency", [((8, time_weight.shape[1]), jnp.float32)], [], 4_000_000_000
    )()
    return pl.pallas_call(
        prepare_kernel,
        out_shape=(
            jax.ShapeDtypeStruct((8, 128), jnp.int32),
            jax.ShapeDtypeStruct((STEPS, 2, C), jnp.float32),
            jax.ShapeDtypeStruct((2, PAIR), jnp.float32),
            jax.ShapeDtypeStruct((2, 3, 2 * C, SECOND + C), jnp.bfloat16),
            jax.ShapeDtypeStruct((2, 2 * SECOND, SECOND + C), jnp.bfloat16),
        ),
        in_specs=[hbm, hbm, hbm, hbm, VMEM, VMEM, VMEM],
        out_specs=(VMEM,) * 5,
        scratch_shapes=[
            pltpu.SMEM(bounds.shape, jnp.int32),
            pltpu.SMEM(timesteps.shape, jnp.int32),
            pltpu.VMEM(gains.shape, jnp.float32),
            pltpu.VMEM(time_weight.shape, jnp.float32),
            pltpu.SemaphoreType.DMA((4,)),
        ],
        compiler_params=pltpu.CompilerParams(vmem_limit_bytes=24 * 1024 * 1024),
        cost_estimate=pl.CostEstimate(
            flops=8_000_000_000, bytes_accessed=1_000_000, transcendentals=10_000
        ),
        name="prepare",
    )(bounds, timesteps, gains, time_weight, frequency, spatial_weight, temporal_weight)


WIDE = ((3, FRAMES, J + 2, 2 * GROUP, LANES), jnp.bfloat16)
THIN = ((3, J + 2, FRAMES * GROUP, LANES), jnp.bfloat16)
ROWS_F32 = ((FRAMES * J, GROUP, PAIR), jnp.float32)


def apply_blocks(step, info, own, far, core, bias, gains, sw, sp, tp):
    part, n_own, n_far = call(
        functools.partial(first_kernel, step),
        "own_and_far_rows",
        [((2, 2 * FIELD, C), jnp.float32), ROWS_F32, ROWS_F32],
        [WIDE, THIN],
        1_000_000,
    )(info, own, far, gains, sw, sp)
    (field,) = call(
        functools.partial(second_kernel, step),
        "residual_blocks",
        [((FIELD, PAIR), jnp.bfloat16)],
        [WIDE, THIN, ((2, FIELD, C), jnp.float32), ROWS_F32],
        4_000_000_000,
    )(info, own, far, core, part, n_own, n_far, bias, gains, sw, sp, tp)
    return field


def body(state, bounds, timesteps, gains, spatial_weight, temporal_weight, time_weight):
    groups = lax.axis_size("rows")
    segments = lax.axis_size("segment")
    sw = spatial_weight.reshape(2, 3, 3 * C, C)
    tw = temporal_weight.reshape(2, 3, C, C)
    made = prepare(bounds, timesteps, gains[0], time_weight[0], sw, tw)
    ahead = [(i, (i + 1) % segments) for i in range(segments)]
    on_chip = [(i, i ^ 1) for i in range(groups)]
    off_chip = [(i, i + 1) for i in range(1, groups - 1, 2)]
    off_chip = off_chip + [(j, i) for i, j in off_chip] + [(0, 0), (groups - 1, groups - 1)]
    off_chip_ahead = [
        (a * groups + i, b * groups + j) for a, b in ahead for i, j in off_chip
    ]

    field = state.reshape(FRAMES, ROWS, HB, J, PAIR).transpose(0, 3, 1, 2, 4).reshape(FIELD, PAIR)
    for step in range(STEPS):
        far = lax.ppermute(field, ("segment", "rows"), off_chip_ahead)
        own = lax.ppermute(field, "segment", ahead)
        if step == 0:
            far, own, made = lax.optimization_barrier((far, own, made))
            info, bias, gain_pairs, sp, tp = made
        core = lax.ppermute(own, "rows", on_chip)
        field = apply_blocks(step, info, own, far, core, bias, gain_pairs, sw, sp, tp)
    field = field.reshape(FRAMES, J, ROWS, HB, PAIR).transpose(0, 2, 3, 1, 4)
    return field.reshape(1, FRAMES, ROWS, W * C)


def solution(mesh):
    placed = (
        P("segment", None, "rows", None),
        P(),
        P(),
        P("segment", None, None),
        P("segment", None, None, None, None, None),
        P("segment", None, None, None, None),
        P("segment", None, None, None),
    )
    return jax.shard_map(
        body,
        mesh=mesh,
        in_specs=placed,
        out_specs=P("segment", None, "rows", None),
        check_vma=False,
    )
```

```python
import functools
import math

import jax
import jax.numpy as jnp
from jax import lax
from jax.experimental import pallas as pl
from jax.experimental.pallas import tpu as pltpu
from jax.sharding import PartitionSpec as P

C = 320
W = 72
STEPS = 2
FRAMES = 2
ROWS = 2

HB = 4
J = W // 2 // HB
PAIR = 2 * C
GROUP = ROWS * HB
FIELD = FRAMES * J * GROUP
PAD = 64
LANES = PAIR + 256
SECOND = C + PAD
EPS = 1e-06


def low_lanes(shape):
    return lax.broadcasted_iota(jnp.int32, shape, len(shape) - 1) < PAD


def normalise(value, gain):
    low = low_lanes(value[..., 256:384].shape)
    square = value * value
    middle = square[..., 256:384]
    first = square[..., 0:128] + square[..., 128:256] + jnp.where(low, middle, 0.0)
    second = square[..., 384:512] + square[..., 512:640] + jnp.where(low, 0.0, middle)
    scale = lax.rsqrt(jnp.sum(first, axis=-1, keepdims=True) / C + EPS)
    other = lax.rsqrt(jnp.sum(second, axis=-1, keepdims=True) / C + EPS)
    scaled = jnp.concatenate(
        [
            value[..., 0:256] * scale,
            value[..., 256:384] * jnp.where(low, scale, other),
            value[..., 384:640] * other,
        ],
        axis=-1,
    )
    return scaled * gain


def load(ref):
    return ref[...].astype(jnp.float32).reshape(FRAMES * J, GROUP, PAIR)


def flip(value):
    return pltpu.roll(value, HB, 1)


def flip_if(odd, value):
    return pltpu.roll(value, HB * odd, 1)


def halves(first, second):
    row = lax.broadcasted_iota(jnp.int32, first.shape, 1)
    return jnp.where(row < HB, first, second)


def shifted_h(value, by):
    rows = value.shape[0]
    moved = pltpu.roll(value, by % rows, 0)
    h = lax.rem(lax.broadcasted_iota(jnp.int32, value.shape, 0), HB)
    edge = 0 if by == 1 else HB - 1
    return jnp.where(h == edge, 0.0, moved)


def put(ref, at, value):
    middle = value[..., 256:384]
    low = low_lanes(middle.shape)
    ref[at + (slice(None), slice(0, PAIR))] = value.astype(jnp.bfloat16)
    ref[at + (slice(None), slice(PAIR, PAIR + 128))] = jnp.where(low, 0.0, middle).astype(
        jnp.bfloat16
    )
    ref[at + (slice(None), slice(PAIR + 128, LANES))] = jnp.where(low, middle, 0.0).astype(
        jnp.bfloat16
    )


def put_wide(ref, dy, first, second):
    tiles = jnp.concatenate([first, second], axis=1).reshape(FRAMES, J, 2 * GROUP, PAIR)
    put(ref, (dy, slice(None), slice(1, J + 1)), tiles)
    for f in range(FRAMES):
        put(ref, (dy, f, 0), shifted_h(tiles[f, J - 1], 1))
        put(ref, (dy, f, J + 1), shifted_h(tiles[f, 0], -1))


def put_thin(ref, dy, value):
    tiles = value.reshape(FRAMES, J, GROUP, PAIR)
    tiles = jnp.concatenate([tiles[0], tiles[1]], axis=1)
    put(ref, (dy, slice(1, J + 1)), tiles)
    put(ref, (dy, 0), shifted_h(tiles[J - 1], 1))
    put(ref, (dy, J + 1), shifted_h(tiles[0], -1))


def rows_of(ref, dy, j0, wide, start, stop):
    if wide:
        return ref[dy, :, j0 : j0 + J, :, start:stop].reshape(-1, stop - start)
    return ref[dy, j0 : j0 + J, :, start:stop].reshape(-1, stop - start)


def silu(value):
    half = 0.5 * value
    return half + half * jnp.tanh(half)


def dot(a, b):
    return jnp.dot(a, b, preferred_element_type=jnp.float32)


def spatial(ref, wide, taps, weights, pairs, slot, odd):
    center, before, after, joint, left, right = [], [], [], [], [], []
    for dy in taps:
        at = dy + odd * (2 - 2 * dy)
        rows = functools.partial(rows_of, ref, dy, wide=wide)
        center.append(rows(1, start=0, stop=PAIR))
        before += [rows(0, start=PAIR, stop=PAIR + 128), rows(0, start=384, stop=PAIR)]
        after += [rows(2, start=0, stop=256), rows(2, start=PAIR + 128, stop=LANES)]
        filler = weights[slot, at, 0:PAD, :]
        joint.append(pairs[slot, at])
        left += [filler, weights[slot, at, 0:C, :]]
        right += [weights[slot, at, 2 * C :, :], filler]
    both = dot(jnp.concatenate(center, axis=1), jnp.concatenate(joint, axis=0))
    even_sum = dot(jnp.concatenate(before, axis=1), jnp.concatenate(left, axis=0))
    odd_sum = dot(jnp.concatenate(after, axis=1), jnp.concatenate(right, axis=0))
    return both[:, :C] + even_sum, both[:, SECOND:] + odd_sum


def temporal(u0, u1, pairs, slot):
    gap = jnp.zeros((u0.shape[0], PAD), u0.dtype)
    both = dot(jnp.concatenate([u0, gap, u1, gap], axis=1), pairs[slot])
    return both[:, :C], both[:, SECOND:]


def frequency_kernel(out):
    half = out.shape[1] // 2
    at = lax.broadcasted_iota(jnp.int32, out.shape, 1)
    index = jnp.where(at < half, at, at - half).astype(jnp.float32)
    out[...] = jnp.exp(-math.log(10000.0) * index / half)


def prepare_kernel(
    bounds_hbm,
    timesteps_hbm,
    gains_hbm,
    time_hbm,
    frequency,
    spatial_weight,
    temporal_weight,
    info,
    bias,
    gain_pairs,
    spatial_pairs,
    temporal_pairs,
    bounds,
    timesteps,
    gains,
    time_weight,
    sems,
):
    copies = [
        pltpu.make_async_copy(source, target, sems.at[n])
        for n, (source, target) in enumerate(
            (
                (bounds_hbm, bounds),
                (timesteps_hbm, timesteps),
                (gains_hbm, gains),
                (time_hbm, time_weight),
            )
        )
    ]
    for copy in copies:
        copy.start()
    for slot in range(2):
        for dy in range(3):
            kernel = spatial_weight.at[slot, dy]
            spatial_pairs[slot, dy, :, 0:C] = kernel[C : 3 * C, :]
            spatial_pairs[slot, dy, :, SECOND : SECOND + C] = kernel[0 : 2 * C, :]
        for frame, lanes in enumerate((slice(0, C), slice(SECOND, SECOND + C))):
            for other in range(2):
                tap = temporal_weight.at[slot, 1 - frame + other]
                temporal_pairs[slot, other * SECOND : other * SECOND + C, lanes] = tap[...]
                temporal_pairs[slot, other * SECOND + C : (other + 1) * SECOND, lanes] = tap[0:PAD, :]
    for copy in copies:
        copy.wait()
    segment = lax.axis_index("segment")
    info[...] = jnp.full(info.shape, bounds[segment + 1] - bounds[segment], jnp.int32)
    gain_pairs[...] = jnp.concatenate([gains[...], gains[...]], axis=1)
    entries = time_weight.shape[1]
    half = entries // 2
    at = lax.broadcasted_iota(jnp.int32, (8, entries), 1)
    step = lax.broadcasted_iota(jnp.int32, (8, entries), 0)
    times = jnp.zeros((8, entries), jnp.int32)
    for s in range(STEPS):
        times = jnp.where(step == s, timesteps[s], times)
    angle = times.astype(jnp.float32) * frequency[...]
    emb = jnp.where(at < half, jnp.cos(angle), jnp.sin(angle))
    for slot in range(2):
        made = jnp.dot(
            emb,
            time_weight[slot],
            precision=lax.Precision.HIGHEST,
            preferred_element_type=jnp.float32,
        )
        for s in range(STEPS):
            bias[s, slot : slot + 1, :] = made[s : s + 1]


def place():
    row_group = lax.axis_index("rows")
    at_end = (row_group == 0) | (row_group == lax.axis_size("rows") - 1)
    return lax.rem(row_group, 2), at_end


def side_of(step):
    return "core" if step == 0 else "far"


def load_far(step, ref):
    odd, at_end = place()
    value = load(ref)
    if step == 0:
        value = flip_if(1 - odd, value)
    return jnp.where(at_end, 0.0, value)


def lay_out(refs, scratch, tiles, turn):
    frames = [ref.at[0, f] for ref in refs for f in range(ref.shape[1])]
    for f in range(FRAMES):
        for j in range(J):
            for h in range(HB):
                at = (h * J + j) * PAIR
                rows = frames[f][:, at : at + PAIR].astype(jnp.float32)
                for n in range(PAIR // 128):
                    scratch[f * J + j, n, pl.ds(h, ROWS, stride=HB), :] = rows[
                        :, n * 128 : (n + 1) * 128
                    ]
    value = jnp.concatenate([scratch[:, n] for n in range(PAIR // 128)], axis=-1)
    tiles[...] = flip_if(turn, value)


def first_kernel(step, info, own, *refs):
    count = jnp.max(info[0:1, :])
    odd, _ = place()
    core_side = side_of(step) == "core"
    sides, refs = refs[: FRAMES - step], refs[FRAMES - step :]
    gains, sw, sp, part, n_own, n_side = refs[:6]
    tiles, (wide, thin, scratch) = refs[6:-3], refs[-3:]
    if step == 0:
        lay_out([own], scratch, tiles[0], odd)
        lay_out(sides, scratch, tiles[1], 1 - odd)
        mine, theirs = tiles[0][...], tiles[1][...]
    else:
        mine, theirs = load(own), load_far(step, sides[0])
    gain = gains[0:1, :].reshape(1, 1, PAIR)
    normed, side_normed = normalise(mine, gain), normalise(theirs, gain)
    n_own[...] = normed
    n_side[...] = side_normed

    @pl.when(count > 1)
    def _():
        if core_side:
            put_wide(wide, 2, normed, flip(side_normed))
        else:
            put_wide(wide, 0, flip(side_normed), normed)
        even, odd_sum = spatial(wide, True, (2 if core_side else 0,), sw, sp, 0, odd)
        part[0], part[1] = even, odd_sum

    @pl.when(count == 1)
    def _():
        put_thin(thin, 1, normed)
        if core_side:
            put_thin(thin, 2, halves(flip(normed), side_normed))
        else:
            put_thin(thin, 0, halves(side_normed, flip(normed)))
        even, odd_sum = spatial(thin, False, (1, 2) if core_side else (0, 1), sw, sp, 0, odd)
        part[0, :FIELD], part[1, :FIELD] = even, odd_sum


def second_kernel(
    step, info, own, far, core, part, n_own, n_side, bias, gains, sw, sp, tp, out, wide, thin, acc, center
):
    count = jnp.max(info[0:1, :])
    odd, at_end = place()
    far_last = side_of(step) == "core"
    mine = own[...] if step == 0 else load(own)
    theirs = load_far(step, far) if far_last else load(core)
    last_normed = normalise(theirs, gains[0:1, :].reshape(1, 1, PAIR))

    @pl.when(count == 1)
    def _():
        if far_last:
            put_thin(thin, 0, halves(last_normed, flip(n_own[...])))
        else:
            put_thin(thin, 2, halves(flip(n_own[...]), last_normed))
        even, odd_sum = spatial(thin, False, (0 if far_last else 2,), sw, sp, 0, odd)
        acc[0], acc[1] = part[0, :FIELD] + even, part[1, :FIELD] + odd_sum
        center[...] = mine

    @pl.when(count > 1)
    def _():
        normed = n_own[...]
        turned = flip(normed)
        if far_last:
            far_normed, core_normed = last_normed, n_side[...]
            put_wide(wide, 0, flip(far_normed), normed)
        else:
            far_normed, core_normed = n_side[...], last_normed
            put_wide(wide, 2, normed, flip(core_normed))
        put_wide(wide, 1, halves(far_normed, turned), halves(turned, core_normed))
        even, odd_sum = spatial(wide, True, (0, 1) if far_last else (1, 2), sw, sp, 0, odd)
        by_far = theirs if far_last else load_far(step, far)
        by_core = core[...] if far_last else theirs
        even = part[0] + even + bias[step, 0:1, :]
        odd_sum = part[1] + odd_sum + bias[step, 0:1, :]
        half = FIELD
        u_even, u_odd = silu(even).astype(jnp.bfloat16), silu(odd_sum).astype(jnp.bfloat16)
        u0 = jnp.concatenate([u_even[:half], u_odd[:half]], axis=0)
        u1 = jnp.concatenate([u_even[half:], u_odd[half:]], axis=0)
        v0, v1 = temporal(u0, u1, tp, 0)
        v_even = jnp.concatenate([v0[:half], v1[:half]], axis=0)
        v_odd = jnp.concatenate([v0[half:], v1[half:]], axis=0)
        change = jnp.concatenate([even + v_even, odd_sum + v_odd], axis=1)
        change = change.reshape(FRAMES * J, 2 * GROUP, PAIR)
        back = flip(mine)
        first = halves(by_far, back) + change[:, :GROUP]
        second = halves(back, by_core) + change[:, GROUP:]
        first = first.astype(jnp.bfloat16).astype(jnp.float32)
        second = second.astype(jnp.bfloat16).astype(jnp.float32)
        row = lax.broadcasted_iota(jnp.int32, first.shape, 1)
        first = jnp.where((row < HB) & at_end, 0.0, first)
        center[...] = halves(flip(first), flip(second))
        gain = gains[1:2, :].reshape(1, 1, PAIR)
        n_first, n_second = normalise(first, gain), normalise(second, gain)
        put_thin(thin, 0, n_first)
        put_thin(thin, 1, halves(flip(n_first), flip(n_second)))
        put_thin(thin, 2, n_second)
        even, odd_sum = spatial(thin, False, (0, 1, 2), sw, sp, 1, odd)
        acc[0], acc[1] = even, odd_sum

    last = count - 1
    shift = bias[step, pl.ds(last, 1), :]
    even = (acc[0] + shift).reshape(J, FRAMES, GROUP, C)
    odd_sum = (acc[1] + shift).reshape(J, FRAMES, GROUP, C)
    u0, u1 = (
        jnp.concatenate(
            [silu(even[:, f]).reshape(-1, C), silu(odd_sum[:, f]).reshape(-1, C)], axis=0
        )
        for f in range(FRAMES)
    )
    v0, v1 = temporal(u0.astype(jnp.bfloat16), u1.astype(jnp.bfloat16), tp, last)
    half = J * GROUP
    for f, v in enumerate((v0, v1)):
        a_even, a_odd = even[:, f].reshape(half, C), odd_sum[:, f].reshape(half, C)
        change = jnp.concatenate([a_even + v[:half], a_odd + v[half:]], axis=1)
        result = center[f * J : (f + 1) * J] + change.reshape(J, GROUP, PAIR)
        if step == STEPS - 1:
            result = flip_if(odd, result)
        out[f * half : (f + 1) * half, :] = result.reshape(half, PAIR).astype(jnp.bfloat16)


VMEM = pl.BlockSpec(memory_space=pltpu.VMEM)


def call(kernel, name, outs, scratch, flops):
    return pl.pallas_call(
        kernel,
        out_shape=tuple(jax.ShapeDtypeStruct(shape, dtype) for shape, dtype in outs),
        out_specs=(VMEM,) * len(outs),
        scratch_shapes=[pltpu.VMEM(shape, dtype) for shape, dtype in scratch],
        compiler_params=pltpu.CompilerParams(vmem_limit_bytes=24 * 1024 * 1024),
        cost_estimate=pl.CostEstimate(
            flops=flops, bytes_accessed=flops // 4_000, transcendentals=0
        ),
        name=name,
    )


def prepare(bounds, timesteps, gains, time_weight, spatial_weight, temporal_weight):
    hbm = pl.BlockSpec(memory_space=pltpu.HBM)
    (frequency,) = call(
        frequency_kernel, "frequency", [((8, time_weight.shape[1]), jnp.float32)], [], 4_000_000_000
    )()
    return pl.pallas_call(
        prepare_kernel,
        out_shape=(
            jax.ShapeDtypeStruct((8, 128), jnp.int32),
            jax.ShapeDtypeStruct((STEPS, 2, C), jnp.float32),
            jax.ShapeDtypeStruct((2, PAIR), jnp.float32),
            jax.ShapeDtypeStruct((2, 3, 2 * C, SECOND + C), jnp.bfloat16),
            jax.ShapeDtypeStruct((2, 2 * SECOND, SECOND + C), jnp.bfloat16),
        ),
        in_specs=[hbm, hbm, hbm, hbm, VMEM, VMEM, VMEM],
        out_specs=(VMEM,) * 5,
        scratch_shapes=[
            pltpu.SMEM(bounds.shape, jnp.int32),
            pltpu.SMEM(timesteps.shape, jnp.int32),
            pltpu.VMEM(gains.shape, jnp.float32),
            pltpu.VMEM(time_weight.shape, jnp.float32),
            pltpu.SemaphoreType.DMA((4,)),
        ],
        compiler_params=pltpu.CompilerParams(vmem_limit_bytes=24 * 1024 * 1024),
        cost_estimate=pl.CostEstimate(
            flops=8_000_000_000, bytes_accessed=1_000_000, transcendentals=10_000
        ),
        name="prepare",
    )(bounds, timesteps, gains, time_weight, frequency, spatial_weight, temporal_weight)


WIDE = ((3, FRAMES, J + 2, 2 * GROUP, LANES), jnp.bfloat16)
THIN = ((3, J + 2, FRAMES * GROUP, LANES), jnp.bfloat16)
ROWS_F32 = ((FRAMES * J, GROUP, PAIR), jnp.float32)


def apply_blocks(step, info, own, far, core, bias, gains, sw, sp, tp):
    sides = core if side_of(step) == "core" else [far]
    part, n_own, n_side, *tiles = call(
        functools.partial(first_kernel, step),
        "own_and_" + side_of(step) + "_rows",
        [((2, 2 * FIELD, C), jnp.float32)] + [ROWS_F32] * (4 if step == 0 else 2),
        [WIDE, THIN, ((FRAMES * J, PAIR // 128, GROUP, 128), jnp.float32)],
        1_000_000,
    )(info, own, *sides, gains, sw, sp)
    if step == 0:
        own, core = tiles
    (field,) = call(
        functools.partial(second_kernel, step),
        "residual_blocks",
        [((FIELD, PAIR), jnp.bfloat16)],
        [WIDE, THIN, ((2, FIELD, C), jnp.float32), ROWS_F32],
        4_000_000_000,
    )(info, own, far, core, part, n_own, n_side, bias, gains, sw, sp, tp)
    return field


def body(state, bounds, timesteps, gains, spatial_weight, temporal_weight, time_weight):
    groups = lax.axis_size("rows")
    segments = lax.axis_size("segment")
    ahead = [(i, (i + 1) % segments) for i in range(segments)]
    on_chip = [(i, i ^ 1) for i in range(groups)]
    off_chip = [(i, i + 1) for i in range(1, groups - 1, 2)]
    off_chip = off_chip + [(j, i) for i, j in off_chip] + [(0, 0), (groups - 1, groups - 1)]
    off_chip_ahead = [
        (a * groups + i, b * groups + j) for a, b in ahead for i, j in off_chip
    ]

    def tiled(value):
        value = value.reshape(FRAMES, ROWS, HB, J, PAIR).transpose(0, 3, 1, 2, 4)
        return value.reshape(FIELD, PAIR)

    field, gains = lax.optimization_barrier((tiled(state), gains))
    far = lax.ppermute(field, ("segment", "rows"), off_chip_ahead)
    own = lax.ppermute(state, "segment", ahead)
    sw = spatial_weight.reshape(2, 3, 3 * C, C)
    tw = temporal_weight.reshape(2, 3, C, C)
    made = prepare(bounds, timesteps, gains[0], time_weight[0], sw, tw)
    own, made = lax.optimization_barrier((own, made))
    info, bias, gain_pairs, sp, tp = made
    core = [lax.ppermute(own[:, f : f + 1], "rows", on_chip) for f in range(FRAMES)]
    field = apply_blocks(
        0, info, own, far, core, bias, gain_pairs, sw, sp, tp
    )
    for step in range(1, STEPS):
        far = lax.ppermute(field, ("segment", "rows"), off_chip_ahead)
        own = lax.ppermute(field, "segment", ahead)
        core = lax.ppermute(own, "rows", on_chip)
        field = apply_blocks(step, info, own, far, core, bias, gain_pairs, sw, sp, tp)
    field = field.reshape(FRAMES, J, ROWS, HB, PAIR).transpose(0, 2, 3, 1, 4)
    return field.reshape(1, FRAMES, ROWS, W * C)


def solution(mesh):
    placed = (
        P("segment", None, "rows", None),
        P(),
        P(),
        P("segment", None, None),
        P("segment", None, None, None, None, None),
        P("segment", None, None, None, None),
        P("segment", None, None, None),
    )
    return jax.shard_map(
        body,
        mesh=mesh,
        in_specs=placed,
        out_specs=P("segment", None, "rows", None),
        check_vma=False,
    )
```

```python
import functools
import math

import jax
import jax.numpy as jnp
from jax import lax
from jax.experimental import pallas as pl
from jax.experimental.pallas import tpu as pltpu
from jax.sharding import PartitionSpec as P

C = 320
W = 72
STEPS = 2
FRAMES = 2
ROWS = 2

HB = 4
J = W // 2 // HB
PAIR = 2 * C
GROUP = ROWS * HB
FIELD = FRAMES * J * GROUP
PAD = 64
LANES = PAIR + 256
SECOND = C + PAD
EPS = 1e-06


def low_lanes(shape):
    return lax.broadcasted_iota(jnp.int32, shape, len(shape) - 1) < PAD


def normalise(value, gain):
    low = low_lanes(value[..., 256:384].shape)
    square = value * value
    middle = square[..., 256:384]
    first = square[..., 0:128] + square[..., 128:256] + jnp.where(low, middle, 0.0)
    second = square[..., 384:512] + square[..., 512:640] + jnp.where(low, 0.0, middle)
    scale = lax.rsqrt(jnp.sum(first, axis=-1, keepdims=True) / C + EPS)
    other = lax.rsqrt(jnp.sum(second, axis=-1, keepdims=True) / C + EPS)
    scaled = jnp.concatenate(
        [
            value[..., 0:256] * scale,
            value[..., 256:384] * jnp.where(low, scale, other),
            value[..., 384:640] * other,
        ],
        axis=-1,
    )
    return scaled * gain


def load(ref):
    return ref[...].astype(jnp.float32).reshape(FRAMES * J, GROUP, PAIR)


def flip(value):
    return pltpu.roll(value, HB, 1)


def flip_if(odd, value):
    return pltpu.roll(value, HB * odd, 1)


def halves(first, second):
    row = lax.broadcasted_iota(jnp.int32, first.shape, 1)
    return jnp.where(row < HB, first, second)


def shifted_h(value, by):
    rows = value.shape[0]
    moved = pltpu.roll(value, by % rows, 0)
    h = lax.rem(lax.broadcasted_iota(jnp.int32, value.shape, 0), HB)
    edge = 0 if by == 1 else HB - 1
    return jnp.where(h == edge, 0.0, moved)


def put(ref, at, value):
    middle = value[..., 256:384]
    low = low_lanes(middle.shape)
    ref[at + (slice(None), slice(0, PAIR))] = value.astype(jnp.bfloat16)
    ref[at + (slice(None), slice(PAIR, PAIR + 128))] = jnp.where(low, 0.0, middle).astype(
        jnp.bfloat16
    )
    ref[at + (slice(None), slice(PAIR + 128, LANES))] = jnp.where(low, middle, 0.0).astype(
        jnp.bfloat16
    )


def put_wide(ref, dy, first, second):
    tiles = jnp.concatenate([first, second], axis=1).reshape(FRAMES, J, 2 * GROUP, PAIR)
    put(ref, (dy, slice(None), slice(1, J + 1)), tiles)
    for f in range(FRAMES):
        put(ref, (dy, f, 0), shifted_h(tiles[f, J - 1], 1))
        put(ref, (dy, f, J + 1), shifted_h(tiles[f, 0], -1))


def put_thin(ref, dy, value):
    tiles = value.reshape(FRAMES, J, GROUP, PAIR)
    tiles = jnp.concatenate([tiles[0], tiles[1]], axis=1)
    put(ref, (dy, slice(1, J + 1)), tiles)
    put(ref, (dy, 0), shifted_h(tiles[J - 1], 1))
    put(ref, (dy, J + 1), shifted_h(tiles[0], -1))


def rows_of(ref, dy, j0, wide, start, stop):
    if wide:
        return ref[dy, :, j0 : j0 + J, :, start:stop].reshape(-1, stop - start)
    return ref[dy, j0 : j0 + J, :, start:stop].reshape(-1, stop - start)


def silu(value):
    half = 0.5 * value
    return half + half * jnp.tanh(half)


def dot(a, b):
    return jnp.dot(a, b, preferred_element_type=jnp.float32)


def spatial(ref, wide, taps, weights, pairs, slot, odd):
    center, before, after, joint, left, right = [], [], [], [], [], []
    for dy in taps:
        at = dy + odd * (2 - 2 * dy)
        rows = functools.partial(rows_of, ref, dy, wide=wide)
        center.append(rows(1, start=0, stop=PAIR))
        before += [rows(0, start=PAIR, stop=PAIR + 128), rows(0, start=384, stop=PAIR)]
        after += [rows(2, start=0, stop=256), rows(2, start=PAIR + 128, stop=LANES)]
        filler = weights[slot, at, 0:PAD, :]
        joint.append(pairs[slot, at])
        left += [filler, weights[slot, at, 0:C, :]]
        right += [weights[slot, at, 2 * C :, :], filler]
    both = dot(jnp.concatenate(center, axis=1), jnp.concatenate(joint, axis=0))
    even_sum = dot(jnp.concatenate(before, axis=1), jnp.concatenate(left, axis=0))
    odd_sum = dot(jnp.concatenate(after, axis=1), jnp.concatenate(right, axis=0))
    return both[:, :C] + even_sum, both[:, SECOND:] + odd_sum


def temporal(u0, u1, pairs, slot):
    gap = jnp.zeros((u0.shape[0], PAD), u0.dtype)
    both = dot(jnp.concatenate([u0, gap, u1, gap], axis=1), pairs[slot])
    return both[:, :C], both[:, SECOND:]


def frequency_kernel(out):
    half = out.shape[1] // 2
    at = lax.broadcasted_iota(jnp.int32, out.shape, 1)
    index = jnp.where(at < half, at, at - half).astype(jnp.float32)
    out[...] = jnp.exp(-math.log(10000.0) * index / half)


def prepare_kernel(
    bounds_hbm,
    timesteps_hbm,
    gains_hbm,
    time_hbm,
    frequency,
    spatial_weight,
    temporal_weight,
    info,
    bias,
    gain_pairs,
    spatial_pairs,
    temporal_pairs,
    bounds,
    timesteps,
    gains,
    time_weight,
    sems,
):
    copies = [
        pltpu.make_async_copy(source, target, sems.at[n])
        for n, (source, target) in enumerate(
            (
                (bounds_hbm, bounds),
                (timesteps_hbm, timesteps),
                (gains_hbm, gains),
                (time_hbm, time_weight),
            )
        )
    ]
    for copy in copies:
        copy.start()
    for slot in range(2):
        for dy in range(3):
            kernel = spatial_weight.at[slot, dy]
            spatial_pairs[slot, dy, :, 0:C] = kernel[C : 3 * C, :]
            spatial_pairs[slot, dy, :, SECOND : SECOND + C] = kernel[0 : 2 * C, :]
        for frame, lanes in enumerate((slice(0, C), slice(SECOND, SECOND + C))):
            for other in range(2):
                tap = temporal_weight.at[slot, 1 - frame + other]
                temporal_pairs[slot, other * SECOND : other * SECOND + C, lanes] = tap[...]
                temporal_pairs[slot, other * SECOND + C : (other + 1) * SECOND, lanes] = tap[0:PAD, :]
    for copy in copies:
        copy.wait()
    segment = lax.axis_index("segment")
    info[...] = jnp.full(info.shape, bounds[segment + 1] - bounds[segment], jnp.int32)
    gain_pairs[...] = jnp.concatenate([gains[...], gains[...]], axis=1)
    entries = time_weight.shape[1]
    half = entries // 2
    at = lax.broadcasted_iota(jnp.int32, (8, entries), 1)
    step = lax.broadcasted_iota(jnp.int32, (8, entries), 0)
    times = jnp.zeros((8, entries), jnp.int32)
    for s in range(STEPS):
        times = jnp.where(step == s, timesteps[s], times)
    angle = times.astype(jnp.float32) * frequency[...]
    emb = jnp.where(at < half, jnp.cos(angle), jnp.sin(angle))
    for slot in range(2):
        made = jnp.dot(
            emb,
            time_weight[slot],
            precision=lax.Precision.HIGHEST,
            preferred_element_type=jnp.float32,
        )
        for s in range(STEPS):
            bias[s, slot : slot + 1, :] = made[s : s + 1]


def place():
    row_group = lax.axis_index("rows")
    at_end = (row_group == 0) | (row_group == lax.axis_size("rows") - 1)
    return lax.rem(row_group, 2), at_end


def side_of(step):
    return "core" if step == 0 else "far"


def load_far(step, ref):
    odd, at_end = place()
    value = load(ref)
    if step == 0:
        value = flip_if(1 - odd, value)
    return jnp.where(at_end, 0.0, value)


def lay_out(refs, scratch, tiles, turn):
    frames = [ref.at[0, f] for ref in refs for f in range(ref.shape[1])]
    for f in range(FRAMES):
        for j in range(J):
            for h in range(HB):
                at = (h * J + j) * PAIR
                rows = frames[f][:, at : at + PAIR].astype(jnp.float32)
                for n in range(PAIR // 128):
                    scratch[f * J + j, n, pl.ds(h, ROWS, stride=HB), :] = rows[
                        :, n * 128 : (n + 1) * 128
                    ]
    value = jnp.concatenate([scratch[:, n] for n in range(PAIR // 128)], axis=-1)
    tiles[...] = flip_if(turn, value)


def first_kernel(step, info, own, *refs):
    count = jnp.max(info[0:1, :])
    odd, _ = place()
    core_side = side_of(step) == "core"
    sides, refs = refs[: FRAMES - step], refs[FRAMES - step :]
    gains, sw, sp, part, n_own, n_side = refs[:6]
    tiles, (wide, thin, scratch) = refs[6:-3], refs[-3:]
    if step == 0:
        lay_out([own], scratch, tiles[0], odd)
        lay_out(sides, scratch, tiles[1], 1 - odd)
        mine, theirs = tiles[0][...], tiles[1][...]
    else:
        mine, theirs = load(own), load_far(step, sides[0])
    gain = gains[0:1, :].reshape(1, 1, PAIR)
    normed, side_normed = normalise(mine, gain), normalise(theirs, gain)
    n_own[...] = normed
    n_side[...] = side_normed

    @pl.when(count > 1)
    def _():
        if core_side:
            put_wide(wide, 2, normed, flip(side_normed))
        else:
            put_wide(wide, 0, flip(side_normed), normed)
        even, odd_sum = spatial(wide, True, (2 if core_side else 0,), sw, sp, 0, odd)
        part[0], part[1] = even, odd_sum

    @pl.when(count == 1)
    def _():
        put_thin(thin, 1, normed)
        if core_side:
            put_thin(thin, 2, halves(flip(normed), side_normed))
        else:
            put_thin(thin, 0, halves(side_normed, flip(normed)))
        even, odd_sum = spatial(thin, False, (1, 2) if core_side else (0, 1), sw, sp, 0, odd)
        part[0, :FIELD], part[1, :FIELD] = even, odd_sum


def second_kernel(
    step, info, own, far, core, part, n_own, n_side, bias, gains, sw, sp, tp, out, wide, thin, acc, center
):
    count = jnp.max(info[0:1, :])
    odd, at_end = place()
    far_last = side_of(step) == "core"
    mine = own[...] if step == 0 else load(own)
    theirs = load_far(step, far) if far_last else load(core)
    last_normed = normalise(theirs, gains[0:1, :].reshape(1, 1, PAIR))

    @pl.when(count == 1)
    def _():
        if far_last:
            put_thin(thin, 0, halves(last_normed, flip(n_own[...])))
        else:
            put_thin(thin, 2, halves(flip(n_own[...]), last_normed))
        even, odd_sum = spatial(thin, False, (0 if far_last else 2,), sw, sp, 0, odd)
        acc[0], acc[1] = part[0, :FIELD] + even, part[1, :FIELD] + odd_sum
        center[...] = mine

    @pl.when(count > 1)
    def _():
        normed = n_own[...]
        turned = flip(normed)
        if far_last:
            far_normed, core_normed = last_normed, n_side[...]
            put_wide(wide, 0, flip(far_normed), normed)
        else:
            far_normed, core_normed = n_side[...], last_normed
            put_wide(wide, 2, normed, flip(core_normed))
        put_wide(wide, 1, halves(far_normed, turned), halves(turned, core_normed))
        even, odd_sum = spatial(wide, True, (0, 1) if far_last else (1, 2), sw, sp, 0, odd)
        by_far = theirs if far_last else load_far(step, far)
        by_core = core[...] if far_last else theirs
        even = part[0] + even + bias[step, 0:1, :]
        odd_sum = part[1] + odd_sum + bias[step, 0:1, :]
        half = FIELD
        u_even, u_odd = silu(even).astype(jnp.bfloat16), silu(odd_sum).astype(jnp.bfloat16)
        u0 = jnp.concatenate([u_even[:half], u_odd[:half]], axis=0)
        u1 = jnp.concatenate([u_even[half:], u_odd[half:]], axis=0)
        v0, v1 = temporal(u0, u1, tp, 0)
        v_even = jnp.concatenate([v0[:half], v1[:half]], axis=0)
        v_odd = jnp.concatenate([v0[half:], v1[half:]], axis=0)
        change = jnp.concatenate([even + v_even, odd_sum + v_odd], axis=1)
        change = change.reshape(FRAMES * J, 2 * GROUP, PAIR)
        back = flip(mine)
        first = halves(by_far, back) + change[:, :GROUP]
        second = halves(back, by_core) + change[:, GROUP:]
        first = first.astype(jnp.bfloat16).astype(jnp.float32)
        second = second.astype(jnp.bfloat16).astype(jnp.float32)
        row = lax.broadcasted_iota(jnp.int32, first.shape, 1)
        first = jnp.where((row < HB) & at_end, 0.0, first)
        center[...] = halves(flip(first), flip(second))
        gain = gains[1:2, :].reshape(1, 1, PAIR)
        n_first, n_second = normalise(first, gain), normalise(second, gain)
        put_thin(thin, 0, n_first)
        put_thin(thin, 1, halves(flip(n_first), flip(n_second)))
        put_thin(thin, 2, n_second)
        even, odd_sum = spatial(thin, False, (0, 1, 2), sw, sp, 1, odd)
        acc[0], acc[1] = even, odd_sum

    last = count - 1
    shift = bias[step, pl.ds(last, 1), :]
    even = (acc[0] + shift).reshape(J, FRAMES, GROUP, C)
    odd_sum = (acc[1] + shift).reshape(J, FRAMES, GROUP, C)
    u0, u1 = (
        jnp.concatenate(
            [silu(even[:, f]).reshape(-1, C), silu(odd_sum[:, f]).reshape(-1, C)], axis=0
        )
        for f in range(FRAMES)
    )
    v0, v1 = temporal(u0.astype(jnp.bfloat16), u1.astype(jnp.bfloat16), tp, last)
    half = J * GROUP
    for f, v in enumerate((v0, v1)):
        a_even, a_odd = even[:, f].reshape(half, C), odd_sum[:, f].reshape(half, C)
        change = jnp.concatenate([a_even + v[:half], a_odd + v[half:]], axis=1)
        result = center[f * J : (f + 1) * J] + change.reshape(J, GROUP, PAIR)
        if step == STEPS - 1:
            result = flip_if(odd, result)
        out[f * half : (f + 1) * half, :] = result.reshape(half, PAIR).astype(jnp.bfloat16)


VMEM = pl.BlockSpec(memory_space=pltpu.VMEM)


def call(kernel, name, outs, scratch, flops):
    return pl.pallas_call(
        kernel,
        out_shape=tuple(jax.ShapeDtypeStruct(shape, dtype) for shape, dtype in outs),
        out_specs=(VMEM,) * len(outs),
        scratch_shapes=[pltpu.VMEM(shape, dtype) for shape, dtype in scratch],
        compiler_params=pltpu.CompilerParams(vmem_limit_bytes=24 * 1024 * 1024),
        cost_estimate=pl.CostEstimate(
            flops=flops, bytes_accessed=flops // 4_000, transcendentals=0
        ),
        name=name,
    )


def prepare(bounds, timesteps, gains, time_weight, spatial_weight, temporal_weight):
    hbm = pl.BlockSpec(memory_space=pltpu.HBM)
    (frequency,) = call(
        frequency_kernel, "frequency", [((8, time_weight.shape[1]), jnp.float32)], [], 4_000_000_000
    )()
    return pl.pallas_call(
        prepare_kernel,
        out_shape=(
            jax.ShapeDtypeStruct((8, 128), jnp.int32),
            jax.ShapeDtypeStruct((STEPS, 2, C), jnp.float32),
            jax.ShapeDtypeStruct((2, PAIR), jnp.float32),
            jax.ShapeDtypeStruct((2, 3, 2 * C, SECOND + C), jnp.bfloat16),
            jax.ShapeDtypeStruct((2, 2 * SECOND, SECOND + C), jnp.bfloat16),
        ),
        in_specs=[hbm, hbm, hbm, hbm, VMEM, VMEM, VMEM],
        out_specs=(VMEM,) * 5,
        scratch_shapes=[
            pltpu.SMEM(bounds.shape, jnp.int32),
            pltpu.SMEM(timesteps.shape, jnp.int32),
            pltpu.VMEM(gains.shape, jnp.float32),
            pltpu.VMEM(time_weight.shape, jnp.float32),
            pltpu.SemaphoreType.DMA((4,)),
        ],
        compiler_params=pltpu.CompilerParams(vmem_limit_bytes=24 * 1024 * 1024),
        cost_estimate=pl.CostEstimate(
            flops=8_000_000_000, bytes_accessed=1_000_000, transcendentals=10_000
        ),
        name="prepare",
    )(bounds, timesteps, gains, time_weight, frequency, spatial_weight, temporal_weight)


WIDE = ((3, FRAMES, J + 2, 2 * GROUP, LANES), jnp.bfloat16)
THIN = ((3, J + 2, FRAMES * GROUP, LANES), jnp.bfloat16)
ROWS_F32 = ((FRAMES * J, GROUP, PAIR), jnp.float32)


def apply_blocks(step, info, own, far, core, bias, gains, sw, sp, tp):
    sides = core if side_of(step) == "core" else [far]
    part, n_own, n_side, *tiles = call(
        functools.partial(first_kernel, step),
        "own_and_" + side_of(step) + "_rows",
        [((2, 2 * FIELD, C), jnp.float32)] + [ROWS_F32] * (4 if step == 0 else 2),
        [WIDE, THIN, ((FRAMES * J, PAIR // 128, GROUP, 128), jnp.float32)],
        1_000_000,
    )(info, own, *sides, gains, sw, sp)
    if step == 0:
        own, core = tiles
    (field,) = call(
        functools.partial(second_kernel, step),
        "residual_blocks",
        [((FIELD, PAIR), jnp.bfloat16)],
        [WIDE, THIN, ((2, FIELD, C), jnp.float32), ROWS_F32],
        4_000_000_000,
    )(info, own, far, core, part, n_own, n_side, bias, gains, sw, sp, tp)
    return field


def body(state, bounds, timesteps, gains, spatial_weight, temporal_weight, time_weight):
    groups = lax.axis_size("rows")
    segments = lax.axis_size("segment")
    ahead = [(i, (i + 1) % segments) for i in range(segments)]
    on_chip = [(i, i ^ 1) for i in range(groups)]
    off_chip = [(i, i + 1) for i in range(1, groups - 1, 2)]
    off_chip = off_chip + [(j, i) for i, j in off_chip] + [(0, 0), (groups - 1, groups - 1)]
    off_chip_ahead = [
        (a * groups + i, b * groups + j) for a, b in ahead for i, j in off_chip
    ]

    def tiled(value):
        value = value.reshape(FRAMES, ROWS, HB, J, PAIR).transpose(0, 3, 1, 2, 4)
        return value.reshape(FIELD, PAIR)

    own = lax.ppermute(state, "segment", ahead)
    field, gains = lax.optimization_barrier((tiled(state), gains))
    sw = spatial_weight.reshape(2, 3, 3 * C, C)
    tw = temporal_weight.reshape(2, 3, C, C)
    made = prepare(bounds, timesteps, gains[0], time_weight[0], sw, tw)
    field, made = lax.optimization_barrier((field, made))
    far = lax.ppermute(field, ("segment", "rows"), off_chip_ahead)
    own, made = lax.optimization_barrier((own, made))
    info, bias, gain_pairs, sp, tp = made
    core = [lax.ppermute(own[:, f : f + 1], "rows", on_chip) for f in range(FRAMES)]
    field = apply_blocks(
        0, info, own, far, core, bias, gain_pairs, sw, sp, tp
    )
    for step in range(1, STEPS):
        far = lax.ppermute(field, ("segment", "rows"), off_chip_ahead)
        own = lax.ppermute(field, "segment", ahead)
        core = lax.ppermute(own, "rows", on_chip)
        field = apply_blocks(step, info, own, far, core, bias, gain_pairs, sw, sp, tp)
    field = field.reshape(FRAMES, J, ROWS, HB, PAIR).transpose(0, 2, 3, 1, 4)
    return field.reshape(1, FRAMES, ROWS, W * C)


def solution(mesh):
    placed = (
        P("segment", None, "rows", None),
        P(),
        P(),
        P("segment", None, None),
        P("segment", None, None, None, None, None),
        P("segment", None, None, None, None),
        P("segment", None, None, None),
    )
    return jax.shard_map(
        body,
        mesh=mesh,
        in_specs=placed,
        out_specs=P("segment", None, "rows", None),
        check_vma=False,
    )
```

```python
import functools
import math

import jax
import jax.numpy as jnp
from jax import lax
from jax.experimental import pallas as pl
from jax.experimental.pallas import tpu as pltpu
from jax.sharding import PartitionSpec as P

C = 320
W = 72
STEPS = 2
FRAMES = 2
ROWS = 2

HB = 4
J = W // 2 // HB
PAIR = 2 * C
GROUP = ROWS * HB
FIELD = FRAMES * J * GROUP
PAD = 64
LANES = PAIR + 256
SECOND = C + PAD
EPS = 1e-06


def low_lanes(shape):
    return lax.broadcasted_iota(jnp.int32, shape, len(shape) - 1) < PAD


def normalise(value, gain):
    low = low_lanes(value[..., 256:384].shape)
    square = value * value
    middle = square[..., 256:384]
    first = square[..., 0:128] + square[..., 128:256] + jnp.where(low, middle, 0.0)
    second = square[..., 384:512] + square[..., 512:640] + jnp.where(low, 0.0, middle)
    scale = lax.rsqrt(jnp.sum(first, axis=-1, keepdims=True) / C + EPS)
    other = lax.rsqrt(jnp.sum(second, axis=-1, keepdims=True) / C + EPS)
    scaled = jnp.concatenate(
        [
            value[..., 0:256] * scale,
            value[..., 256:384] * jnp.where(low, scale, other),
            value[..., 384:640] * other,
        ],
        axis=-1,
    )
    return scaled * gain


def load(ref):
    return ref[...].astype(jnp.float32).reshape(FRAMES * J, GROUP, PAIR)


def flip(value):
    return pltpu.roll(value, HB, 1)


def flip_if(odd, value):
    return pltpu.roll(value, HB * odd, 1)


def halves(first, second):
    row = lax.broadcasted_iota(jnp.int32, first.shape, 1)
    return jnp.where(row < HB, first, second)


def shifted_h(value, by):
    rows = value.shape[0]
    moved = pltpu.roll(value, by % rows, 0)
    h = lax.rem(lax.broadcasted_iota(jnp.int32, value.shape, 0), HB)
    edge = 0 if by == 1 else HB - 1
    return jnp.where(h == edge, 0.0, moved)


def put(ref, at, value):
    middle = value[..., 256:384]
    low = low_lanes(middle.shape)
    ref[at + (slice(None), slice(0, PAIR))] = value.astype(jnp.bfloat16)
    ref[at + (slice(None), slice(PAIR, PAIR + 128))] = jnp.where(low, 0.0, middle).astype(
        jnp.bfloat16
    )
    ref[at + (slice(None), slice(PAIR + 128, LANES))] = jnp.where(low, middle, 0.0).astype(
        jnp.bfloat16
    )


def put_wide(ref, dy, first, second):
    tiles = jnp.concatenate([first, second], axis=1).reshape(FRAMES, J, 2 * GROUP, PAIR)
    put(ref, (dy, slice(None), slice(1, J + 1)), tiles)
    for f in range(FRAMES):
        put(ref, (dy, f, 0), shifted_h(tiles[f, J - 1], 1))
        put(ref, (dy, f, J + 1), shifted_h(tiles[f, 0], -1))


def put_thin(ref, dy, value):
    tiles = value.reshape(FRAMES, J, GROUP, PAIR)
    tiles = jnp.concatenate([tiles[0], tiles[1]], axis=1)
    put(ref, (dy, slice(1, J + 1)), tiles)
    put(ref, (dy, 0), shifted_h(tiles[J - 1], 1))
    put(ref, (dy, J + 1), shifted_h(tiles[0], -1))


def rows_of(ref, dy, j0, wide, start, stop):
    if wide:
        return ref[dy, :, j0 : j0 + J, :, start:stop].reshape(-1, stop - start)
    return ref[dy, j0 : j0 + J, :, start:stop].reshape(-1, stop - start)


def silu(value):
    half = 0.5 * value
    return half + half * jnp.tanh(half)


def dot(a, b):
    return jnp.dot(a, b, preferred_element_type=jnp.float32)


def spatial(ref, wide, taps, weights, pairs, slot, odd):
    center, before, after, joint, left, right = [], [], [], [], [], []
    for dy in taps:
        at = dy + odd * (2 - 2 * dy)
        rows = functools.partial(rows_of, ref, dy, wide=wide)
        center.append(rows(1, start=0, stop=PAIR))
        before += [rows(0, start=PAIR, stop=PAIR + 128), rows(0, start=384, stop=PAIR)]
        after += [rows(2, start=0, stop=256), rows(2, start=PAIR + 128, stop=LANES)]
        filler = weights[slot, at, 0:PAD, :]
        joint.append(pairs[slot, at])
        left += [filler, weights[slot, at, 0:C, :]]
        right += [weights[slot, at, 2 * C :, :], filler]
    both = dot(jnp.concatenate(center, axis=1), jnp.concatenate(joint, axis=0))
    even_sum = dot(jnp.concatenate(before, axis=1), jnp.concatenate(left, axis=0))
    odd_sum = dot(jnp.concatenate(after, axis=1), jnp.concatenate(right, axis=0))
    return both[:, :C] + even_sum, both[:, SECOND:] + odd_sum


def temporal(u0, u1, pairs, slot):
    gap = jnp.zeros((u0.shape[0], PAD), u0.dtype)
    both = dot(jnp.concatenate([u0, gap, u1, gap], axis=1), pairs[slot])
    return both[:, :C], both[:, SECOND:]


def pairs_kernel(spatial_weight, temporal_weight, spatial_pairs, temporal_pairs):
    for slot in range(2):
        for dy in range(3):
            kernel = spatial_weight.at[slot, dy]
            spatial_pairs[slot, dy, :, 0:C] = kernel[C : 3 * C, :]
            spatial_pairs[slot, dy, :, SECOND : SECOND + C] = kernel[0 : 2 * C, :]
        for frame, lanes in enumerate((slice(0, C), slice(SECOND, SECOND + C))):
            for other in range(2):
                tap = temporal_weight.at[slot, 1 - frame + other]
                temporal_pairs[slot, other * SECOND : other * SECOND + C, lanes] = tap[...]
                temporal_pairs[slot, other * SECOND + C : (other + 1) * SECOND, lanes] = tap[0:PAD, :]


def frequency_kernel(out):
    half = out.shape[1] // 2
    at = lax.broadcasted_iota(jnp.int32, out.shape, 1)
    index = jnp.where(at < half, at, at - half).astype(jnp.float32)
    out[...] = jnp.exp(-math.log(10000.0) * index / half)


def prepare_kernel(
    bounds_hbm,
    timesteps_hbm,
    gains_hbm,
    time_hbm,
    frequency,
    info,
    bias,
    gain_pairs,
    bounds,
    timesteps,
    gains,
    time_weight,
    sems,
):
    copies = [
        pltpu.make_async_copy(source, target, sems.at[n])
        for n, (source, target) in enumerate(
            (
                (bounds_hbm, bounds),
                (timesteps_hbm, timesteps),
                (gains_hbm, gains),
                (time_hbm, time_weight),
            )
        )
    ]
    for copy in copies:
        copy.start()
    for copy in copies:
        copy.wait()
    segment = lax.axis_index("segment")
    info[...] = jnp.full(info.shape, bounds[segment + 1] - bounds[segment], jnp.int32)
    gain_pairs[...] = jnp.concatenate([gains[...], gains[...]], axis=1)
    entries = time_weight.shape[1]
    half = entries // 2
    at = lax.broadcasted_iota(jnp.int32, (8, entries), 1)
    step = lax.broadcasted_iota(jnp.int32, (8, entries), 0)
    times = jnp.zeros((8, entries), jnp.int32)
    for s in range(STEPS):
        times = jnp.where(step == s, timesteps[s], times)
    angle = times.astype(jnp.float32) * frequency[...]
    emb = jnp.where(at < half, jnp.cos(angle), jnp.sin(angle))
    for slot in range(2):
        made = jnp.dot(
            emb,
            time_weight[slot],
            precision=lax.Precision.HIGHEST,
            preferred_element_type=jnp.float32,
        )
        for s in range(STEPS):
            bias[s, slot : slot + 1, :] = made[s : s + 1]


def place():
    row_group = lax.axis_index("rows")
    at_end = (row_group == 0) | (row_group == lax.axis_size("rows") - 1)
    return lax.rem(row_group, 2), at_end


def side_of(step):
    return "core" if step == 0 else "far"


def load_far(step, ref):
    odd, at_end = place()
    value = load(ref)
    if step == 0:
        value = flip_if(1 - odd, value)
    return jnp.where(at_end, 0.0, value)


def lay_out(refs, scratch, tiles, turn):
    frames = [ref.at[0, f] for ref in refs for f in range(ref.shape[1])]
    for f in range(FRAMES):
        for j in range(J):
            for h in range(HB):
                at = (h * J + j) * PAIR
                rows = frames[f][:, at : at + PAIR].astype(jnp.float32)
                for n in range(PAIR // 128):
                    scratch[f * J + j, n, pl.ds(h, ROWS, stride=HB), :] = rows[
                        :, n * 128 : (n + 1) * 128
                    ]
    value = jnp.concatenate([scratch[:, n] for n in range(PAIR // 128)], axis=-1)
    tiles[...] = flip_if(turn, value)


def first_kernel(step, info, own, *refs):
    count = jnp.max(info[0:1, :])
    odd, _ = place()
    core_side = side_of(step) == "core"
    sides, refs = refs[: FRAMES - step], refs[FRAMES - step :]
    gains, sw, sp, part, n_own, n_side = refs[:6]
    tiles, (wide, thin, scratch) = refs[6:-3], refs[-3:]
    if step == 0:
        lay_out([own], scratch, tiles[0], odd)
        lay_out(sides, scratch, tiles[1], 1 - odd)
        mine, theirs = tiles[0][...], tiles[1][...]
    else:
        mine, theirs = load(own), load_far(step, sides[0])
    gain = gains[0:1, :].reshape(1, 1, PAIR)
    normed, side_normed = normalise(mine, gain), normalise(theirs, gain)
    n_own[...] = normed
    n_side[...] = side_normed

    @pl.when(count > 1)
    def _():
        if core_side:
            put_wide(wide, 2, normed, flip(side_normed))
        else:
            put_wide(wide, 0, flip(side_normed), normed)
        even, odd_sum = spatial(wide, True, (2 if core_side else 0,), sw, sp, 0, odd)
        part[0], part[1] = even, odd_sum

    @pl.when(count == 1)
    def _():
        put_thin(thin, 1, normed)
        if core_side:
            put_thin(thin, 2, halves(flip(normed), side_normed))
        else:
            put_thin(thin, 0, halves(side_normed, flip(normed)))
        even, odd_sum = spatial(thin, False, (1, 2) if core_side else (0, 1), sw, sp, 0, odd)
        part[0, :FIELD], part[1, :FIELD] = even, odd_sum


def second_kernel(
    step, info, own, far, core, part, n_own, n_side, bias, gains, sw, sp, tp, out, wide, thin, acc, center
):
    count = jnp.max(info[0:1, :])
    odd, at_end = place()
    far_last = side_of(step) == "core"
    mine = own[...] if step == 0 else load(own)
    theirs = load_far(step, far) if far_last else load(core)
    last_normed = normalise(theirs, gains[0:1, :].reshape(1, 1, PAIR))

    @pl.when(count == 1)
    def _():
        if far_last:
            put_thin(thin, 0, halves(last_normed, flip(n_own[...])))
        else:
            put_thin(thin, 2, halves(flip(n_own[...]), last_normed))
        even, odd_sum = spatial(thin, False, (0 if far_last else 2,), sw, sp, 0, odd)
        acc[0], acc[1] = part[0, :FIELD] + even, part[1, :FIELD] + odd_sum
        center[...] = mine

    @pl.when(count > 1)
    def _():
        normed = n_own[...]
        turned = flip(normed)
        if far_last:
            far_normed, core_normed = last_normed, n_side[...]
            put_wide(wide, 0, flip(far_normed), normed)
        else:
            far_normed, core_normed = n_side[...], last_normed
            put_wide(wide, 2, normed, flip(core_normed))
        put_wide(wide, 1, halves(far_normed, turned), halves(turned, core_normed))
        even, odd_sum = spatial(wide, True, (0, 1) if far_last else (1, 2), sw, sp, 0, odd)
        by_far = theirs if far_last else load_far(step, far)
        by_core = core[...] if far_last else theirs
        even = part[0] + even + bias[step, 0:1, :]
        odd_sum = part[1] + odd_sum + bias[step, 0:1, :]
        half = FIELD
        u_even, u_odd = silu(even).astype(jnp.bfloat16), silu(odd_sum).astype(jnp.bfloat16)
        u0 = jnp.concatenate([u_even[:half], u_odd[:half]], axis=0)
        u1 = jnp.concatenate([u_even[half:], u_odd[half:]], axis=0)
        v0, v1 = temporal(u0, u1, tp, 0)
        v_even = jnp.concatenate([v0[:half], v1[:half]], axis=0)
        v_odd = jnp.concatenate([v0[half:], v1[half:]], axis=0)
        change = jnp.concatenate([even + v_even, odd_sum + v_odd], axis=1)
        change = change.reshape(FRAMES * J, 2 * GROUP, PAIR)
        back = flip(mine)
        first = halves(by_far, back) + change[:, :GROUP]
        second = halves(back, by_core) + change[:, GROUP:]
        first = first.astype(jnp.bfloat16).astype(jnp.float32)
        second = second.astype(jnp.bfloat16).astype(jnp.float32)
        row = lax.broadcasted_iota(jnp.int32, first.shape, 1)
        first = jnp.where((row < HB) & at_end, 0.0, first)
        center[...] = halves(flip(first), flip(second))
        gain = gains[1:2, :].reshape(1, 1, PAIR)
        n_first, n_second = normalise(first, gain), normalise(second, gain)
        put_thin(thin, 0, n_first)
        put_thin(thin, 1, halves(flip(n_first), flip(n_second)))
        put_thin(thin, 2, n_second)
        even, odd_sum = spatial(thin, False, (0, 1, 2), sw, sp, 1, odd)
        acc[0], acc[1] = even, odd_sum

    last = count - 1
    shift = bias[step, pl.ds(last, 1), :]
    even = (acc[0] + shift).reshape(J, FRAMES, GROUP, C)
    odd_sum = (acc[1] + shift).reshape(J, FRAMES, GROUP, C)
    u0, u1 = (
        jnp.concatenate(
            [silu(even[:, f]).reshape(-1, C), silu(odd_sum[:, f]).reshape(-1, C)], axis=0
        )
        for f in range(FRAMES)
    )
    v0, v1 = temporal(u0.astype(jnp.bfloat16), u1.astype(jnp.bfloat16), tp, last)
    half = J * GROUP
    for f, v in enumerate((v0, v1)):
        a_even, a_odd = even[:, f].reshape(half, C), odd_sum[:, f].reshape(half, C)
        change = jnp.concatenate([a_even + v[:half], a_odd + v[half:]], axis=1)
        result = center[f * J : (f + 1) * J] + change.reshape(J, GROUP, PAIR)
        if step == STEPS - 1:
            result = flip_if(odd, result)
        out[f * half : (f + 1) * half, :] = result.reshape(half, PAIR).astype(jnp.bfloat16)


VMEM = pl.BlockSpec(memory_space=pltpu.VMEM)


def call(kernel, name, outs, scratch, flops):
    return pl.pallas_call(
        kernel,
        out_shape=tuple(jax.ShapeDtypeStruct(shape, dtype) for shape, dtype in outs),
        out_specs=(VMEM,) * len(outs),
        scratch_shapes=[pltpu.VMEM(shape, dtype) for shape, dtype in scratch],
        compiler_params=pltpu.CompilerParams(vmem_limit_bytes=24 * 1024 * 1024),
        cost_estimate=pl.CostEstimate(
            flops=flops, bytes_accessed=flops // 4_000, transcendentals=0
        ),
        name=name,
    )


def prepare(bounds, timesteps, gains, time_weight):
    hbm = pl.BlockSpec(memory_space=pltpu.HBM)
    (frequency,) = call(
        frequency_kernel, "frequency", [((8, time_weight.shape[1]), jnp.float32)], [], 4_000_000_000
    )()
    return pl.pallas_call(
        prepare_kernel,
        out_shape=(
            jax.ShapeDtypeStruct((8, 128), jnp.int32),
            jax.ShapeDtypeStruct((STEPS, 2, C), jnp.float32),
            jax.ShapeDtypeStruct((2, PAIR), jnp.float32),
        ),
        in_specs=[hbm, hbm, hbm, hbm, VMEM],
        out_specs=(VMEM,) * 3,
        scratch_shapes=[
            pltpu.SMEM(bounds.shape, jnp.int32),
            pltpu.SMEM(timesteps.shape, jnp.int32),
            pltpu.VMEM(gains.shape, jnp.float32),
            pltpu.VMEM(time_weight.shape, jnp.float32),
            pltpu.SemaphoreType.DMA((4,)),
        ],
        compiler_params=pltpu.CompilerParams(vmem_limit_bytes=24 * 1024 * 1024),
        cost_estimate=pl.CostEstimate(
            flops=8_000_000_000, bytes_accessed=1_000_000, transcendentals=10_000
        ),
        name="prepare",
    )(bounds, timesteps, gains, time_weight, frequency)


WIDE = ((3, FRAMES, J + 2, 2 * GROUP, LANES), jnp.bfloat16)
THIN = ((3, J + 2, FRAMES * GROUP, LANES), jnp.bfloat16)
ROWS_F32 = ((FRAMES * J, GROUP, PAIR), jnp.float32)


def apply_blocks(step, info, own, far, core, bias, gains, sw, sp, tp):
    sides = core if side_of(step) == "core" else [far]
    part, n_own, n_side, *tiles = call(
        functools.partial(first_kernel, step),
        "own_and_" + side_of(step) + "_rows",
        [((2, 2 * FIELD, C), jnp.float32)] + [ROWS_F32] * (4 if step == 0 else 2),
        [WIDE, THIN, ((FRAMES * J, PAIR // 128, GROUP, 128), jnp.float32)],
        1_000_000,
    )(info, own, *sides, gains, sw, sp)
    if step == 0:
        own, core = tiles
    (field,) = call(
        functools.partial(second_kernel, step),
        "residual_blocks",
        [((FIELD, PAIR), jnp.bfloat16)],
        [WIDE, THIN, ((2, FIELD, C), jnp.float32), ROWS_F32],
        4_000_000_000,
    )(info, own, far, core, part, n_own, n_side, bias, gains, sw, sp, tp)
    return field


def body(state, bounds, timesteps, gains, spatial_weight, temporal_weight, time_weight):
    groups = lax.axis_size("rows")
    segments = lax.axis_size("segment")
    ahead = [(i, (i + 1) % segments) for i in range(segments)]
    on_chip = [(i, i ^ 1) for i in range(groups)]
    off_chip = [(i, i + 1) for i in range(1, groups - 1, 2)]
    off_chip = off_chip + [(j, i) for i, j in off_chip] + [(0, 0), (groups - 1, groups - 1)]
    off_chip_ahead = [
        (a * groups + i, b * groups + j) for a, b in ahead for i, j in off_chip
    ]

    def tiled(value):
        value = value.reshape(FRAMES, ROWS, HB, J, PAIR).transpose(0, 3, 1, 2, 4)
        return value.reshape(FIELD, PAIR)

    own = lax.ppermute(state, "segment", ahead)
    field, gains = lax.optimization_barrier((tiled(state), gains))
    sw = spatial_weight.reshape(2, 3, 3 * C, C)
    tw = temporal_weight.reshape(2, 3, C, C)
    made = prepare(bounds, timesteps, gains[0], time_weight[0])
    field, made = lax.optimization_barrier((field, made))
    far = lax.ppermute(field, ("segment", "rows"), off_chip_ahead)
    sw, tw, made = lax.optimization_barrier((sw, tw, made))
    side_by_side = call(
        pairs_kernel,
        "weight_pairs",
        [((2, 3, 2 * C, SECOND + C), jnp.bfloat16), ((2, 2 * SECOND, SECOND + C), jnp.bfloat16)],
        [],
        4_000_000_000,
    )(sw, tw)
    own, made, side_by_side = lax.optimization_barrier((own, made, side_by_side))
    info, bias, gain_pairs = made
    sp, tp = side_by_side
    core = [lax.ppermute(own[:, f : f + 1], "rows", on_chip) for f in range(FRAMES)]
    field = apply_blocks(
        0, info, own, far, core, bias, gain_pairs, sw, sp, tp
    )
    for step in range(1, STEPS):
        far = lax.ppermute(field, ("segment", "rows"), off_chip_ahead)
        own = lax.ppermute(field, "segment", ahead)
        core = lax.ppermute(own, "rows", on_chip)
        field = apply_blocks(step, info, own, far, core, bias, gain_pairs, sw, sp, tp)
    field = field.reshape(FRAMES, J, ROWS, HB, PAIR).transpose(0, 2, 3, 1, 4)
    return field.reshape(1, FRAMES, ROWS, W * C)


def solution(mesh):
    placed = (
        P("segment", None, "rows", None),
        P(),
        P(),
        P("segment", None, None),
        P("segment", None, None, None, None, None),
        P("segment", None, None, None, None),
        P("segment", None, None, None),
    )
    return jax.shard_map(
        body,
        mesh=mesh,
        in_specs=placed,
        out_specs=P("segment", None, "rows", None),
        check_vma=False,
    )
```

```python
import functools
import math

import jax
import jax.numpy as jnp
from jax import lax
from jax.experimental import pallas as pl
from jax.experimental.pallas import tpu as pltpu
from jax.sharding import PartitionSpec as P

C = 320
W = 72
STEPS = 2
FRAMES = 2
ROWS = 2

HB = 4
J = W // 2 // HB
PAIR = 2 * C
GROUP = ROWS * HB
FIELD = FRAMES * J * GROUP
PAD = 64
LANES = PAIR + 256
SECOND = C + PAD
EPS = 1e-06


def low_lanes(shape):
    return lax.broadcasted_iota(jnp.int32, shape, len(shape) - 1) < PAD


def normalise(value, gain):
    low = low_lanes(value[..., 256:384].shape)
    square = value * value
    middle = square[..., 256:384]
    first = square[..., 0:128] + square[..., 128:256] + jnp.where(low, middle, 0.0)
    second = square[..., 384:512] + square[..., 512:640] + jnp.where(low, 0.0, middle)
    scale = lax.rsqrt(jnp.sum(first, axis=-1, keepdims=True) / C + EPS)
    other = lax.rsqrt(jnp.sum(second, axis=-1, keepdims=True) / C + EPS)
    scaled = jnp.concatenate(
        [
            value[..., 0:256] * scale,
            value[..., 256:384] * jnp.where(low, scale, other),
            value[..., 384:640] * other,
        ],
        axis=-1,
    )
    return scaled * gain


def load(ref):
    return ref[...].astype(jnp.float32).reshape(FRAMES * J, GROUP, PAIR)


def flip(value):
    return pltpu.roll(value, HB, 1)


def flip_if(odd, value):
    return pltpu.roll(value, HB * odd, 1)


def halves(first, second):
    row = lax.broadcasted_iota(jnp.int32, first.shape, 1)
    return jnp.where(row < HB, first, second)


def shifted_h(value, by):
    rows = value.shape[0]
    moved = pltpu.roll(value, by % rows, 0)
    h = lax.rem(lax.broadcasted_iota(jnp.int32, value.shape, 0), HB)
    edge = 0 if by == 1 else HB - 1
    return jnp.where(h == edge, 0.0, moved)


def put(ref, at, value):
    middle = value[..., 256:384]
    low = low_lanes(middle.shape)
    ref[at + (slice(None), slice(0, PAIR))] = value.astype(jnp.bfloat16)
    ref[at + (slice(None), slice(PAIR, PAIR + 128))] = jnp.where(low, 0.0, middle).astype(
        jnp.bfloat16
    )
    ref[at + (slice(None), slice(PAIR + 128, LANES))] = jnp.where(low, middle, 0.0).astype(
        jnp.bfloat16
    )


def put_wide(ref, dy, first, second):
    tiles = jnp.concatenate([first, second], axis=1).reshape(FRAMES, J, 2 * GROUP, PAIR)
    put(ref, (dy, slice(None), slice(1, J + 1)), tiles)
    for f in range(FRAMES):
        put(ref, (dy, f, 0), shifted_h(tiles[f, J - 1], 1))
        put(ref, (dy, f, J + 1), shifted_h(tiles[f, 0], -1))


def put_thin(ref, dy, value):
    tiles = value.reshape(FRAMES, J, GROUP, PAIR)
    tiles = jnp.concatenate([tiles[0], tiles[1]], axis=1)
    put(ref, (dy, slice(1, J + 1)), tiles)
    put(ref, (dy, 0), shifted_h(tiles[J - 1], 1))
    put(ref, (dy, J + 1), shifted_h(tiles[0], -1))


def rows_of(ref, dy, j0, wide, start, stop):
    if wide:
        return ref[dy, :, j0 : j0 + J, :, start:stop].reshape(-1, stop - start)
    return ref[dy, j0 : j0 + J, :, start:stop].reshape(-1, stop - start)


def silu(value):
    half = 0.5 * value
    return half + half * jnp.tanh(half)


def dot(a, b):
    return jnp.dot(a, b, preferred_element_type=jnp.float32)


def spatial(ref, wide, taps, weights, pairs, slot, odd):
    center, before, after, joint, left, right = [], [], [], [], [], []
    for dy in taps:
        at = dy + odd * (2 - 2 * dy)
        rows = functools.partial(rows_of, ref, dy, wide=wide)
        center.append(rows(1, start=0, stop=PAIR))
        before += [rows(0, start=PAIR, stop=PAIR + 128), rows(0, start=384, stop=PAIR)]
        after += [rows(2, start=0, stop=256), rows(2, start=PAIR + 128, stop=LANES)]
        filler = weights[slot, at, 0:PAD, :]
        joint.append(pairs[slot, at])
        left += [filler, weights[slot, at, 0:C, :]]
        right += [weights[slot, at, 2 * C :, :], filler]
    both = dot(jnp.concatenate(center, axis=1), jnp.concatenate(joint, axis=0))
    even_sum = dot(jnp.concatenate(before, axis=1), jnp.concatenate(left, axis=0))
    odd_sum = dot(jnp.concatenate(after, axis=1), jnp.concatenate(right, axis=0))
    return both[:, :C] + even_sum, both[:, SECOND:] + odd_sum


def temporal(u0, u1, pairs, slot):
    gap = jnp.zeros((u0.shape[0], PAD), u0.dtype)
    both = dot(jnp.concatenate([u0, gap, u1, gap], axis=1), pairs[slot])
    return both[:, :C], both[:, SECOND:]


def pairs_kernel(spatial_weight, temporal_weight, spatial_pairs, temporal_pairs):
    for slot in range(2):
        for dy in range(3):
            kernel = spatial_weight.at[slot, dy]
            spatial_pairs[slot, dy, :, 0:C] = kernel[C : 3 * C, :]
            spatial_pairs[slot, dy, :, SECOND : SECOND + C] = kernel[0 : 2 * C, :]
        for frame, lanes in enumerate((slice(0, C), slice(SECOND, SECOND + C))):
            for other in range(2):
                tap = temporal_weight.at[slot, 1 - frame + other]
                temporal_pairs[slot, other * SECOND : other * SECOND + C, lanes] = tap[...]
                temporal_pairs[slot, other * SECOND + C : (other + 1) * SECOND, lanes] = tap[0:PAD, :]


def frequency_kernel(out):
    half = out.shape[1] // 2
    at = lax.broadcasted_iota(jnp.int32, out.shape, 1)
    index = jnp.where(at < half, at, at - half).astype(jnp.float32)
    out[...] = jnp.exp(-math.log(10000.0) * index / half)


def prepare_kernel(
    bounds_hbm,
    timesteps_hbm,
    gains_hbm,
    time_hbm,
    frequency,
    info,
    bias,
    gain_pairs,
    bounds,
    timesteps,
    gains,
    time_weight,
    sems,
):
    copies = [
        pltpu.make_async_copy(source, target, sems.at[n])
        for n, (source, target) in enumerate(
            (
                (bounds_hbm, bounds),
                (timesteps_hbm, timesteps),
                (gains_hbm, gains),
                (time_hbm, time_weight),
            )
        )
    ]
    for copy in copies:
        copy.start()
    for copy in copies:
        copy.wait()
    segment = lax.axis_index("segment")
    info[...] = jnp.full(info.shape, bounds[segment + 1] - bounds[segment], jnp.int32)
    gain_pairs[...] = jnp.concatenate([gains[...], gains[...]], axis=1)
    entries = time_weight.shape[1]
    half = entries // 2
    at = lax.broadcasted_iota(jnp.int32, (8, entries), 1)
    step = lax.broadcasted_iota(jnp.int32, (8, entries), 0)
    times = jnp.zeros((8, entries), jnp.int32)
    for s in range(STEPS):
        times = jnp.where(step == s, timesteps[s], times)
    angle = times.astype(jnp.float32) * frequency[...]
    emb = jnp.where(at < half, jnp.cos(angle), jnp.sin(angle))
    for slot in range(2):
        made = jnp.dot(
            emb,
            time_weight[slot],
            precision=lax.Precision.HIGHEST,
            preferred_element_type=jnp.float32,
        )
        for s in range(STEPS):
            bias[s, slot : slot + 1, :] = made[s : s + 1]


def place():
    row_group = lax.axis_index("rows")
    at_end = (row_group == 0) | (row_group == lax.axis_size("rows") - 1)
    return lax.rem(row_group, 2), at_end


def side_of(step):
    return "core" if step == 0 else "far"


def load_far(step, ref):
    odd, at_end = place()
    value = load(ref)
    if step == 0:
        value = flip_if(1 - odd, value)
    return jnp.where(at_end, 0.0, value)


def lay_out(refs, scratch, tiles, turn):
    frames = [ref.at[0, f] for ref in refs for f in range(ref.shape[1])]
    for f in range(FRAMES):
        for j in range(J):
            for h in range(HB):
                at = (h * J + j) * PAIR
                rows = frames[f][:, at : at + PAIR].astype(jnp.float32)
                for n in range(PAIR // 128):
                    scratch[f * J + j, n, pl.ds(h, ROWS, stride=HB), :] = rows[
                        :, n * 128 : (n + 1) * 128
                    ]
    value = jnp.concatenate([scratch[:, n] for n in range(PAIR // 128)], axis=-1)
    tiles[...] = flip_if(turn, value)


def first_kernel(step, info, own, *refs):
    count = jnp.max(info[0:1, :])
    odd, _ = place()
    core_side = side_of(step) == "core"
    sides, refs = refs[: FRAMES - step], refs[FRAMES - step :]
    gains, sw, sp, part, n_own, n_side = refs[:6]
    tiles, (wide, thin, scratch) = refs[6:-3], refs[-3:]
    if step == 0:
        lay_out([own], scratch, tiles[0], odd)
        lay_out(sides, scratch, tiles[1], 1 - odd)
        mine, theirs = tiles[0][...], tiles[1][...]
    else:
        mine, theirs = load(own), load_far(step, sides[0])
    gain = gains[0:1, :].reshape(1, 1, PAIR)
    normed, side_normed = normalise(mine, gain), normalise(theirs, gain)
    n_own[...] = normed
    n_side[...] = side_normed

    @pl.when(count > 1)
    def _():
        if core_side:
            put_wide(wide, 2, normed, flip(side_normed))
        else:
            put_wide(wide, 0, flip(side_normed), normed)
        even, odd_sum = spatial(wide, True, (2 if core_side else 0,), sw, sp, 0, odd)
        part[0], part[1] = even, odd_sum

    @pl.when(count == 1)
    def _():
        put_thin(thin, 1, normed)
        if core_side:
            put_thin(thin, 2, halves(flip(normed), side_normed))
        else:
            put_thin(thin, 0, halves(side_normed, flip(normed)))
        even, odd_sum = spatial(thin, False, (1, 2) if core_side else (0, 1), sw, sp, 0, odd)
        part[0, :FIELD], part[1, :FIELD] = even, odd_sum


def second_kernel(
    step, info, own, far, core, part, n_own, n_side, bias, gains, sw, sp, tp, out, wide, thin, acc, center
):
    count = jnp.max(info[0:1, :])
    odd, at_end = place()
    far_last = side_of(step) == "core"
    mine = own[...] if step == 0 else load(own)
    theirs = load_far(step, far) if far_last else load(core)
    last_normed = normalise(theirs, gains[0:1, :].reshape(1, 1, PAIR))

    @pl.when(count == 1)
    def _():
        if far_last:
            put_thin(thin, 0, halves(last_normed, flip(n_own[...])))
        else:
            put_thin(thin, 2, halves(flip(n_own[...]), last_normed))
        even, odd_sum = spatial(thin, False, (0 if far_last else 2,), sw, sp, 0, odd)
        acc[0], acc[1] = part[0, :FIELD] + even, part[1, :FIELD] + odd_sum
        center[...] = mine

    @pl.when(count > 1)
    def _():
        normed = n_own[...]
        turned = flip(normed)
        if far_last:
            far_normed, core_normed = last_normed, n_side[...]
            put_wide(wide, 0, flip(far_normed), normed)
        else:
            far_normed, core_normed = n_side[...], last_normed
            put_wide(wide, 2, normed, flip(core_normed))
        put_wide(wide, 1, halves(far_normed, turned), halves(turned, core_normed))
        even, odd_sum = spatial(wide, True, (0, 1) if far_last else (1, 2), sw, sp, 0, odd)
        by_far = theirs if far_last else load_far(step, far)
        by_core = core[...] if far_last else theirs
        even = part[0] + even + bias[step, 0:1, :]
        odd_sum = part[1] + odd_sum + bias[step, 0:1, :]
        half = FIELD
        u_even, u_odd = silu(even).astype(jnp.bfloat16), silu(odd_sum).astype(jnp.bfloat16)
        u0 = jnp.concatenate([u_even[:half], u_odd[:half]], axis=0)
        u1 = jnp.concatenate([u_even[half:], u_odd[half:]], axis=0)
        v0, v1 = temporal(u0, u1, tp, 0)
        v_even = jnp.concatenate([v0[:half], v1[:half]], axis=0)
        v_odd = jnp.concatenate([v0[half:], v1[half:]], axis=0)
        change = jnp.concatenate([even + v_even, odd_sum + v_odd], axis=1)
        change = change.reshape(FRAMES * J, 2 * GROUP, PAIR)
        back = flip(mine)
        first = halves(by_far, back) + change[:, :GROUP]
        second = halves(back, by_core) + change[:, GROUP:]
        first = first.astype(jnp.bfloat16).astype(jnp.float32)
        second = second.astype(jnp.bfloat16).astype(jnp.float32)
        row = lax.broadcasted_iota(jnp.int32, first.shape, 1)
        first = jnp.where((row < HB) & at_end, 0.0, first)
        center[...] = halves(flip(first), flip(second))
        gain = gains[1:2, :].reshape(1, 1, PAIR)
        n_first, n_second = normalise(first, gain), normalise(second, gain)
        put_thin(thin, 0, n_first)
        put_thin(thin, 1, halves(flip(n_first), flip(n_second)))
        put_thin(thin, 2, n_second)
        even, odd_sum = spatial(thin, False, (0, 1, 2), sw, sp, 1, odd)
        acc[0], acc[1] = even, odd_sum

    last = count - 1
    shift = bias[step, pl.ds(last, 1), :]
    even = (acc[0] + shift).reshape(J, FRAMES, GROUP, C)
    odd_sum = (acc[1] + shift).reshape(J, FRAMES, GROUP, C)
    u0, u1 = (
        jnp.concatenate(
            [silu(even[:, f]).reshape(-1, C), silu(odd_sum[:, f]).reshape(-1, C)], axis=0
        )
        for f in range(FRAMES)
    )
    v0, v1 = temporal(u0.astype(jnp.bfloat16), u1.astype(jnp.bfloat16), tp, last)
    half = J * GROUP
    for f, v in enumerate((v0, v1)):
        a_even, a_odd = even[:, f].reshape(half, C), odd_sum[:, f].reshape(half, C)
        change = jnp.concatenate([a_even + v[:half], a_odd + v[half:]], axis=1)
        result = center[f * J : (f + 1) * J] + change.reshape(J, GROUP, PAIR)
        if step == STEPS - 1:
            result = flip_if(odd, result)
        out[f * half : (f + 1) * half, :] = result.reshape(half, PAIR).astype(jnp.bfloat16)


VMEM = pl.BlockSpec(memory_space=pltpu.VMEM)


def call(kernel, name, outs, scratch, flops):
    return pl.pallas_call(
        kernel,
        out_shape=tuple(jax.ShapeDtypeStruct(shape, dtype) for shape, dtype in outs),
        out_specs=(VMEM,) * len(outs),
        scratch_shapes=[pltpu.VMEM(shape, dtype) for shape, dtype in scratch],
        compiler_params=pltpu.CompilerParams(vmem_limit_bytes=24 * 1024 * 1024),
        cost_estimate=pl.CostEstimate(
            flops=flops, bytes_accessed=flops // 4_000, transcendentals=0
        ),
        name=name,
    )


def prepare(bounds, timesteps, gains, time_weight):
    hbm = pl.BlockSpec(memory_space=pltpu.HBM)
    (frequency,) = call(
        frequency_kernel, "frequency", [((8, time_weight.shape[1]), jnp.float32)], [], 4_000_000_000
    )()
    return pl.pallas_call(
        prepare_kernel,
        out_shape=(
            jax.ShapeDtypeStruct((8, 128), jnp.int32),
            jax.ShapeDtypeStruct((STEPS, 2, C), jnp.float32),
            jax.ShapeDtypeStruct((2, PAIR), jnp.float32),
        ),
        in_specs=[hbm, hbm, hbm, hbm, VMEM],
        out_specs=(VMEM,) * 3,
        scratch_shapes=[
            pltpu.SMEM(bounds.shape, jnp.int32),
            pltpu.SMEM(timesteps.shape, jnp.int32),
            pltpu.VMEM(gains.shape, jnp.float32),
            pltpu.VMEM(time_weight.shape, jnp.float32),
            pltpu.SemaphoreType.DMA((4,)),
        ],
        compiler_params=pltpu.CompilerParams(vmem_limit_bytes=24 * 1024 * 1024),
        cost_estimate=pl.CostEstimate(
            flops=8_000_000_000, bytes_accessed=1_000_000, transcendentals=10_000
        ),
        name="prepare",
    )(bounds, timesteps, gains, time_weight, frequency)


WIDE = ((3, FRAMES, J + 2, 2 * GROUP, LANES), jnp.bfloat16)
THIN = ((3, J + 2, FRAMES * GROUP, LANES), jnp.bfloat16)
ROWS_F32 = ((FRAMES * J, GROUP, PAIR), jnp.float32)


def apply_blocks(step, info, own, far, core, bias, gains, sw, sp, tp):
    sides = core if side_of(step) == "core" else [far]
    part, n_own, n_side, *tiles = call(
        functools.partial(first_kernel, step),
        "own_and_" + side_of(step) + "_rows",
        [((2, 2 * FIELD, C), jnp.float32)] + [ROWS_F32] * (4 if step == 0 else 2),
        [WIDE, THIN, ((FRAMES * J, PAIR // 128, GROUP, 128), jnp.float32)],
        1_000_000,
    )(info, own, *sides, gains, sw, sp)
    if step == 0:
        own, core = tiles
    (field,) = call(
        functools.partial(second_kernel, step),
        "residual_blocks",
        [((FIELD, PAIR), jnp.bfloat16)],
        [WIDE, THIN, ((2, FIELD, C), jnp.float32), ROWS_F32],
        4_000_000_000,
    )(info, own, far, core, part, n_own, n_side, bias, gains, sw, sp, tp)
    return field


def body(state, bounds, timesteps, gains, spatial_weight, temporal_weight, time_weight):
    groups = lax.axis_size("rows")
    segments = lax.axis_size("segment")
    ahead = [(i, (i + 1) % segments) for i in range(segments)]
    on_chip = [(i, i ^ 1) for i in range(groups)]
    off_chip = [(i, i + 1) for i in range(1, groups - 1, 2)]
    off_chip = off_chip + [(j, i) for i, j in off_chip] + [(0, 0), (groups - 1, groups - 1)]
    off_chip_ahead = [
        (a * groups + i, b * groups + j) for a, b in ahead for i, j in off_chip
    ]

    def tiled(value):
        value = value.reshape(FRAMES, ROWS, HB, J, PAIR).transpose(0, 3, 1, 2, 4)
        return value.reshape(FIELD, PAIR)

    own = lax.ppermute(state, "segment", ahead)
    field, gains = lax.optimization_barrier((tiled(state), gains))
    sw = spatial_weight.reshape(2, 3, 3 * C, C)
    tw = temporal_weight.reshape(2, 3, C, C)
    made = prepare(bounds, timesteps, gains[0], time_weight[0])
    sw, tw, made = lax.optimization_barrier((sw, tw, made))
    side_by_side = call(
        pairs_kernel,
        "weight_pairs",
        [((2, 3, 2 * C, SECOND + C), jnp.bfloat16), ((2, 2 * SECOND, SECOND + C), jnp.bfloat16)],
        [],
        4_000_000_000,
    )(sw, tw)
    field, side_by_side = lax.optimization_barrier((field, side_by_side))
    far = lax.ppermute(field, ("segment", "rows"), off_chip_ahead)
    own, made, side_by_side = lax.optimization_barrier((own, made, side_by_side))
    info, bias, gain_pairs = made
    sp, tp = side_by_side
    core = [lax.ppermute(own[:, f : f + 1], "rows", on_chip) for f in range(FRAMES)]
    field = apply_blocks(
        0, info, own, far, core, bias, gain_pairs, sw, sp, tp
    )
    for step in range(1, STEPS):
        far = lax.ppermute(field, ("segment", "rows"), off_chip_ahead)
        own = lax.ppermute(field, "segment", ahead)
        core = lax.ppermute(own, "rows", on_chip)
        field = apply_blocks(step, info, own, far, core, bias, gain_pairs, sw, sp, tp)
    field = field.reshape(FRAMES, J, ROWS, HB, PAIR).transpose(0, 2, 3, 1, 4)
    return field.reshape(1, FRAMES, ROWS, W * C)


def solution(mesh):
    placed = (
        P("segment", None, "rows", None),
        P(),
        P(),
        P("segment", None, None),
        P("segment", None, None, None, None, None),
        P("segment", None, None, None, None),
        P("segment", None, None, None),
    )
    return jax.shard_map(
        body,
        mesh=mesh,
        in_specs=placed,
        out_specs=P("segment", None, "rows", None),
        check_vma=False,
    )
```

```python
import functools
import math

import jax
import jax.numpy as jnp
from jax import lax
from jax.experimental import pallas as pl
from jax.experimental.pallas import tpu as pltpu
from jax.sharding import PartitionSpec as P

C = 320
W = 72
STEPS = 2
FRAMES = 2
ROWS = 2

HB = 4
J = W // 2 // HB
PAIR = 2 * C
GROUP = ROWS * HB
FIELD = FRAMES * J * GROUP
PAD = 64
LANES = PAIR + 256
SECOND = C + PAD
EPS = 1e-06


def low_lanes(shape):
    return lax.broadcasted_iota(jnp.int32, shape, len(shape) - 1) < PAD


def normalise(value, gain):
    low = low_lanes(value[..., 256:384].shape)
    square = value * value
    middle = square[..., 256:384]
    first = square[..., 0:128] + square[..., 128:256] + jnp.where(low, middle, 0.0)
    second = square[..., 384:512] + square[..., 512:640] + jnp.where(low, 0.0, middle)
    scale = lax.rsqrt(jnp.sum(first, axis=-1, keepdims=True) / C + EPS)
    other = lax.rsqrt(jnp.sum(second, axis=-1, keepdims=True) / C + EPS)
    scaled = jnp.concatenate(
        [
            value[..., 0:256] * scale,
            value[..., 256:384] * jnp.where(low, scale, other),
            value[..., 384:640] * other,
        ],
        axis=-1,
    )
    return scaled * gain


def load(ref):
    return ref[...].astype(jnp.float32).reshape(FRAMES * J, GROUP, PAIR)


def flip(value):
    return pltpu.roll(value, HB, 1)


def flip_if(odd, value):
    return pltpu.roll(value, HB * odd, 1)


def halves(first, second):
    row = lax.broadcasted_iota(jnp.int32, first.shape, 1)
    return jnp.where(row < HB, first, second)


def shifted_h(value, by):
    rows = value.shape[0]
    moved = pltpu.roll(value, by % rows, 0)
    h = lax.rem(lax.broadcasted_iota(jnp.int32, value.shape, 0), HB)
    edge = 0 if by == 1 else HB - 1
    return jnp.where(h == edge, 0.0, moved)


def put(ref, at, value):
    middle = value[..., 256:384]
    low = low_lanes(middle.shape)
    ref[at + (slice(None), slice(0, PAIR))] = value.astype(jnp.bfloat16)
    ref[at + (slice(None), slice(PAIR, PAIR + 128))] = jnp.where(low, 0.0, middle).astype(
        jnp.bfloat16
    )
    ref[at + (slice(None), slice(PAIR + 128, LANES))] = jnp.where(low, middle, 0.0).astype(
        jnp.bfloat16
    )


def put_wide(ref, dy, first, second):
    tiles = jnp.concatenate([first, second], axis=1).reshape(FRAMES, J, 2 * GROUP, PAIR)
    put(ref, (dy, slice(None), slice(1, J + 1)), tiles)
    for f in range(FRAMES):
        put(ref, (dy, f, 0), shifted_h(tiles[f, J - 1], 1))
        put(ref, (dy, f, J + 1), shifted_h(tiles[f, 0], -1))


def put_thin(ref, dy, value):
    tiles = value.reshape(FRAMES, J, GROUP, PAIR)
    tiles = jnp.concatenate([tiles[0], tiles[1]], axis=1)
    put(ref, (dy, slice(1, J + 1)), tiles)
    put(ref, (dy, 0), shifted_h(tiles[J - 1], 1))
    put(ref, (dy, J + 1), shifted_h(tiles[0], -1))


def rows_of(ref, dy, j0, wide, start, stop):
    if wide:
        return ref[dy, :, j0 : j0 + J, :, start:stop].reshape(-1, stop - start)
    return ref[dy, j0 : j0 + J, :, start:stop].reshape(-1, stop - start)


def silu(value):
    half = 0.5 * value
    return half + half * jnp.tanh(half)


def dot(a, b):
    return jnp.dot(a, b, preferred_element_type=jnp.float32)


def spatial(ref, wide, taps, weights, pairs, slot, odd):
    center, before, after, joint, left, right = [], [], [], [], [], []
    for dy in taps:
        at = dy + odd * (2 - 2 * dy)
        rows = functools.partial(rows_of, ref, dy, wide=wide)
        center.append(rows(1, start=0, stop=PAIR))
        before += [rows(0, start=PAIR, stop=PAIR + 128), rows(0, start=384, stop=PAIR)]
        after += [rows(2, start=0, stop=256), rows(2, start=PAIR + 128, stop=LANES)]
        filler = weights[slot, at, 0:PAD, :]
        joint.append(pairs[slot, at])
        left += [filler, weights[slot, at, 0:C, :]]
        right += [weights[slot, at, 2 * C :, :], filler]
    both = dot(jnp.concatenate(center, axis=1), jnp.concatenate(joint, axis=0))
    even_sum = dot(jnp.concatenate(before, axis=1), jnp.concatenate(left, axis=0))
    odd_sum = dot(jnp.concatenate(after, axis=1), jnp.concatenate(right, axis=0))
    return both[:, :C] + even_sum, both[:, SECOND:] + odd_sum


def temporal(u0, u1, pairs, slot):
    gap = jnp.zeros((u0.shape[0], PAD), u0.dtype)
    both = dot(jnp.concatenate([u0, gap, u1, gap], axis=1), pairs[slot])
    return both[:, :C], both[:, SECOND:]


def spatial_pairs_kernel(spatial_weight, spatial_pairs):
    for slot in range(2):
        for dy in range(3):
            kernel = spatial_weight.at[slot, dy]
            spatial_pairs[slot, dy, :, 0:C] = kernel[C : 3 * C, :]
            spatial_pairs[slot, dy, :, SECOND : SECOND + C] = kernel[0 : 2 * C, :]


def temporal_pairs_kernel(temporal_weight, temporal_pairs):
    for slot in range(2):
        for frame, lanes in enumerate((slice(0, C), slice(SECOND, SECOND + C))):
            for other in range(2):
                tap = temporal_weight.at[slot, 1 - frame + other]
                temporal_pairs[slot, other * SECOND : other * SECOND + C, lanes] = tap[...]
                temporal_pairs[slot, other * SECOND + C : (other + 1) * SECOND, lanes] = tap[0:PAD, :]


def frequency_kernel(out):
    half = out.shape[1] // 2
    at = lax.broadcasted_iota(jnp.int32, out.shape, 1)
    index = jnp.where(at < half, at, at - half).astype(jnp.float32)
    out[...] = jnp.exp(-math.log(10000.0) * index / half)


def prepare_kernel(
    bounds_hbm,
    timesteps_hbm,
    gains_hbm,
    time_hbm,
    frequency,
    info,
    bias,
    gain_pairs,
    bounds,
    timesteps,
    gains,
    time_weight,
    sems,
):
    copies = [
        pltpu.make_async_copy(source, target, sems.at[n])
        for n, (source, target) in enumerate(
            (
                (bounds_hbm, bounds),
                (timesteps_hbm, timesteps),
                (gains_hbm, gains),
                (time_hbm, time_weight),
            )
        )
    ]
    for copy in copies:
        copy.start()
    for copy in copies:
        copy.wait()
    segment = lax.axis_index("segment")
    info[...] = jnp.full(info.shape, bounds[segment + 1] - bounds[segment], jnp.int32)
    gain_pairs[...] = jnp.concatenate([gains[...], gains[...]], axis=1)
    entries = time_weight.shape[1]
    half = entries // 2
    at = lax.broadcasted_iota(jnp.int32, (8, entries), 1)
    step = lax.broadcasted_iota(jnp.int32, (8, entries), 0)
    times = jnp.zeros((8, entries), jnp.int32)
    for s in range(STEPS):
        times = jnp.where(step == s, timesteps[s], times)
    angle = times.astype(jnp.float32) * frequency[...]
    emb = jnp.where(at < half, jnp.cos(angle), jnp.sin(angle))
    for slot in range(2):
        made = jnp.dot(
            emb,
            time_weight[slot],
            precision=lax.Precision.HIGHEST,
            preferred_element_type=jnp.float32,
        )
        for s in range(STEPS):
            bias[s, slot : slot + 1, :] = made[s : s + 1]


def place():
    row_group = lax.axis_index("rows")
    at_end = (row_group == 0) | (row_group == lax.axis_size("rows") - 1)
    return lax.rem(row_group, 2), at_end


def side_of(step):
    return "core" if step == 0 else "far"


def load_far(step, ref):
    odd, at_end = place()
    value = load(ref)
    if step == 0:
        value = flip_if(1 - odd, value)
    return jnp.where(at_end, 0.0, value)


def lay_out(refs, scratch, tiles, turn):
    frames = [ref.at[0, f] for ref in refs for f in range(ref.shape[1])]
    for f in range(FRAMES):
        for j in range(J):
            for h in range(HB):
                at = (h * J + j) * PAIR
                rows = frames[f][:, at : at + PAIR].astype(jnp.float32)
                for n in range(PAIR // 128):
                    scratch[f * J + j, n, pl.ds(h, ROWS, stride=HB), :] = rows[
                        :, n * 128 : (n + 1) * 128
                    ]
    value = jnp.concatenate([scratch[:, n] for n in range(PAIR // 128)], axis=-1)
    tiles[...] = flip_if(turn, value)


def first_kernel(step, info, own, *refs):
    count = jnp.max(info[0:1, :])
    odd, _ = place()
    core_side = side_of(step) == "core"
    sides, refs = refs[: FRAMES - step], refs[FRAMES - step :]
    gains, sw, sp, part, n_own, n_side = refs[:6]
    tiles, (wide, thin, scratch) = refs[6:-3], refs[-3:]
    if step == 0:
        lay_out([own], scratch, tiles[0], odd)
        lay_out(sides, scratch, tiles[1], 1 - odd)
        mine, theirs = tiles[0][...], tiles[1][...]
    else:
        mine, theirs = load(own), load_far(step, sides[0])
    gain = gains[0:1, :].reshape(1, 1, PAIR)
    normed, side_normed = normalise(mine, gain), normalise(theirs, gain)
    n_own[...] = normed
    n_side[...] = side_normed

    @pl.when(count > 1)
    def _():
        if core_side:
            put_wide(wide, 2, normed, flip(side_normed))
        else:
            put_wide(wide, 0, flip(side_normed), normed)
        even, odd_sum = spatial(wide, True, (2 if core_side else 0,), sw, sp, 0, odd)
        part[0], part[1] = even, odd_sum

    @pl.when(count == 1)
    def _():
        put_thin(thin, 1, normed)
        if core_side:
            put_thin(thin, 2, halves(flip(normed), side_normed))
        else:
            put_thin(thin, 0, halves(side_normed, flip(normed)))
        even, odd_sum = spatial(thin, False, (1, 2) if core_side else (0, 1), sw, sp, 0, odd)
        part[0, :FIELD], part[1, :FIELD] = even, odd_sum


def second_kernel(
    step, info, own, far, core, part, n_own, n_side, bias, gains, sw, sp, tp, out, wide, thin, acc, center
):
    count = jnp.max(info[0:1, :])
    odd, at_end = place()
    far_last = side_of(step) == "core"
    mine = own[...] if step == 0 else load(own)
    theirs = load_far(step, far) if far_last else load(core)
    last_normed = normalise(theirs, gains[0:1, :].reshape(1, 1, PAIR))

    @pl.when(count == 1)
    def _():
        if far_last:
            put_thin(thin, 0, halves(last_normed, flip(n_own[...])))
        else:
            put_thin(thin, 2, halves(flip(n_own[...]), last_normed))
        even, odd_sum = spatial(thin, False, (0 if far_last else 2,), sw, sp, 0, odd)
        acc[0], acc[1] = part[0, :FIELD] + even, part[1, :FIELD] + odd_sum
        center[...] = mine

    @pl.when(count > 1)
    def _():
        normed = n_own[...]
        turned = flip(normed)
        if far_last:
            far_normed, core_normed = last_normed, n_side[...]
            put_wide(wide, 0, flip(far_normed), normed)
        else:
            far_normed, core_normed = n_side[...], last_normed
            put_wide(wide, 2, normed, flip(core_normed))
        put_wide(wide, 1, halves(far_normed, turned), halves(turned, core_normed))
        even, odd_sum = spatial(wide, True, (0, 1) if far_last else (1, 2), sw, sp, 0, odd)
        by_far = theirs if far_last else load_far(step, far)
        by_core = core[...] if far_last else theirs
        even = part[0] + even + bias[step, 0:1, :]
        odd_sum = part[1] + odd_sum + bias[step, 0:1, :]
        half = FIELD
        u_even, u_odd = silu(even).astype(jnp.bfloat16), silu(odd_sum).astype(jnp.bfloat16)
        u0 = jnp.concatenate([u_even[:half], u_odd[:half]], axis=0)
        u1 = jnp.concatenate([u_even[half:], u_odd[half:]], axis=0)
        v0, v1 = temporal(u0, u1, tp, 0)
        v_even = jnp.concatenate([v0[:half], v1[:half]], axis=0)
        v_odd = jnp.concatenate([v0[half:], v1[half:]], axis=0)
        change = jnp.concatenate([even + v_even, odd_sum + v_odd], axis=1)
        change = change.reshape(FRAMES * J, 2 * GROUP, PAIR)
        back = flip(mine)
        first = halves(by_far, back) + change[:, :GROUP]
        second = halves(back, by_core) + change[:, GROUP:]
        first = first.astype(jnp.bfloat16).astype(jnp.float32)
        second = second.astype(jnp.bfloat16).astype(jnp.float32)
        row = lax.broadcasted_iota(jnp.int32, first.shape, 1)
        first = jnp.where((row < HB) & at_end, 0.0, first)
        center[...] = halves(flip(first), flip(second))
        gain = gains[1:2, :].reshape(1, 1, PAIR)
        n_first, n_second = normalise(first, gain), normalise(second, gain)
        put_thin(thin, 0, n_first)
        put_thin(thin, 1, halves(flip(n_first), flip(n_second)))
        put_thin(thin, 2, n_second)
        even, odd_sum = spatial(thin, False, (0, 1, 2), sw, sp, 1, odd)
        acc[0], acc[1] = even, odd_sum

    last = count - 1
    shift = bias[step, pl.ds(last, 1), :]
    even = (acc[0] + shift).reshape(J, FRAMES, GROUP, C)
    odd_sum = (acc[1] + shift).reshape(J, FRAMES, GROUP, C)
    u0, u1 = (
        jnp.concatenate(
            [silu(even[:, f]).reshape(-1, C), silu(odd_sum[:, f]).reshape(-1, C)], axis=0
        )
        for f in range(FRAMES)
    )
    v0, v1 = temporal(u0.astype(jnp.bfloat16), u1.astype(jnp.bfloat16), tp, last)
    half = J * GROUP
    for f, v in enumerate((v0, v1)):
        a_even, a_odd = even[:, f].reshape(half, C), odd_sum[:, f].reshape(half, C)
        change = jnp.concatenate([a_even + v[:half], a_odd + v[half:]], axis=1)
        result = center[f * J : (f + 1) * J] + change.reshape(J, GROUP, PAIR)
        if step == STEPS - 1:
            result = flip_if(odd, result)
        out[f * half : (f + 1) * half, :] = result.reshape(half, PAIR).astype(jnp.bfloat16)


VMEM = pl.BlockSpec(memory_space=pltpu.VMEM)


def call(kernel, name, outs, scratch, flops):
    return pl.pallas_call(
        kernel,
        out_shape=tuple(jax.ShapeDtypeStruct(shape, dtype) for shape, dtype in outs),
        out_specs=(VMEM,) * len(outs),
        scratch_shapes=[pltpu.VMEM(shape, dtype) for shape, dtype in scratch],
        compiler_params=pltpu.CompilerParams(vmem_limit_bytes=24 * 1024 * 1024),
        cost_estimate=pl.CostEstimate(
            flops=flops, bytes_accessed=flops // 4_000, transcendentals=0
        ),
        name=name,
    )


def prepare(bounds, timesteps, gains, time_weight):
    hbm = pl.BlockSpec(memory_space=pltpu.HBM)
    (frequency,) = call(
        frequency_kernel, "frequency", [((8, time_weight.shape[1]), jnp.float32)], [], 4_000_000_000
    )()
    return pl.pallas_call(
        prepare_kernel,
        out_shape=(
            jax.ShapeDtypeStruct((8, 128), jnp.int32),
            jax.ShapeDtypeStruct((STEPS, 2, C), jnp.float32),
            jax.ShapeDtypeStruct((2, PAIR), jnp.float32),
        ),
        in_specs=[hbm, hbm, hbm, hbm, VMEM],
        out_specs=(VMEM,) * 3,
        scratch_shapes=[
            pltpu.SMEM(bounds.shape, jnp.int32),
            pltpu.SMEM(timesteps.shape, jnp.int32),
            pltpu.VMEM(gains.shape, jnp.float32),
            pltpu.VMEM(time_weight.shape, jnp.float32),
            pltpu.SemaphoreType.DMA((4,)),
        ],
        compiler_params=pltpu.CompilerParams(vmem_limit_bytes=24 * 1024 * 1024),
        cost_estimate=pl.CostEstimate(
            flops=8_000_000_000, bytes_accessed=1_000_000, transcendentals=10_000
        ),
        name="prepare",
    )(bounds, timesteps, gains, time_weight, frequency)


WIDE = ((3, FRAMES, J + 2, 2 * GROUP, LANES), jnp.bfloat16)
THIN = ((3, J + 2, FRAMES * GROUP, LANES), jnp.bfloat16)
ROWS_F32 = ((FRAMES * J, GROUP, PAIR), jnp.float32)


def apply_blocks(step, info, own, far, core, bias, gains, sw, sp, tp):
    sides = core if side_of(step) == "core" else [far]
    part, n_own, n_side, *tiles = call(
        functools.partial(first_kernel, step),
        "own_and_" + side_of(step) + "_rows",
        [((2, 2 * FIELD, C), jnp.float32)] + [ROWS_F32] * (4 if step == 0 else 2),
        [WIDE, THIN, ((FRAMES * J, PAIR // 128, GROUP, 128), jnp.float32)],
        1_000_000,
    )(info, own, *sides, gains, sw, sp)
    if step == 0:
        own, core = tiles
    (field,) = call(
        functools.partial(second_kernel, step),
        "residual_blocks",
        [((FIELD, PAIR), jnp.bfloat16)],
        [WIDE, THIN, ((2, FIELD, C), jnp.float32), ROWS_F32],
        4_000_000_000,
    )(info, own, far, core, part, n_own, n_side, bias, gains, sw, sp, tp)
    return field


def body(state, bounds, timesteps, gains, spatial_weight, temporal_weight, time_weight):
    groups = lax.axis_size("rows")
    segments = lax.axis_size("segment")
    ahead = [(i, (i + 1) % segments) for i in range(segments)]
    on_chip = [(i, i ^ 1) for i in range(groups)]
    off_chip = [(i, i + 1) for i in range(1, groups - 1, 2)]
    off_chip = off_chip + [(j, i) for i, j in off_chip] + [(0, 0), (groups - 1, groups - 1)]
    off_chip_ahead = [
        (a * groups + i, b * groups + j) for a, b in ahead for i, j in off_chip
    ]

    def tiled(value):
        value = value.reshape(FRAMES, ROWS, HB, J, PAIR).transpose(0, 3, 1, 2, 4)
        return value.reshape(FIELD, PAIR)

    own = lax.ppermute(state, "segment", ahead)
    field, gains = lax.optimization_barrier((tiled(state), gains))
    sw = spatial_weight.reshape(2, 3, 3 * C, C)
    tw = temporal_weight.reshape(2, 3, C, C)
    made = prepare(bounds, timesteps, gains[0], time_weight[0])
    sw, made = lax.optimization_barrier((sw, made))
    (sp,) = call(
        spatial_pairs_kernel,
        "spatial_pairs",
        [((2, 3, 2 * C, SECOND + C), jnp.bfloat16)],
        [],
        4_000_000_000,
    )(sw)
    field, sp, tw = lax.optimization_barrier((field, sp, tw))
    far = lax.ppermute(field, ("segment", "rows"), off_chip_ahead)
    (tp,) = call(
        temporal_pairs_kernel,
        "temporal_pairs",
        [((2, 2 * SECOND, SECOND + C), jnp.bfloat16)],
        [],
        1_000_000_000,
    )(tw)
    own, made, sp, tp = lax.optimization_barrier((own, made, sp, tp))
    info, bias, gain_pairs = made
    core = [lax.ppermute(own[:, f : f + 1], "rows", on_chip) for f in range(FRAMES)]
    field = apply_blocks(
        0, info, own, far, core, bias, gain_pairs, sw, sp, tp
    )
    for step in range(1, STEPS):
        far = lax.ppermute(field, ("segment", "rows"), off_chip_ahead)
        own = lax.ppermute(field, "segment", ahead)
        core = lax.ppermute(own, "rows", on_chip)
        field = apply_blocks(step, info, own, far, core, bias, gain_pairs, sw, sp, tp)
    field = field.reshape(FRAMES, J, ROWS, HB, PAIR).transpose(0, 2, 3, 1, 4)
    return field.reshape(1, FRAMES, ROWS, W * C)


def solution(mesh):
    placed = (
        P("segment", None, "rows", None),
        P(),
        P(),
        P("segment", None, None),
        P("segment", None, None, None, None, None),
        P("segment", None, None, None, None),
        P("segment", None, None, None),
    )
    return jax.shard_map(
        body,
        mesh=mesh,
        in_specs=placed,
        out_specs=P("segment", None, "rows", None),
        check_vma=False,
    )
```

```python
import functools
import math

import jax
import jax.numpy as jnp
from jax import lax
from jax.experimental import pallas as pl
from jax.experimental.pallas import tpu as pltpu
from jax.sharding import PartitionSpec as P

C = 320
W = 72
STEPS = 2
FRAMES = 2
ROWS = 2

HB = 4
J = W // 2 // HB
PAIR = 2 * C
GROUP = ROWS * HB
FIELD = FRAMES * J * GROUP
PAD = 64
LANES = PAIR + 256
SECOND = C + PAD
EPS = 1e-06


def low_lanes(shape):
    return lax.broadcasted_iota(jnp.int32, shape, len(shape) - 1) < PAD


def normalise(value, gain):
    low = low_lanes(value[..., 256:384].shape)
    square = value * value
    middle = square[..., 256:384]
    first = square[..., 0:128] + square[..., 128:256] + jnp.where(low, middle, 0.0)
    second = square[..., 384:512] + square[..., 512:640] + jnp.where(low, 0.0, middle)
    scale = lax.rsqrt(jnp.sum(first, axis=-1, keepdims=True) / C + EPS)
    other = lax.rsqrt(jnp.sum(second, axis=-1, keepdims=True) / C + EPS)
    scaled = jnp.concatenate(
        [
            value[..., 0:256] * scale,
            value[..., 256:384] * jnp.where(low, scale, other),
            value[..., 384:640] * other,
        ],
        axis=-1,
    )
    return scaled * gain


def load(ref):
    return ref[...].astype(jnp.float32).reshape(FRAMES * J, GROUP, PAIR)


def flip(value):
    return pltpu.roll(value, HB, 1)


def flip_if(odd, value):
    return pltpu.roll(value, HB * odd, 1)


def halves(first, second):
    row = lax.broadcasted_iota(jnp.int32, first.shape, 1)
    return jnp.where(row < HB, first, second)


def shifted_h(value, by):
    rows = value.shape[0]
    moved = pltpu.roll(value, by % rows, 0)
    h = lax.rem(lax.broadcasted_iota(jnp.int32, value.shape, 0), HB)
    edge = 0 if by == 1 else HB - 1
    return jnp.where(h == edge, 0.0, moved)


def put(ref, at, value):
    middle = value[..., 256:384]
    low = low_lanes(middle.shape)
    ref[at + (slice(None), slice(0, PAIR))] = value.astype(jnp.bfloat16)
    ref[at + (slice(None), slice(PAIR, PAIR + 128))] = jnp.where(low, 0.0, middle).astype(
        jnp.bfloat16
    )
    ref[at + (slice(None), slice(PAIR + 128, LANES))] = jnp.where(low, middle, 0.0).astype(
        jnp.bfloat16
    )


def put_wide(ref, dy, first, second):
    tiles = jnp.concatenate([first, second], axis=1).reshape(FRAMES, J, 2 * GROUP, PAIR)
    put(ref, (dy, slice(None), slice(1, J + 1)), tiles)
    for f in range(FRAMES):
        put(ref, (dy, f, 0), shifted_h(tiles[f, J - 1], 1))
        put(ref, (dy, f, J + 1), shifted_h(tiles[f, 0], -1))


def put_thin(ref, dy, value):
    tiles = value.reshape(FRAMES, J, GROUP, PAIR)
    tiles = jnp.concatenate([tiles[0], tiles[1]], axis=1)
    put(ref, (dy, slice(1, J + 1)), tiles)
    put(ref, (dy, 0), shifted_h(tiles[J - 1], 1))
    put(ref, (dy, J + 1), shifted_h(tiles[0], -1))


def rows_of(ref, dy, j0, wide, start, stop):
    if wide:
        return ref[dy, :, j0 : j0 + J, :, start:stop].reshape(-1, stop - start)
    return ref[dy, j0 : j0 + J, :, start:stop].reshape(-1, stop - start)


def silu(value):
    half = 0.5 * value
    return half + half * jnp.tanh(half)


def dot(a, b):
    return jnp.dot(a, b, preferred_element_type=jnp.float32)


def spatial(ref, wide, taps, weights, pairs, slot, odd):
    center, before, after, joint, left, right = [], [], [], [], [], []
    for dy in taps:
        at = dy + odd * (2 - 2 * dy)
        rows = functools.partial(rows_of, ref, dy, wide=wide)
        center.append(rows(1, start=0, stop=PAIR))
        before += [rows(0, start=PAIR, stop=PAIR + 128), rows(0, start=384, stop=PAIR)]
        after += [rows(2, start=0, stop=256), rows(2, start=PAIR + 128, stop=LANES)]
        filler = weights[slot, at, 0:PAD, :]
        joint.append(pairs[0, at])
        left += [filler, weights[slot, at, 0:C, :]]
        right += [weights[slot, at, 2 * C :, :], filler]
    both = dot(jnp.concatenate(center, axis=1), jnp.concatenate(joint, axis=0))
    even_sum = dot(jnp.concatenate(before, axis=1), jnp.concatenate(left, axis=0))
    odd_sum = dot(jnp.concatenate(after, axis=1), jnp.concatenate(right, axis=0))
    return both[:, :C] + even_sum, both[:, SECOND:] + odd_sum


def temporal(u0, u1, pairs, slot):
    gap = jnp.zeros((u0.shape[0], PAD), u0.dtype)
    both = dot(jnp.concatenate([u0, gap, u1, gap], axis=1), pairs[slot])
    return both[:, :C], both[:, SECOND:]


def spatial_pairs_kernel(slot, spatial_weight, spatial_pairs):
    for dy in range(3):
        kernel = spatial_weight.at[slot, dy]
        spatial_pairs[0, dy, :, 0:C] = kernel[C : 3 * C, :]
        spatial_pairs[0, dy, :, SECOND : SECOND + C] = kernel[0 : 2 * C, :]


def temporal_pairs_kernel(temporal_weight, temporal_pairs):
    for slot in range(2):
        for frame, lanes in enumerate((slice(0, C), slice(SECOND, SECOND + C))):
            for other in range(2):
                tap = temporal_weight.at[slot, 1 - frame + other]
                temporal_pairs[slot, other * SECOND : other * SECOND + C, lanes] = tap[...]
                temporal_pairs[slot, other * SECOND + C : (other + 1) * SECOND, lanes] = tap[0:PAD, :]


def frequency_kernel(out):
    half = out.shape[1] // 2
    at = lax.broadcasted_iota(jnp.int32, out.shape, 1)
    index = jnp.where(at < half, at, at - half).astype(jnp.float32)
    out[...] = jnp.exp(-math.log(10000.0) * index / half)


def prepare_kernel(
    bounds_hbm,
    timesteps_hbm,
    gains_hbm,
    time_hbm,
    frequency,
    info,
    bias,
    gain_pairs,
    bounds,
    timesteps,
    gains,
    time_weight,
    sems,
):
    copies = [
        pltpu.make_async_copy(source, target, sems.at[n])
        for n, (source, target) in enumerate(
            (
                (bounds_hbm, bounds),
                (timesteps_hbm, timesteps),
                (gains_hbm, gains),
                (time_hbm, time_weight),
            )
        )
    ]
    for copy in copies:
        copy.start()
    for copy in copies:
        copy.wait()
    segment = lax.axis_index("segment")
    info[...] = jnp.full(info.shape, bounds[segment + 1] - bounds[segment], jnp.int32)
    gain_pairs[...] = jnp.concatenate([gains[...], gains[...]], axis=1)
    entries = time_weight.shape[1]
    half = entries // 2
    at = lax.broadcasted_iota(jnp.int32, (8, entries), 1)
    step = lax.broadcasted_iota(jnp.int32, (8, entries), 0)
    times = jnp.zeros((8, entries), jnp.int32)
    for s in range(STEPS):
        times = jnp.where(step == s, timesteps[s], times)
    angle = times.astype(jnp.float32) * frequency[...]
    emb = jnp.where(at < half, jnp.cos(angle), jnp.sin(angle))
    for slot in range(2):
        made = jnp.dot(
            emb,
            time_weight[slot],
            precision=lax.Precision.HIGHEST,
            preferred_element_type=jnp.float32,
        )
        for s in range(STEPS):
            bias[s, slot : slot + 1, :] = made[s : s + 1]


def place():
    row_group = lax.axis_index("rows")
    at_end = (row_group == 0) | (row_group == lax.axis_size("rows") - 1)
    return lax.rem(row_group, 2), at_end


def side_of(step):
    return "core" if step == 0 else "far"


def load_far(step, ref):
    odd, at_end = place()
    value = load(ref)
    if step == 0:
        value = flip_if(1 - odd, value)
    return jnp.where(at_end, 0.0, value)


def lay_out(refs, scratch, tiles, turn):
    frames = [ref.at[0, f] for ref in refs for f in range(ref.shape[1])]
    for f in range(FRAMES):
        for j in range(J):
            for h in range(HB):
                at = (h * J + j) * PAIR
                rows = frames[f][:, at : at + PAIR].astype(jnp.float32)
                for n in range(PAIR // 128):
                    scratch[f * J + j, n, pl.ds(h, ROWS, stride=HB), :] = rows[
                        :, n * 128 : (n + 1) * 128
                    ]
    value = jnp.concatenate([scratch[:, n] for n in range(PAIR // 128)], axis=-1)
    tiles[...] = flip_if(turn, value)


def first_kernel(step, info, own, *refs):
    count = jnp.max(info[0:1, :])
    odd, _ = place()
    core_side = side_of(step) == "core"
    sides, refs = refs[: FRAMES - step], refs[FRAMES - step :]
    gains, sw, sp, part, n_own, n_side = refs[:6]
    tiles, (wide, thin, scratch) = refs[6:-3], refs[-3:]
    if step == 0:
        lay_out([own], scratch, tiles[0], odd)
        lay_out(sides, scratch, tiles[1], 1 - odd)
        mine, theirs = tiles[0][...], tiles[1][...]
    else:
        mine, theirs = load(own), load_far(step, sides[0])
    gain = gains[0:1, :].reshape(1, 1, PAIR)
    normed, side_normed = normalise(mine, gain), normalise(theirs, gain)
    n_own[...] = normed
    n_side[...] = side_normed

    @pl.when(count > 1)
    def _():
        if core_side:
            put_wide(wide, 2, normed, flip(side_normed))
        else:
            put_wide(wide, 0, flip(side_normed), normed)
        even, odd_sum = spatial(wide, True, (2 if core_side else 0,), sw, sp, 0, odd)
        part[0], part[1] = even, odd_sum

    @pl.when(count == 1)
    def _():
        put_thin(thin, 1, normed)
        if core_side:
            put_thin(thin, 2, halves(flip(normed), side_normed))
        else:
            put_thin(thin, 0, halves(side_normed, flip(normed)))
        even, odd_sum = spatial(thin, False, (1, 2) if core_side else (0, 1), sw, sp, 0, odd)
        part[0, :FIELD], part[1, :FIELD] = even, odd_sum


def second_kernel(
    step, info, own, far, core, part, n_own, n_side, bias, gains, sw, sp, sp1, tp, out, wide, thin, acc, center
):
    count = jnp.max(info[0:1, :])
    odd, at_end = place()
    far_last = side_of(step) == "core"
    mine = own[...] if step == 0 else load(own)
    theirs = load_far(step, far) if far_last else load(core)
    last_normed = normalise(theirs, gains[0:1, :].reshape(1, 1, PAIR))

    @pl.when(count == 1)
    def _():
        if far_last:
            put_thin(thin, 0, halves(last_normed, flip(n_own[...])))
        else:
            put_thin(thin, 2, halves(flip(n_own[...]), last_normed))
        even, odd_sum = spatial(thin, False, (0 if far_last else 2,), sw, sp, 0, odd)
        acc[0], acc[1] = part[0, :FIELD] + even, part[1, :FIELD] + odd_sum
        center[...] = mine

    @pl.when(count > 1)
    def _():
        normed = n_own[...]
        turned = flip(normed)
        if far_last:
            far_normed, core_normed = last_normed, n_side[...]
            put_wide(wide, 0, flip(far_normed), normed)
        else:
            far_normed, core_normed = n_side[...], last_normed
            put_wide(wide, 2, normed, flip(core_normed))
        put_wide(wide, 1, halves(far_normed, turned), halves(turned, core_normed))
        even, odd_sum = spatial(wide, True, (0, 1) if far_last else (1, 2), sw, sp, 0, odd)
        by_far = theirs if far_last else load_far(step, far)
        by_core = core[...] if far_last else theirs
        even = part[0] + even + bias[step, 0:1, :]
        odd_sum = part[1] + odd_sum + bias[step, 0:1, :]
        half = FIELD
        u_even, u_odd = silu(even).astype(jnp.bfloat16), silu(odd_sum).astype(jnp.bfloat16)
        u0 = jnp.concatenate([u_even[:half], u_odd[:half]], axis=0)
        u1 = jnp.concatenate([u_even[half:], u_odd[half:]], axis=0)
        v0, v1 = temporal(u0, u1, tp, 0)
        v_even = jnp.concatenate([v0[:half], v1[:half]], axis=0)
        v_odd = jnp.concatenate([v0[half:], v1[half:]], axis=0)
        change = jnp.concatenate([even + v_even, odd_sum + v_odd], axis=1)
        change = change.reshape(FRAMES * J, 2 * GROUP, PAIR)
        back = flip(mine)
        first = halves(by_far, back) + change[:, :GROUP]
        second = halves(back, by_core) + change[:, GROUP:]
        first = first.astype(jnp.bfloat16).astype(jnp.float32)
        second = second.astype(jnp.bfloat16).astype(jnp.float32)
        row = lax.broadcasted_iota(jnp.int32, first.shape, 1)
        first = jnp.where((row < HB) & at_end, 0.0, first)
        center[...] = halves(flip(first), flip(second))
        gain = gains[1:2, :].reshape(1, 1, PAIR)
        n_first, n_second = normalise(first, gain), normalise(second, gain)
        put_thin(thin, 0, n_first)
        put_thin(thin, 1, halves(flip(n_first), flip(n_second)))
        put_thin(thin, 2, n_second)
        even, odd_sum = spatial(thin, False, (0, 1, 2), sw, sp1, 1, odd)
        acc[0], acc[1] = even, odd_sum

    last = count - 1
    shift = bias[step, pl.ds(last, 1), :]
    even = (acc[0] + shift).reshape(J, FRAMES, GROUP, C)
    odd_sum = (acc[1] + shift).reshape(J, FRAMES, GROUP, C)
    u0, u1 = (
        jnp.concatenate(
            [silu(even[:, f]).reshape(-1, C), silu(odd_sum[:, f]).reshape(-1, C)], axis=0
        )
        for f in range(FRAMES)
    )
    v0, v1 = temporal(u0.astype(jnp.bfloat16), u1.astype(jnp.bfloat16), tp, last)
    half = J * GROUP
    for f, v in enumerate((v0, v1)):
        a_even, a_odd = even[:, f].reshape(half, C), odd_sum[:, f].reshape(half, C)
        change = jnp.concatenate([a_even + v[:half], a_odd + v[half:]], axis=1)
        result = center[f * J : (f + 1) * J] + change.reshape(J, GROUP, PAIR)
        if step == STEPS - 1:
            result = flip_if(odd, result)
        out[f * half : (f + 1) * half, :] = result.reshape(half, PAIR).astype(jnp.bfloat16)


VMEM = pl.BlockSpec(memory_space=pltpu.VMEM)


def call(kernel, name, outs, scratch, flops):
    return pl.pallas_call(
        kernel,
        out_shape=tuple(jax.ShapeDtypeStruct(shape, dtype) for shape, dtype in outs),
        out_specs=(VMEM,) * len(outs),
        scratch_shapes=[pltpu.VMEM(shape, dtype) for shape, dtype in scratch],
        compiler_params=pltpu.CompilerParams(vmem_limit_bytes=24 * 1024 * 1024),
        cost_estimate=pl.CostEstimate(
            flops=flops, bytes_accessed=flops // 4_000, transcendentals=0
        ),
        name=name,
    )


def prepare(bounds, timesteps, gains, time_weight):
    hbm = pl.BlockSpec(memory_space=pltpu.HBM)
    (frequency,) = call(
        frequency_kernel, "frequency", [((8, time_weight.shape[1]), jnp.float32)], [], 4_000_000_000
    )()
    return pl.pallas_call(
        prepare_kernel,
        out_shape=(
            jax.ShapeDtypeStruct((8, 128), jnp.int32),
            jax.ShapeDtypeStruct((STEPS, 2, C), jnp.float32),
            jax.ShapeDtypeStruct((2, PAIR), jnp.float32),
        ),
        in_specs=[hbm, hbm, hbm, hbm, VMEM],
        out_specs=(VMEM,) * 3,
        scratch_shapes=[
            pltpu.SMEM(bounds.shape, jnp.int32),
            pltpu.SMEM(timesteps.shape, jnp.int32),
            pltpu.VMEM(gains.shape, jnp.float32),
            pltpu.VMEM(time_weight.shape, jnp.float32),
            pltpu.SemaphoreType.DMA((4,)),
        ],
        compiler_params=pltpu.CompilerParams(vmem_limit_bytes=24 * 1024 * 1024),
        cost_estimate=pl.CostEstimate(
            flops=8_000_000_000, bytes_accessed=1_000_000, transcendentals=10_000
        ),
        name="prepare",
    )(bounds, timesteps, gains, time_weight, frequency)


WIDE = ((3, FRAMES, J + 2, 2 * GROUP, LANES), jnp.bfloat16)
THIN = ((3, J + 2, FRAMES * GROUP, LANES), jnp.bfloat16)
ROWS_F32 = ((FRAMES * J, GROUP, PAIR), jnp.float32)


def apply_blocks(step, info, own, far, core, bias, gains, sw, sp, tp):
    sides = core if side_of(step) == "core" else [far]
    part, n_own, n_side, *tiles = call(
        functools.partial(first_kernel, step),
        "own_and_" + side_of(step) + "_rows",
        [((2, 2 * FIELD, C), jnp.float32)] + [ROWS_F32] * (4 if step == 0 else 2),
        [WIDE, THIN, ((FRAMES * J, PAIR // 128, GROUP, 128), jnp.float32)],
        1_000_000,
    )(info, own, *sides, gains, sw, sp[0])
    if step == 0:
        own, core = tiles
    (field,) = call(
        functools.partial(second_kernel, step),
        "residual_blocks",
        [((FIELD, PAIR), jnp.bfloat16)],
        [WIDE, THIN, ((2, FIELD, C), jnp.float32), ROWS_F32],
        4_000_000_000,
    )(info, own, far, core, part, n_own, n_side, bias, gains, sw, *sp, tp)
    return field


def body(state, bounds, timesteps, gains, spatial_weight, temporal_weight, time_weight):
    groups = lax.axis_size("rows")
    segments = lax.axis_size("segment")
    ahead = [(i, (i + 1) % segments) for i in range(segments)]
    on_chip = [(i, i ^ 1) for i in range(groups)]
    off_chip = [(i, i + 1) for i in range(1, groups - 1, 2)]
    off_chip = off_chip + [(j, i) for i, j in off_chip] + [(0, 0), (groups - 1, groups - 1)]
    off_chip_ahead = [
        (a * groups + i, b * groups + j) for a, b in ahead for i, j in off_chip
    ]

    def tiled(value):
        value = value.reshape(FRAMES, ROWS, HB, J, PAIR).transpose(0, 3, 1, 2, 4)
        return value.reshape(FIELD, PAIR)

    own = lax.ppermute(state, "segment", ahead)
    field, gains = lax.optimization_barrier((tiled(state), gains))
    sw = spatial_weight.reshape(2, 3, 3 * C, C)
    tw = temporal_weight.reshape(2, 3, C, C)
    made = prepare(bounds, timesteps, gains[0], time_weight[0])
    sw, made = lax.optimization_barrier((sw, made))
    def side_by_side(slot, weight):
        (made,) = call(
            functools.partial(spatial_pairs_kernel, slot),
            "spatial_pairs",
            [((1, 3, 2 * C, SECOND + C), jnp.bfloat16)],
            [],
            2_000_000_000,
        )(weight)
        return made

    sp0 = side_by_side(0, sw)
    field, sp0, sw, tw = lax.optimization_barrier((field, sp0, sw, tw))
    far = lax.ppermute(field, ("segment", "rows"), off_chip_ahead)
    (tp,) = call(
        temporal_pairs_kernel,
        "temporal_pairs",
        [((2, 2 * SECOND, SECOND + C), jnp.bfloat16)],
        [],
        1_000_000_000,
    )(tw)
    sp = (sp0, side_by_side(1, sw))
    own, made, sp, tp = lax.optimization_barrier((own, made, sp, tp))
    info, bias, gain_pairs = made
    core = [lax.ppermute(own[:, f : f + 1], "rows", on_chip) for f in range(FRAMES)]
    field = apply_blocks(
        0, info, own, far, core, bias, gain_pairs, sw, sp, tp
    )
    for step in range(1, STEPS):
        far = lax.ppermute(field, ("segment", "rows"), off_chip_ahead)
        own = lax.ppermute(field, "segment", ahead)
        core = lax.ppermute(own, "rows", on_chip)
        field = apply_blocks(step, info, own, far, core, bias, gain_pairs, sw, sp, tp)
    field = field.reshape(FRAMES, J, ROWS, HB, PAIR).transpose(0, 2, 3, 1, 4)
    return field.reshape(1, FRAMES, ROWS, W * C)


def solution(mesh):
    placed = (
        P("segment", None, "rows", None),
        P(),
        P(),
        P("segment", None, None),
        P("segment", None, None, None, None, None),
        P("segment", None, None, None, None),
        P("segment", None, None, None),
    )
    return jax.shard_map(
        body,
        mesh=mesh,
        in_specs=placed,
        out_specs=P("segment", None, "rows", None),
        check_vma=False,
    )
```
